32 devices in a mesh: dom: 8 (over z, y), feat: 4 (over x, core).
Axes of the slice: x: 2, y: 2, z: 4, core: 2. Of those that a mesh axis runs over, the one named last changes fastest.
Arguments:
- features: float32 [16384, 100], P('dom', 'feat'), may hold values from -6 to 6
- inner_adj: int32 [16384, 2048], P('dom'), may hold values 0 or 1
- bound_adj: int32 [16384, 256], P('dom'), may hold values 0 or 1
- keep_slots: int32 [8, 256], P('dom'), may hold values 0 or 1
- send_index: int32 [8, 8, 32], P('dom'), may hold values from 0 to 2047
- labels: int32 [16384], P('dom'), may hold values from 0 to 46
- train_mask: int32 [16384], P('dom'), may hold values from 0 to 1
- w_in: float32 [2, 100, 256], P(None, 'feat'), may hold values from -0.4375 to 0.4375
- w_mid: float32 [2, 256, 256], P(None, 'feat'), may hold values from -0.25 to 0.25
- w_out: float32 [2, 256, 47], P(None, 'feat'), may hold values from -0.75 to 0.75
- norm_params: float32 [2, 2, 256], P(None, None, 'feat'), as said below
- m_in: float32 [2, 100, 256], P(None, 'feat'), may hold values from -0.00030517578 to 0.00030517578
- m_mid: float32 [2, 256, 256], P(None, 'feat'), may hold values from -0.00030517578 to 0.00030517578
- m_out: float32 [2, 256, 47], P(None, 'feat'), may hold values from -0.00030517578 to 0.00030517578
- m_norms: float32 [2, 2, 256], P(None, None, 'feat'), may hold values from -0.00061035156 to 0.00061035156
- v_in: float32 [2, 100, 256], P(None, 'feat'), may hold values from 2.4112654e-10 to 3.8580246e-09
- v_mid: float32 [2, 256, 256], P(None, 'feat'), may hold values from 2.4112654e-10 to 3.8580246e-09
- v_out: float32 [2, 256, 47], P(None, 'feat'), may hold values from 2.4112654e-10 to 3.8580246e-09
- v_norms: float32 [2, 2, 256], P(None, None, 'feat'), may hold values from 9.645061e-10 to 1.44675925e-08
Outputs:
- loss_sum: float32 [], replicated
- train_count: float32 [], replicated
- grad_norm: float32 [], replicated
- new_in: float32 [2, 100, 256], P(None, 'feat')
- new_mid: float32 [2, 256, 256], P(None, 'feat')
- new_out: float32 [2, 256, 47], P(None, 'feat')
- new_norms: float32 [2, 2, 256], P(None, None, 'feat')
- first_in: float32 [2, 100, 256], P(None, 'feat')
- first_mid: float32 [2, 256, 256], P(None, 'feat')
- first_out: float32 [2, 256, 47], P(None, 'feat')
- first_norms: float32 [2, 2, 256], P(None, None, 'feat')
- second_in: float32 [2, 100, 256], P(None, 'feat')
- second_mid: float32 [2, 256, 256], P(None, 'feat')
- second_out: float32 [2, 256, 47], P(None, 'feat')
- second_norms: float32 [2, 2, 256], P(None, None, 'feat')
- copy_in: bfloat16 [2, 100, 256], P(None, 'feat')
- copy_mid: bfloat16 [2, 256, 256], P(None, 'feat')
- copy_out: bfloat16 [2, 256, 47], P(None, 'feat')
The draws below stay inside these ranges and needn't reach their ends.
Inputs may be any that keep to these rules, and one draw needn't show every extreme that they name: `norm_params`: gains positive.
All inputs are finite; a program needn't handle non-finite values. No bound on the sum of `inner_adj` or of `bound_adj` or of `keep_slots` on one device may be relied on, other than what follows from the above.
Results may differ from the reference program's by a relative error of at most 0.004.
Values may be sent and summed in bfloat16 or wider, within the bound.
No kernel may reach another device: no remote copies, remote signals or barrier semaphores. Data moves between devices by JAX's collectives and lax.ppermute only.
A program may use at most 128 MiB of HBM per device.

```python
import math
import jax
import jax.numpy as jnp
from jax import lax

IN = 100
HID = 256
CLS = 47
NODES_DEV = 2048
HP = 32
STEP = 5
PARTS_SIZE = 8
NODES = 16384
HALO = 256
NPARAM = 207360


def draw_train_mask(key, part):
    key = jax.random.fold_in(key, 7)
    ticket = jax.random.randint(key, (NODES,), 0, 1000)
    owner = jnp.arange(NODES, dtype=jnp.int32) // NODES_DEV
    level = 250 + 500 * owner // max(PARTS_SIZE - 1, 1)
    return (ticket < level).astype(jnp.int32)


def draw_norm_params(key, part):
    key = jax.random.fold_in(key, 11)
    key_gain, key_shift = jax.random.split(key)
    rising = jnp.arange(HID, dtype=jnp.float32) / HID
    gains = (0.5 + 1.5 * rising) * jax.random.uniform(key_gain, (2, HID), jnp.float32, 0.8, 1.2)
    shifts = 0.3 * jax.random.normal(key_shift, (2, HID), jnp.float32)
    return jnp.stack([gains, shifts], 1)


def plant(array, own_key, smallest, top_value):
    longest = array.shape.index(max(array.shape))
    spots = []
    for shift in (0, 1):
        where = [jax.random.randint(jax.random.fold_in(own_key, axis), (), 0, length) for axis, length in enumerate(array.shape)]
        where[longest] = (where[longest] + shift) % array.shape[longest]
        spots.append(tuple(where))
    return array.at[spots[0]].set(smallest).at[spots[1]].set(top_value)


def levels(stream_key, dims, cuts, least, high):
    level, own = 1.0, jax.random.fold_in(stream_key, 6)
    for axis_at, blocks in cuts:
        steps = jnp.exp(jax.random.uniform(jax.random.fold_in(own, axis_at), (blocks,), jnp.float32, least / len(cuts), high / len(cuts)))
        level = level * jnp.repeat(steps, dims[axis_at] // blocks).reshape([-1 if axis == axis_at else 1 for axis in range(len(dims))])
    return level


def gaussian(own_key, extent, scale, limit, cuts=(), kind=jnp.bfloat16):
    array = jax.random.normal(own_key, extent, jnp.float32) * scale
    if len(cuts) > 0:
        array = levels(own_key, extent, cuts, -0.22, 0.18) * array
    return jnp.clip(array, min=-limit, max=limit).astype(kind)


def setup_inputs(seed: int = 0) -> dict:
    key_of = jax.random.split(jax.random.key(seed), 20)
    return {
        "features": gaussian(key_of[0], (NODES, IN), 1.0, 6.0, ((0, 8), (1, 4)), jnp.float32),
        "inner_adj": plant((jax.random.randint(key_of[1], (NODES, NODES_DEV), 0, NODES_DEV) < min(32, NODES_DEV // 4)).astype(jnp.int32), jax.random.fold_in(key_of[1], 1), 0, 1),
        "bound_adj": plant((jax.random.randint(key_of[2], (NODES, HALO), 0, HALO) < min(64, HALO // 2)).astype(jnp.int32), jax.random.fold_in(key_of[2], 1), 0, 1),
        "keep_slots": plant((jax.random.randint(key_of[3], (PARTS_SIZE, HALO), 0, 10) < 1).astype(jnp.int32), jax.random.fold_in(key_of[3], 1), 0, 1),
        "send_index": plant(jax.random.randint(key_of[4], (PARTS_SIZE, PARTS_SIZE, HP), 0, NODES_DEV), jax.random.fold_in(key_of[4], 1), 0, NODES_DEV - 1).astype(jnp.int32),
        "labels": plant(jax.random.randint(key_of[5], (NODES,), 0, CLS), jax.random.fold_in(key_of[5], 1), 0, CLS - 1).astype(jnp.int32),
        "train_mask": draw_train_mask(jax.random.fold_in(key_of[19], 71), 0),
        "w_in": gaussian(key_of[7], (2, IN, HID), (2 * IN) ** -0.5, 0.4375, ((1, 4),), jnp.float32),
        "w_mid": gaussian(key_of[8], (2, HID, HID), (2 * HID) ** -0.5, 0.25, ((1, 4),), jnp.float32),
        "w_out": gaussian(key_of[9], (2, HID, CLS), (HID // 4) ** -0.5, 0.75, ((1, 4),), jnp.float32),
        "norm_params": draw_norm_params(jax.random.fold_in(key_of[19], 71), 0),
        "m_in": gaussian(key_of[11], (2, IN, HID), (0.01 / NPARAM ** 0.5), 0.00030517578, ((1, 4),), jnp.float32),
        "m_mid": gaussian(key_of[12], (2, HID, HID), (0.01 / NPARAM ** 0.5), 0.00030517578, ((1, 4),), jnp.float32),
        "m_out": gaussian(key_of[13], (2, HID, CLS), (0.01 / NPARAM ** 0.5), 0.00030517578, ((1, 4),), jnp.float32),
        "m_norms": gaussian(key_of[14], (2, 2, HID), (0.02 / NPARAM ** 0.5), 0.00061035156, ((2, 4),), jnp.float32),
        "v_in": jnp.clip(jnp.exp(math.log(3.858024566483209e-09) - 2.7725887 * jax.random.uniform(key_of[15], (2, IN, HID), jnp.float32) ** levels(key_of[15], (2, IN, HID), ((1, 4),), -0.2, 0.2)), 2.4112653540520057e-10, 3.858024566483209e-09),
        "v_mid": jnp.clip(jnp.exp(math.log(3.858024566483209e-09) - 2.7725887 * jax.random.uniform(key_of[16], (2, HID, HID), jnp.float32) ** levels(key_of[16], (2, HID, HID), ((1, 4),), -0.2, 0.2)), 2.4112653540520057e-10, 3.858024566483209e-09),
        "v_out": jnp.clip(jnp.exp(math.log(3.858024566483209e-09) - 2.7725887 * jax.random.uniform(key_of[17], (2, HID, CLS), jnp.float32) ** levels(key_of[17], (2, HID, CLS), ((1, 4),), -0.2, 0.2)), 2.4112653540520057e-10, 3.858024566483209e-09),
        "v_norms": jnp.clip(jnp.exp(math.log(1.4467592457378942e-08) - 2.7080502 * jax.random.uniform(key_of[18], (2, 2, HID), jnp.float32) ** levels(key_of[18], (2, 2, HID), ((2, 4),), -0.2, 0.2)), 9.645061416208023e-10, 1.4467592457378942e-08),
    }


NORM_EPS = 1e-05
PEN_WEIGHT = 0.001
CLIP_LEVEL = 0.01
RATE = 0.05
BETA_ONE = 0.5
BETA_TWO = 0.5
ADAM_EPS = 1e-08
DECAY = 0.01
HIGH = lax.Precision.HIGHEST

@jax.custom_vjp
def low(v):
    return lax.optimization_barrier(v.astype(jnp.bfloat16)).astype(jnp.float32)

@jax.custom_vjp
def low_back(v):
    return v

def low_keep(v):
    return (low(v), None)

def low_pass(kept, grad):
    return (grad,)

def back_keep(v):
    return (v, None)

def back_low(kept, grad):
    return (low(grad),)
low.defvjp(low_keep, low_pass)
low_back.defvjp(back_keep, back_low)

def dense(operand, weight_mat):
    return jnp.dot(operand, weight_mat, precision=HIGH, preferred_element_type=jnp.float32)

def halo_take(values, send_index):
    owners = jnp.arange(PARTS_SIZE, dtype=jnp.int32)[None, :, None] * NODES_DEV
    take_index = jnp.transpose(send_index, (1, 0, 2)) + owners
    return values[take_index.reshape(PARTS_SIZE, HALO)]

def sage_layer(hidden, weight, gain, shift, graph_data, send_index):
    inner_f, edge_f, inv_deg = graph_data
    feat_width = hidden.shape[1]
    h_low = low(hidden)
    halo_in = low_back(halo_take(h_low, send_index))
    summed = jnp.einsum('pij,pjf->pif', inner_f, h_low.reshape(PARTS_SIZE, NODES_DEV, feat_width), precision=HIGH)
    summed = summed + jnp.einsum('pih,phf->pif', edge_f, halo_in, precision=HIGH)
    summed = low_back(summed)
    mean_low = low(summed * inv_deg[:, :, None]).reshape(NODES, feat_width)
    w_low = low(weight)
    joined = low_back(dense(h_low, w_low[0]) + dense(mean_low, w_low[1]))
    if gain is None:
        return joined
    center = lax.optimization_barrier(jnp.mean(joined, -1, keepdims=True))
    spread = lax.optimization_barrier(jnp.mean(joined * joined, -1, keepdims=True)) - center * center
    normed = (joined - center) * lax.rsqrt(spread + NORM_EPS) * gain + shift
    return jax.nn.silu(normed)

def adam_step(param, grad, first, second):
    first_new = BETA_ONE * first + (1.0 - BETA_ONE) * grad
    second_new = BETA_TWO * second + (1.0 - BETA_TWO) * grad * grad
    first_hat = first_new / (1.0 - BETA_ONE ** STEP)
    second_hat = second_new / (1.0 - BETA_TWO ** STEP)
    fresh = param - RATE * (first_hat / (jnp.sqrt(second_hat) + ADAM_EPS) + DECAY * param)
    return (fresh, first_new, second_new)

def reference(features, inner_adj, bound_adj, keep_slots, send_index, labels, train_mask, w_in, w_mid, w_out, norm_params, m_in, m_mid, m_out, m_norms, v_in, v_mid, v_out, v_norms):
    inner_f = inner_adj.reshape(PARTS_SIZE, NODES_DEV, NODES_DEV).astype(jnp.float32)
    edge_int = bound_adj.reshape(PARTS_SIZE, NODES_DEV, HALO) * keep_slots[:, None, :]
    edge_f = edge_int.astype(jnp.float32)
    degree = (lax.optimization_barrier(jnp.sum(inner_adj, 1)).reshape(PARTS_SIZE, NODES_DEV) + lax.optimization_barrier(jnp.sum(edge_int, 2))).astype(jnp.float32)
    inv_deg = 1.0 / jnp.maximum(degree, 1.0)
    graph_data = (inner_f, edge_f, inv_deg)
    weights = train_mask.astype(jnp.float32)
    row_deg = lax.optimization_barrier(jnp.sum(edge_f, 2))
    col_deg = lax.optimization_barrier(jnp.sum(edge_f, 1))

    def loss_fn(w_first, w_second, w_head, norm_all):
        hidden = sage_layer(features, w_first, norm_all[0, 0], norm_all[0, 1], graph_data, send_index)
        hidden = sage_layer(hidden, w_second, norm_all[1, 0], norm_all[1, 1], graph_data, send_index)
        logits = sage_layer(hidden, w_head, None, None, graph_data, send_index)
        row_top = lax.optimization_barrier(jnp.max(logits, -1, keepdims=True))
        log_total = row_top[:, 0] + jnp.log(lax.optimization_barrier(jnp.sum(jnp.exp(logits - row_top), -1)))
        target = jnp.take_along_axis(logits, labels[:, None], 1)[:, 0]
        ce_sum = jnp.sum(weights * (log_total - target))
        count_all = jnp.sum(weights)
        pred_low = low(logits)
        halo_pred = low_back(halo_take(pred_low, send_index))
        own_pred = pred_low.reshape(PARTS_SIZE, NODES_DEV, CLS)
        cross_term = jnp.einsum('pic,phc->pih', own_pred, halo_pred, precision=HIGH)
        penalty = jnp.sum(row_deg * lax.optimization_barrier(jnp.sum(own_pred * own_pred, -1))) - 2.0 * jnp.sum(edge_f * cross_term)
        penalty = penalty + jnp.sum(col_deg * lax.optimization_barrier(jnp.sum(halo_pred * halo_pred, -1)))
        total_loss = ce_sum + PEN_WEIGHT * penalty
        return (total_loss / count_all, (total_loss, count_all))
    params = (w_in, w_mid, w_out, norm_params)
    mean_loss, pullback, aux_out = jax.vjp(loss_fn, *params, has_aux=True)
    grads = pullback(jnp.ones_like(mean_loss))
    square_sum = jnp.sum(grads[0] * grads[0]) + jnp.sum(grads[1] * grads[1])
    square_sum = square_sum + jnp.sum(grads[2] * grads[2]) + jnp.sum(grads[3] * grads[3])
    grad_norm = jnp.sqrt(square_sum)
    factor = jnp.minimum(1.0, CLIP_LEVEL / (grad_norm + 1e-06))
    firsts = (m_in, m_mid, m_out, m_norms)
    seconds = (v_in, v_mid, v_out, v_norms)
    results = [adam_step(params[item], grads[item] * factor, firsts[item], seconds[item]) for item in range(4)]
    return (aux_out[0], aux_out[1], grad_norm, results[0][0], results[1][0], results[2][0], results[3][0], results[0][1], results[1][1], results[2][1], results[3][1], results[0][2], results[1][2], results[2][2], results[3][2], results[0][0].astype(jnp.bfloat16), results[1][0].astype(jnp.bfloat16), results[2][0].astype(jnp.bfloat16))
```

```python
import functools

import jax
import jax.numpy as jnp
from jax import lax
from jax.experimental import pallas as pl
from jax.experimental.pallas import tpu as pltpu
from jax.sharding import PartitionSpec as P

HID = 256
STEP = 5

NORM_EPS = 1e-05
PEN_WEIGHT = 0.001
CLIP_LEVEL = 0.01
RATE = 0.05
BETA_ONE = 0.5
BETA_TWO = 0.5
ADAM_EPS = 1e-08
DECAY = 0.01

BF = jnp.bfloat16
F32 = jnp.float32
LANE = 128
FEAT_PAD = 32
MIB = 1 << 20
CONVERT_TILE = 256

VMEM = pl.BlockSpec(memory_space=pltpu.VMEM)
SMEM = pl.BlockSpec(memory_space=pltpu.SMEM)
ANY = pl.BlockSpec(memory_space=pl.ANY)


def dot_nn(a, b):
    return jnp.dot(a, b, preferred_element_type=F32)


def dot_tn(a, b):
    return lax.dot_general(a, b, (((0,), (0,)), ((), ())), preferred_element_type=F32)


def dot_nt(a, b):
    return lax.dot_general(a, b, (((1,), (1,)), ((), ())), preferred_element_type=F32)


def iota(shape, axis):
    return lax.broadcasted_iota(jnp.int32, shape, axis)


def place(rows, cols, shift, turned=False):
    dims = (cols, rows) if turned else (rows, cols)
    return (iota(dims, int(turned)) + shift == iota(dims, int(not turned))).astype(F32).astype(BF)


def widen(x):
    return x.astype(F32)


def bf_parts(x, count):
    parts = []
    for _ in range(count):
        part = x.astype(BF)
        parts.append(part)
        x = x - widen(part)
    return parts


def rows_of(i, tile):
    return pl.ds(pl.multiple_of(i * tile, tile), tile)


def call(kernel, outs, *args, mib=24, flops=0, smem_in=(), any_in=(), smem_out=(), scratch=()):
    size = sum(a.size * a.dtype.itemsize for a in (*args, *outs))
    return pl.pallas_call(
        kernel,
        out_shape=outs,
        in_specs=[SMEM if i in smem_in else ANY if i in any_in else VMEM for i in range(len(args))],
        out_specs=[SMEM if i in smem_out else VMEM for i in range(len(outs))],
        scratch_shapes=list(scratch),
        cost_estimate=pl.CostEstimate(flops=flops, bytes_accessed=size // 4, transcendentals=0),
        compiler_params=pltpu.CompilerParams(vmem_limit_bytes=mib * MIB),
    )(*args)


def shape(*dims, dtype=F32):
    return jax.ShapeDtypeStruct(dims, dtype)


def pack_kernel(idx_ref, feat_ref, w_in_ref, w_mid_ref, w_out_ref, norm_ref, at_ref, sel_ref, pack_ref, at_out):
    at_out[0] = at_ref[0]
    slots, nodes = sel_ref.shape
    parts, each = idx_ref.shape[1:]
    eye = iota((each, each), 0) == iota((each, each), 1)
    for p in range(parts):
        column = jnp.sum(jnp.where(eye, idx_ref[0, p : p + 1, :].astype(F32), 0.0), 1, keepdims=True)
        hot = iota((each, nodes), 1) == column.astype(jnp.int32)
        sel_ref[p * each : (p + 1) * each, :] = hot.astype(F32).astype(BF)

    width, share = feat_ref.shape[0], w_mid_ref.shape[1]
    rows = dot_nn(place(FEAT_PAD, width, 0), feat_ref[...].astype(BF))
    ones = iota((FEAT_PAD, nodes), 0) == FEAT_PAD - 1
    blocks = [jnp.zeros((FEAT_PAD, HID), F32) for _ in range(3)]
    for layer in range(2):
        for p, part in enumerate(bf_parts(norm_ref[layer], 3)):
            part = dot_nn(part, place(share, HID, 0)).astype(BF)
            blocks[p] = blocks[p] + dot_nn(place(2, FEAT_PAD, NORM_AT + 2 * layer, turned=True), part)
    blocks.append(jnp.zeros((FEAT_PAD, nodes - 3 * HID), F32))
    pack_ref[0:FEAT_PAD, :] = (jnp.where(ones, 1.0, rows) + jnp.concatenate(blocks, 1)).astype(BF)
    for k in range(2):
        for r in range(0, share, 16):
            b = (k * share + r) // 16
            pack_ref[MID_AT : MID_AT + 16, b * HID : (b + 1) * HID] = w_mid_ref[k, r : r + 16, :].astype(BF)
        spread = dot_nn(place(FEAT_PAD, width, 0), w_in_ref[:, k, :].astype(BF)).astype(BF)
        for r in range(0, FEAT_PAD, 16):
            b = (share + k * FEAT_PAD + r) // 16
            pack_ref[OUT_AT : OUT_AT + 16, b * HID : (b + 1) * HID] = spread[r : r + 16, :]
        classes = w_out_ref.shape[0]
        turned = dot_tn(w_out_ref[:, k, :].astype(BF), place(classes, LANE, 0)).astype(BF)
        for r in range(0, share, 16):
            b = r // 16
            pack_ref[OUT_AT : OUT_AT + 16, b * HID + k * LANE : b * HID + (k + 1) * LANE] = turned[r : r + 16, :]


MID_AT = FEAT_PAD
OUT_AT = FEAT_PAD + 16
NORM_AT = FEAT_PAD - 6
PACK_ROWS = FEAT_PAD + 32


def convert_kernel(adj_ref, bound_ref, keep_ref, after_ref, adj_out, edge_out):
    del after_ref
    adj_out[...] = adj_ref[...].astype(F32).astype(BF)
    edge_out[...] = (bound_ref[...] * keep_ref[...]).astype(F32).astype(BF)


def convert(adj, bound, keep, after):
    rows, nodes = adj.shape
    halo = bound.shape[1]

    def tile(width):
        return pl.BlockSpec((CONVERT_TILE, width), lambda i: (i, 0))

    return pl.pallas_call(
        convert_kernel,
        grid=(rows // CONVERT_TILE,),
        in_specs=[tile(nodes), tile(halo), pl.BlockSpec((1, halo), lambda i: (0, 0)), pl.BlockSpec(memory_space=pl.ANY)],
        out_specs=[tile(nodes), tile(halo)],
        out_shape=[shape(rows, nodes, dtype=BF), shape(rows, halo, dtype=BF)],
        cost_estimate=pl.CostEstimate(flops=0, bytes_accessed=6 * MIB, transcendentals=0),
        compiler_params=pltpu.CompilerParams(vmem_limit_bytes=16 * MIB),
    )(adj, bound, keep, after)


def spread_kernel(packed_ref, sel_ref, after_ref, ft_ref, send_ref):
    del after_ref
    feats = packed_ref.shape[0]
    row = iota((FEAT_PAD, ft_ref.shape[1]), 0)
    for f in range(feats):
        rows = widen(packed_ref[f, 0:FEAT_PAD, :])
        keep = (row < NORM_AT) | (row == FEAT_PAD - 1)
        ft_ref[f * FEAT_PAD : (f + 1) * FEAT_PAD, :] = jnp.where(keep, rows, 0.0).astype(BF)
    send_ref[...] = dot_nt(sel_ref[...], ft_ref[...]).astype(BF)


def place_back(share, f):
    row, col = iota((HID, HID), 0), iota((HID, HID), 1)
    return ((row + f * share == col) & (row < share)).astype(F32).astype(BF)


def unpack(packed_ref, win_ref, wmid_ref, wout_ref, norm_ref):
    feats = packed_ref.shape[0]
    share = HID // feats
    norms = jnp.zeros((8, HID), F32)
    pick = place(8, FEAT_PAD, NORM_AT)
    for f in range(feats):
        for k in range(2):
            for r in range(0, share, 16):
                b = (k * share + r) // 16
                wmid_ref[k, f * share + r : f * share + r + 16, :] = packed_ref[f, MID_AT : MID_AT + 16, b * HID : (b + 1) * HID]
                b = r // 16
                wout_ref[k, f * share + r : f * share + r + 16, :] = packed_ref[
                    f, OUT_AT : OUT_AT + 16, b * HID + k * LANE : b * HID + (k + 1) * LANE
                ]
            for r in range(0, FEAT_PAD, 16):
                b = (share + k * FEAT_PAD + r) // 16
                win_ref[k, f * FEAT_PAD + r : f * FEAT_PAD + r + 16, :] = packed_ref[
                    f, OUT_AT : OUT_AT + 16, b * HID : (b + 1) * HID
                ]
        for p in range(3):
            part = dot_nn(pick, packed_ref[f, 0:FEAT_PAD, p * HID : (p + 1) * HID]).astype(BF)
            norms = norms + dot_nn(part, place_back(share, f))
    norm_ref[...] = norms


TILE = 1024


def both(x):
    return jnp.concatenate([x, x], 1)


def loop(count, tile, body, carry=0):
    return lax.fori_loop(0, count // tile, lambda i, c: body(rows_of(i, tile), c), carry)


def norm_forward(joined, norm_ref, layer):
    center = jnp.sum(joined, 1, keepdims=True) * (1.0 / HID)
    spread = jnp.sum(joined * joined, 1, keepdims=True) * (1.0 / HID) - center * center
    inv_std = lax.rsqrt(spread + NORM_EPS)
    x_hat = (joined - center) * inv_std
    normed = x_hat * norm_ref[2 * layer : 2 * layer + 1, :] + norm_ref[2 * layer + 1 : 2 * layer + 2, :]
    gate = 0.5 * jnp.tanh(0.5 * normed) + 0.5
    return inv_std, x_hat, normed * gate, gate * (1.0 + normed * (1.0 - gate))


def keep_norm(s, parts, xhat_ref, slope_ref, istd_ref, h_ref):
    inv_std, x_hat, hidden, slope = parts
    xhat_ref[s, :] = x_hat
    slope_ref[s, :] = slope
    istd_ref[s, :] = jnp.broadcast_to(inv_std, (x_hat.shape[0], LANE))
    h_ref[s, :] = hidden.astype(BF)


def first_kernel(adj_ref, edge_ref, recv_ref, packed_ref, ft_ref, sel_ref,
                 row_ref, col_ref, wmid_ref, wout_ref, norm_ref,
                 mean_ref, xhat_ref, slope_ref, istd_ref, h_ref, invd_ref, send_ref, win_ref):
    nodes, halo = edge_ref.shape
    unpack(packed_ref, win_ref, wmid_ref, wout_ref, norm_ref)

    row_ref[...] = dot_nn(edge_ref[...], jnp.ones((halo, LANE), BF))
    col_ref[...] = dot_tn(edge_ref[...], jnp.ones((nodes, LANE), BF))

    def gather(s, _):
        summed = dot_nt(adj_ref[s, :], ft_ref[...]) + dot_nn(edge_ref[s, :], recv_ref[...])
        inv_deg = 1.0 / jnp.maximum(summed[:, LANE - 1 : LANE], 1.0)
        invd_ref[s, :] = jnp.broadcast_to(inv_deg, summed.shape)
        mean_ref[s, :] = (summed * inv_deg).astype(BF)
        return 0

    loop(nodes, TILE, gather)

    def apply(s, _):
        joined = dot_tn(ft_ref[:, s], win_ref[0]) + dot_nn(mean_ref[s, :], win_ref[1])
        keep_norm(s, norm_forward(joined, norm_ref, 0), xhat_ref, slope_ref, istd_ref, h_ref)
        return 0

    loop(nodes, TILE, apply)
    send_ref[...] = dot_nn(sel_ref[...], h_ref[...]).astype(BF)


def gather_mean(adj_ref, hin_ref, edge_ref, halo_ref, invd_ref, mean_ref):
    def gather(s, _):
        summed = dot_nn(adj_ref[s, :], hin_ref[...]) + dot_nn(edge_ref[s, :], halo_ref[...])
        mean_ref[s, :] = (summed * both(invd_ref[s, :])).astype(BF)
        return 0

    loop(adj_ref.shape[0], TILE, gather)


def second_kernel(adj_ref, edge_ref, halo_ref, hin_ref, w_ref, norm_ref, invd_ref, sel_ref,
                  mean_ref, xhat_ref, slope_ref, istd_ref, h_ref, send_ref):
    gather_mean(adj_ref, hin_ref, edge_ref, halo_ref, invd_ref, mean_ref)

    def apply(s, _):
        joined = dot_nn(hin_ref[s, :], w_ref[0]) + dot_nn(mean_ref[s, :], w_ref[1])
        keep_norm(s, norm_forward(joined, norm_ref, 1), xhat_ref, slope_ref, istd_ref, h_ref)
        return 0

    loop(adj_ref.shape[0], TILE, apply)
    send_ref[...] = dot_nn(sel_ref[...], h_ref[...]).astype(BF)


def split_count(x):
    high = jnp.floor(x * (1.0 / 256.0))
    return high, x - 256.0 * high


def head_kernel(adj_ref, edge_ref, halo_ref, hin_ref, w_ref, invd_ref, sel_ref, mask_ref, col_ref,
                mean_ref, logit_ref, pred_ref, cross_ref, mine_ref, send_ref):
    gather_mean(adj_ref, hin_ref, edge_ref, halo_ref, invd_ref, mean_ref)

    def apply(s, _):
        logits = dot_nn(hin_ref[s, :], w_ref[0]) + dot_nn(mean_ref[s, :], w_ref[1])
        logit_ref[s, :] = logits
        pred_ref[s, :] = logits.astype(BF)
        return 0

    loop(adj_ref.shape[0], TILE, apply)
    mine = dot_nn(sel_ref[...], pred_ref[...])
    mine_ref[...] = mine
    cross = dot_tn(edge_ref[...], pred_ref[...])
    cross_ref[...] = cross
    high, low = bf_parts(cross, 2)
    count = jnp.sum(mask_ref[...].astype(F32), keepdims=True)
    lane = iota(mine.shape, 1)
    count_high, count_low = split_count(count)
    col_high, col_low = split_count(col_ref[...])
    extra = jnp.where(lane == 64, count_high, 0.0) + jnp.where(lane == 65, count_low, 0.0)
    extra = extra + jnp.where(lane == 66, col_high, 0.0) + jnp.where(lane == 67, col_low, 0.0)
    send_ref[:, 0:LANE] = (mine + pltpu.roll(widen(low), 64, 1)).astype(BF)
    send_ref[:, LANE:] = (widen(high) + extra).astype(BF)


def spread_row(values, row):
    pick = (iota(values.shape, 0) == row).astype(F32).astype(BF)
    return dot_tn(values.astype(F32).astype(BF), pick)


def logit_grad_kernel(logit_ref, label_ref, mask_ref, row_ref, pred_ref, edge_ref, recv_ref, mine_ref, cross_ref, col_ref,
                      sel_ref, w_ref, invd_ref,
                      grad_ref, gs_ref, send_ref, loss_ref, hp_ref, ret_ref, lab_ref, wgt_ref, *, classes, each):
    slots = mine_ref.shape[0]
    nodes = logit_ref.shape[0]
    first, second = widen(recv_ref[:, 0:LANE]), widen(recv_ref[:, LANE:])
    lane = iota((slots, LANE), 1)
    low_half = lane < 64
    halo_pred = jnp.where(low_half, first, 0.0)
    back_cross = jnp.where(low_half, second + pltpu.roll(first, 64, 1), 0.0)
    count = 256.0 * jnp.sum(jnp.where(lane == 64, second, 0.0), keepdims=True)
    count = (count + jnp.sum(jnp.where(lane == 65, second, 0.0), keepdims=True)) * (1.0 / each)
    col_back = 256.0 * second[:, 66:67] + second[:, 67:68]
    scale = 2.0 * PEN_WEIGHT / count
    inv_count = 1.0 / count
    hp_ref[...] = halo_pred.astype(BF)
    ret_ref[...] = (scale * (col_back * mine_ref[...] - back_cross)).astype(BF)
    pen = jnp.sum(col_ref[...] * (halo_pred * halo_pred), keepdims=True)
    pen = pen - 2.0 * jnp.sum(halo_pred * cross_ref[...], keepdims=True)
    for r in range(nodes // LANE):
        lab_ref[r * LANE : (r + 1) * LANE, :] = spread_row(label_ref[...], r)
        wgt_ref[r * LANE : (r + 1) * LANE, :] = spread_row(mask_ref[...], r)

    def body(s, carry):
        ce_sum, pen_sum = carry
        logits = logit_ref[s, :]
        lane = iota(logits.shape, 1)
        real = lane < classes
        top = jnp.max(jnp.where(real, logits, -jnp.inf), 1, keepdims=True)
        shifted = jnp.where(real, jnp.exp(jnp.where(real, logits - top, 0.0)), 0.0)
        total = jnp.sum(shifted, 1, keepdims=True)
        hot = (lane.astype(F32) == lab_ref[s, :]).astype(F32)
        target = jnp.sum(logits * hot, 1, keepdims=True)
        weight = wgt_ref[s, :]
        ce_sum = ce_sum + jnp.sum(weight[:, 0:1] * (top + jnp.log(total) - target), keepdims=True)
        pred = widen(pred_ref[s, :])
        drawn = row_ref[s, :] * pred
        pen_sum = pen_sum + jnp.sum(drawn * pred, keepdims=True)
        own = drawn - dot_nn(edge_ref[s, :], hp_ref[...])
        back = dot_tn(sel_ref[:, s], ret_ref[...])
        grad = ((inv_count * weight) * (shifted * (1.0 / total) - hot) + scale * own + back).astype(BF)
        grad_ref[s, :] = grad
        gs_ref[s, :] = (dot_nt(grad, w_ref[1]) * both(invd_ref[s, :])).astype(BF)
        return ce_sum, pen_sum

    zero = jnp.zeros((1, 1), F32)
    ce_sum, pen_sum = loop(nodes, TILE, body, (zero, zero))
    row = iota((8, LANE), 0)
    loss_ref[...] = (jnp.where(row == 0, ce_sum, 0.0) + jnp.where(row == 1, pen + pen_sum, 0.0)
                     + jnp.where(row == 2, count, 0.0))
    send_ref[...] = dot_tn(edge_ref[...], gs_ref[...]).astype(BF)


BACK_TILE = 512


def layer_back(adj_ref, gs_ref, grad_ref, w_ref, sel_ref, halo_ref, slope_ref, xhat_ref, istd_ref, norm_ref, layer, own_ref, gj_ref):
    nodes = adj_ref.shape[0]

    def pull(s, _):
        own_ref[s, :] = (dot_tn(adj_ref[:, s], gs_ref[...]) + dot_nt(grad_ref[s, :], w_ref[0])
                         + dot_tn(sel_ref[:, s], halo_ref[...]))
        return 0

    loop(nodes, BACK_TILE, pull)

    def body(s, carry):
        gain_sum, bias_sum = carry
        grad_pre = own_ref[s, :] * slope_ref[s, :]
        x_hat = xhat_ref[s, :]
        grad_x = grad_pre * norm_ref[2 * layer : 2 * layer + 1, :]
        mean_one = jnp.sum(grad_x, 1, keepdims=True) * (1.0 / HID)
        mean_two = jnp.sum(grad_x * x_hat, 1, keepdims=True) * (1.0 / HID)
        gj_ref[s, :] = (both(istd_ref[s, :]) * (grad_x - mean_one - x_hat * mean_two)).astype(BF)
        gain_sum = gain_sum + jnp.sum(grad_pre * x_hat, 0, keepdims=True)
        bias_sum = bias_sum + jnp.sum(grad_pre, 0, keepdims=True)
        return gain_sum, bias_sum

    zero = jnp.zeros((1, HID), F32)
    return loop(nodes, TILE, body, (zero, zero))


def second_back_kernel(adj_ref, gsin_ref, grad_ref, wout_ref, recv_ref, sel_ref, slope_ref, xhat_ref, istd_ref, norm_ref, w_ref,
                       invd_ref, edge_ref, h_two_ref, mean_head_ref, h_one_ref, mean_two_ref, at_ref,
                       gj_ref, gs_ref, send_ref, sums_ref, own_ref, full_ref, head_ref, *, each):
    gain_sum, bias_sum = layer_back(
        adj_ref, gsin_ref, grad_ref, wout_ref, sel_ref, recv_ref, slope_ref, xhat_ref, istd_ref, norm_ref, 1, own_ref, gj_ref
    )
    row = iota((8, HID), 0)
    sums_ref[...] = jnp.where(row == 2, gain_sum, 0.0) + jnp.where(row == 3, bias_sum, 0.0)

    def body(s, _):
        gs_ref[s, :] = (dot_nt(gj_ref[s, :], w_ref[1]) * both(invd_ref[s, :])).astype(BF)
        return 0

    loop(adj_ref.shape[0], TILE, body)
    parts = send_ref.shape[0]
    send_ref[:, 0:each, :] = dot_tn(edge_ref[...], gs_ref[...]).astype(BF).reshape(parts, each, HID)
    head_ref[:, 0:LANE] = dot_tn(h_two_ref[...], grad_ref[...])
    head_ref[:, LANE:] = dot_tn(mean_head_ref[...], grad_ref[...])
    full_ref[0] = dot_tn(h_one_ref[...], gj_ref[...])
    full_ref[1] = dot_tn(mean_two_ref[...], gj_ref[...])
    share = HID // FEATS
    start = at_ref[0] * share
    for q in range(parts):
        if q * 16 < 2 * share:
            k, r = divmod(q * 16, share)
            send_ref[q, each : each + 16, :] = full_ref[k, pl.ds(pl.multiple_of(start + r, 16), 16), :].astype(BF)
            rows = head_ref[pl.ds(pl.multiple_of(start + q * 8, 8), 8), :]
            high, low = bf_parts(rows, 2)
            send_ref[q, each + 16 : each + 32, :] = jnp.concatenate([widen(high), widen(low)], 0).astype(BF)
        else:
            send_ref[q, each : each + 32, :] = jnp.zeros((32, HID), BF)


FEATS = 4


def first_back_kernel(adj_ref, gsin_ref, grad_ref, w_ref, recv_ref, sel_ref, slope_ref, xhat_ref, istd_ref, norm_ref,
                      ft_ref, mean_ref, loss_ref, sums_ref, at_ref,
                      send_ref, gj_ref, own_ref, full_ref, halo_ref, *, each):
    parts = recv_ref.shape[0]
    halo_ref[...] = recv_ref[:, 0:each, :].reshape(halo_ref.shape)
    gain_sum, bias_sum = layer_back(
        adj_ref, gsin_ref, grad_ref, w_ref, sel_ref, halo_ref, slope_ref, xhat_ref, istd_ref, norm_ref, 0, own_ref, gj_ref
    )
    row = iota((8, HID), 0)
    sums = sums_ref[...] + jnp.where(row == 0, gain_sum, 0.0) + jnp.where(row == 1, bias_sum, 0.0)
    full_ref[0] = dot_nn(ft_ref[...], gj_ref[...])
    full_ref[1] = dot_tn(mean_ref[...], gj_ref[...])
    at = rows_of(at_ref[0], FEAT_PAD)
    mid = jnp.zeros((16, HID), F32)
    out = jnp.zeros((16, HID), F32)
    for q in range(parts):
        mid = mid + widen(recv_ref[q, each : each + 16, :])
        out = out + widen(recv_ref[q, each + 16 : each + 32, :])
    out = out + pltpu.roll(out, 8, 0)
    mid_high, mid_low = bf_parts(mid, 2)
    out_high, out_low = bf_parts(out, 2)
    out = jnp.where(iota((16, HID), 0) < 8, widen(out_high), widen(out_low))
    high, low = bf_parts(sums, 2)
    lane = iota((8, HID), 1)
    tail = jnp.zeros((8, HID), F32)
    for which in range(2):
        for p, part in enumerate(bf_parts(jnp.broadcast_to(loss_ref[which : which + 1, 0:1], (8, HID)), 3)):
            tail = tail + jnp.where((lane == p) & (row == which), widen(part), 0.0)
    message = jnp.concatenate(
        [full_ref[0, at, :], full_ref[1, at, :], jnp.where(row < 4, widen(high), 0.0) + pltpu.roll(widen(low), 4, 0), tail,
         widen(mid_high), widen(mid_low), out], 0
    ).astype(BF)
    for q in range(parts):
        send_ref[q] = message


NORM_ROW = 2 * FEAT_PAD
CHUNK_ROW = NORM_ROW + 16
MESSAGE_ROWS = CHUNK_ROW + 48


def total_kernel(recv_ref, grads_ref, mid_ref, out_ref, square_ref, *, width):
    parts = recv_ref.shape[0]
    grads = jnp.zeros((CHUNK_ROW, HID), F32)
    for q in range(parts):
        grads = grads + widen(recv_ref[q, 0:CHUNK_ROW, :])
    norms = grads[NORM_ROW : NORM_ROW + 8, :]
    norms = jnp.where(iota((8, HID), 0) < 4, norms + pltpu.roll(norms, 4, 0), 0.0)
    grads_ref[...] = grads
    grads_ref[NORM_ROW : NORM_ROW + 8, :] = norms
    for q in range(mid_ref.shape[0] // 16):
        at = CHUNK_ROW
        mid_ref[q * 16 : q * 16 + 16, :] = widen(recv_ref[q, at : at + 16, :]) + widen(recv_ref[q, at + 16 : at + 32, :])
        rows = widen(recv_ref[q, at + 32 : at + 48, :])
        out_ref[q * 8 : q * 8 + 8, :] = rows[0:8, :] + rows[8:16, :]
    weight_row = (iota((NORM_ROW, HID), 0) & (FEAT_PAD - 1)) < width
    first = jnp.where(weight_row, grads[0:NORM_ROW, :], 0.0)
    square = jnp.sum(first * first, keepdims=True)
    square = square + jnp.sum(mid_ref[...] * mid_ref[...], keepdims=True)
    square = square + jnp.sum(out_ref[...] * out_ref[...], keepdims=True)
    row = iota((8, LANE), 0)
    square_ref[...] = jnp.where(row == 1, jnp.sum(norms * norms, keepdims=True), square)


def adam(param, grad, first, second):
    first_new = BETA_ONE * first + (1.0 - BETA_ONE) * grad
    second_new = BETA_TWO * second + (1.0 - BETA_TWO) * grad * grad
    first_hat = first_new / (1.0 - BETA_ONE**STEP)
    second_hat = second_new / (1.0 - BETA_TWO**STEP)
    fresh = param - RATE * (first_hat / (jnp.sqrt(second_hat) + ADAM_EPS) + DECAY * param)
    return fresh, first_new, second_new


def update_kernel(grads_ref, gmid_ref, gout_ref, sq0_ref, sq1_ref, sq2_ref, sq3_ref, loss_ref,
                  w_in, w_mid, w_out, norm, m_in, m_mid, m_out, m_norm, v_in, v_mid, v_out, v_norm, at_ref,
                  loss_out, count_out, gnorm_out,
                  nw_in, nw_mid, nw_out, nnorm, nm_in, nm_mid, nm_out, nm_norm, nv_in, nv_mid, nv_out, nv_norm,
                  c_in, c_mid, c_out):
    tail = jnp.sum(grads_ref[NORM_ROW + 8 : NORM_ROW + 16, :], 1, keepdims=True)
    loss_out[...] = tail[0:1] + PEN_WEIGHT * tail[1:2]
    count_out[...] = loss_ref[2:3, 0:1]
    square = (sq0_ref[0:1, 0:1] + sq1_ref[0:1, 0:1]) + (sq2_ref[0:1, 0:1] + sq3_ref[0:1, 0:1])
    grad_norm = jnp.sqrt(square + sq0_ref[1:2, 0:1])
    gnorm_out[...] = grad_norm
    factor = jnp.minimum(1.0, CLIP_LEVEL / (grad_norm + 1e-06))

    def step(index, grad, w, m, v, nw, nm, nv, copy):
        fresh, first, second = adam(w[index], grad * factor, m[index], v[index])
        nw[index], nm[index], nv[index] = fresh, first, second
        if copy is not None:
            copy[index] = fresh.astype(BF)

    every = slice(None)
    width, _, share = w_in.shape[0], 2, w_mid.shape[1]
    classes = w_out.shape[0]
    for k in range(2):
        step((every, k, every), grads_ref[k * FEAT_PAD : k * FEAT_PAD + width, :], w_in, m_in, v_in, nw_in, nm_in, nv_in, c_in)
        step(k, gmid_ref[k * share : (k + 1) * share, :], w_mid, m_mid, v_mid, nw_mid, nm_mid, nv_mid, c_mid)
        turned = jnp.transpose(gout_ref[:, k * LANE : (k + 1) * LANE])[0:classes, :]
        step((every, k, every), turned, w_out, m_out, v_out, nw_out, nm_out, nv_out, c_out)
    whole = grads_ref[NORM_ROW : NORM_ROW + 8, :]
    mine = jnp.zeros((8, share), F32)
    for f in range(HID // share):
        mine = mine + jnp.where(at_ref[0] == f, whole[:, f * share : (f + 1) * share], 0.0)
    for layer in range(2):
        step(layer, mine[2 * layer : 2 * layer + 2, :], norm, m_norm, v_norm, nnorm, nm_norm, nv_norm, None)


def exchange(x, parts):
    return lax.all_to_all(x.reshape(parts, -1, x.shape[-1]), "dom", split_axis=0, concat_axis=0, tiled=True)


def native(w_in, w_mid, w_out, norm):
    return (jnp.transpose(w_in, (1, 0, 2)), w_mid, jnp.transpose(w_out, (2, 0, 1)), norm)


def restore(w_in, w_mid, w_out, *norm):
    return (jnp.transpose(w_in, (1, 0, 2)), w_mid, jnp.transpose(w_out, (1, 2, 0)), *norm)


def shards(
    features,
    inner_adj,
    bound_adj,
    keep_slots,
    send_index,
    labels,
    train_mask,
    w_in,
    w_mid,
    w_out,
    norm_params,
    m_in,
    m_mid,
    m_out,
    m_norms,
    v_in,
    v_mid,
    v_out,
    v_norms,
    *,
    parts,
    feats,
):
    nodes = features.shape[0]
    each = send_index.shape[2]
    halo = parts * each
    classes = w_out.shape[2]
    share = w_mid.shape[1]
    width = features.shape[1]
    run = functools.partial(call, mib=24 if parts <= 16 else 48)
    labels = labels.reshape(nodes // LANE, LANE)
    mask = train_mask.reshape(nodes // LANE, LANE)
    params = native(w_in, w_mid, w_out, norm_params)
    firsts = native(m_in, m_mid, m_out, m_norms)
    seconds = native(v_in, v_mid, v_out, v_norms)
    feat_at = lax.axis_index("feat").astype(jnp.int32).reshape(1)

    def bf(*dims):
        return shape(*dims, dtype=BF)

    sel, packed, at = run(
        pack_kernel, [bf(halo, nodes), bf(PACK_ROWS, nodes), shape(1, dtype=jnp.int32)],
        send_index, features.T, *params, feat_at, smem_in=(6,), smem_out=(2,),
    )
    packed = lax.all_gather(packed, "feat", axis=0)
    adj, edge = convert(inner_adj, bound_adj, keep_slots, packed)
    ft, send = run(spread_kernel, [bf(feats * FEAT_PAD, nodes), bf(halo, LANE)], packed, sel, adj, any_in=(2,))
    recv = exchange(send, parts).reshape(halo, LANE)
    (row_deg, col_deg, wmid, wout, norms,
     mean_one, xhat_one, slope_one, istd_one, h_one, inv_deg, send) = run(
        first_kernel,
        [shape(nodes, LANE), shape(halo, LANE), bf(2, HID, HID), bf(2, HID, LANE), shape(8, HID),
         bf(nodes, LANE), shape(nodes, HID), shape(nodes, HID), shape(nodes, LANE), bf(nodes, HID), shape(nodes, LANE), bf(halo, HID)],
        adj, edge, recv, packed, ft, sel,
        scratch=[pltpu.VMEM((2, feats * FEAT_PAD, HID), BF)],
    )
    halo_one = exchange(send, parts).reshape(halo, HID)
    mean_two, xhat_two, slope_two, istd_two, h_two, send = run(
        second_kernel,
        [bf(nodes, HID), shape(nodes, HID), shape(nodes, HID), shape(nodes, LANE), bf(nodes, HID), bf(halo, HID)],
        adj, edge, halo_one, h_one, wmid, norms, inv_deg, sel,
    )
    halo_two = exchange(send, parts).reshape(halo, HID)
    mean_head, logits, pred, cross, mine, send = run(
        head_kernel,
        [bf(nodes, HID), shape(nodes, LANE), bf(nodes, LANE), shape(halo, LANE), shape(halo, LANE), bf(halo, HID)],
        adj, edge, halo_two, h_two, wout, inv_deg, sel, mask, col_deg,
    )
    recv = exchange(send, parts).reshape(halo, HID)
    grad, grad_sum, send, losses = run(
        functools.partial(logit_grad_kernel, classes=classes, each=each),
        [bf(nodes, LANE), bf(nodes, HID), bf(halo, HID), shape(8, LANE)],
        logits, labels, mask, row_deg, pred, edge, recv, mine, cross, col_deg, sel, wout, inv_deg,
        scratch=[pltpu.VMEM((halo, LANE), BF), pltpu.VMEM((halo, LANE), BF), pltpu.VMEM((nodes, LANE), F32), pltpu.VMEM((nodes, LANE), F32)],
    )
    recv = exchange(send, parts).reshape(halo, HID)
    joined_two, grad_sum, send, norm_sums = run(
        functools.partial(second_back_kernel, each=each),
        [bf(nodes, HID), bf(nodes, HID), bf(parts, each + 32, HID), shape(8, HID)],
        adj, grad_sum, grad, wout, recv, sel, slope_two, xhat_two, istd_two, norms, wmid, inv_deg, edge,
        h_two, mean_head, h_one, mean_two, at, smem_in=(17,),
        scratch=[pltpu.VMEM((nodes, HID), F32), pltpu.VMEM((2, HID, HID), F32), pltpu.VMEM((HID, HID), F32)],
    )
    recv = exchange(send, parts)
    send, = run(
        functools.partial(first_back_kernel, each=each), [bf(parts, MESSAGE_ROWS, HID)],
        adj, grad_sum, joined_two, wmid, recv, sel, slope_one, xhat_one, istd_one, norms, ft, mean_one, losses, norm_sums, at,
        smem_in=(14,),
        scratch=[pltpu.VMEM((nodes, HID), BF), pltpu.VMEM((nodes, HID), F32), pltpu.VMEM((2, feats * FEAT_PAD, HID), F32),
                 pltpu.VMEM((halo, HID), BF)],
    )
    recv = exchange(send, parts)
    grads, gmid, gout, square = run(
        functools.partial(total_kernel, width=width),
        [shape(CHUNK_ROW, HID), shape(2 * share, HID), shape(share, HID), shape(8, LANE)], recv,
    )
    squares = [square]
    for k in range(1, feats):
        squares.append(lax.ppermute(square, "feat", [(s, s ^ k) for s in range(feats)]))
    outs = [shape(1, 1)] * 3 + [shape(*p.shape) for p in params] * 3 + [bf(*p.shape) for p in params[:3]]
    result = run(update_kernel, outs, grads, gmid, gout, *squares, losses, *params, *firsts, *seconds, at, smem_in=(20,))
    return (
        tuple(r.reshape(()) for r in result[:3])
        + restore(*result[3:7]) + restore(*result[7:11]) + restore(*result[11:15]) + restore(*result[15:])
    )


def solution(mesh):
    weight = P(None, "feat", None)
    norm = P(None, None, "feat")
    placed = (
        P("dom", "feat"), P("dom", None), P("dom", None), P("dom", None), P("dom", None, None), P("dom"), P("dom"),
    ) + (weight, weight, weight, norm) * 3
    return jax.shard_map(
        functools.partial(shards, parts=mesh.shape["dom"], feats=mesh.shape["feat"]),
        mesh=mesh,
        in_specs=placed,
        out_specs=(P(), P(), P()) + (weight, weight, weight, norm) * 3 + (weight,) * 3,
        check_vma=False,
    )
```

```python
import functools

import jax
import jax.numpy as jnp
from jax import lax
from jax.experimental import pallas as pl
from jax.experimental.pallas import tpu as pltpu
from jax.sharding import PartitionSpec as P

HID = 256
STEP = 5

NORM_EPS = 1e-05
PEN_WEIGHT = 0.001
CLIP_LEVEL = 0.01
RATE = 0.05
BETA_ONE = 0.5
BETA_TWO = 0.5
ADAM_EPS = 1e-08
DECAY = 0.01

BF = jnp.bfloat16
F32 = jnp.float32
LANE = 128
FEAT_PAD = 32
MIB = 1 << 20
CONVERT_TILE = 256

VMEM = pl.BlockSpec(memory_space=pltpu.VMEM)
SMEM = pl.BlockSpec(memory_space=pltpu.SMEM)
ANY = pl.BlockSpec(memory_space=pl.ANY)
HBM = pl.BlockSpec(memory_space=pltpu.HBM)


def dot_nn(a, b):
    return jnp.dot(a, b, preferred_element_type=F32)


def dot_tn(a, b):
    return lax.dot_general(a, b, (((0,), (0,)), ((), ())), preferred_element_type=F32)


def dot_nt(a, b):
    return lax.dot_general(a, b, (((1,), (1,)), ((), ())), preferred_element_type=F32)


def iota(shape, axis):
    return lax.broadcasted_iota(jnp.int32, shape, axis)


def place(rows, cols, shift, turned=False):
    dims = (cols, rows) if turned else (rows, cols)
    return (iota(dims, int(turned)) + shift == iota(dims, int(not turned))).astype(F32).astype(BF)


def widen(x):
    return x.astype(F32)


def bf_parts(x, count):
    parts = []
    for _ in range(count):
        part = x.astype(BF)
        parts.append(part)
        x = x - widen(part)
    return parts


def both(x):
    return jnp.concatenate([x, x], 1)


def rows_of(i, tile):
    return pl.ds(pl.multiple_of(i * tile, tile), tile)


def call(kernel, outs, *args, mib=24, flops=0, smem_in=(), any_in=(), hbm_in=(), smem_out=(), scratch=()):
    size = sum(a.size * a.dtype.itemsize for a in (*args, *outs))
    return pl.pallas_call(
        kernel,
        out_shape=outs,
        in_specs=[SMEM if i in smem_in else ANY if i in any_in else HBM if i in hbm_in else VMEM for i in range(len(args))],
        out_specs=[SMEM if i in smem_out else VMEM for i in range(len(outs))],
        scratch_shapes=list(scratch),
        cost_estimate=pl.CostEstimate(flops=flops, bytes_accessed=size // 4, transcendentals=0),
        compiler_params=pltpu.CompilerParams(vmem_limit_bytes=mib * MIB),
    )(*args)


def shape(*dims, dtype=F32):
    return jax.ShapeDtypeStruct(dims, dtype)


def pack_kernel(feat_hbm, w_in_hbm, w_mid_hbm, w_out_hbm, norm_hbm, at_ref, pack_ref, at_out,
                feat_ref, w_in_ref, w_mid_ref, w_out_ref, norm_ref, sems):
    sources = (feat_hbm, w_mid_hbm, w_in_hbm, w_out_hbm, norm_hbm)
    targets = (feat_ref, w_mid_ref, w_in_ref, w_out_ref, norm_ref)
    copies = [pltpu.make_async_copy(src, dst, sems.at[i]) for i, (src, dst) in enumerate(zip(sources, targets))]
    for copy in copies:
        copy.start()
    at_out[0] = at_ref[0]
    for copy in copies:
        copy.wait()
    nodes = feat_ref.shape[1]
    width, share = feat_ref.shape[0], w_mid_ref.shape[1]
    classes = w_out_ref.shape[0]
    rows = dot_nn(place(FEAT_PAD, width, 0), feat_ref[...].astype(BF))
    ones = iota((FEAT_PAD, nodes), 0) == FEAT_PAD - 1
    blocks = [jnp.zeros((FEAT_PAD, HID), F32) for _ in range(3)]
    for layer in range(2):
        for p, part in enumerate(bf_parts(norm_ref[layer], 3)):
            part = dot_nn(part, place(share, HID, 0)).astype(BF)
            blocks[p] = blocks[p] + dot_nn(place(2, FEAT_PAD, NORM_AT + 2 * layer, turned=True), part)
    blocks.append(jnp.zeros((FEAT_PAD, nodes - 3 * HID), F32))
    rows = (jnp.where(ones, 1.0, rows) + jnp.concatenate(blocks, 1)).astype(BF)
    at = 0
    for b in range(nodes // HID):
        pack_ref[at : at + FEAT_PAD, :] = rows[:, b * HID : (b + 1) * HID]
        at += FEAT_PAD
    for k in range(2):
        pack_ref[at : at + share, :] = w_mid_ref[k].astype(BF)
        at += share
    for k in range(2):
        pack_ref[at : at + FEAT_PAD, :] = dot_nn(place(FEAT_PAD, width, 0), w_in_ref[:, k, :].astype(BF)).astype(BF)
        at += FEAT_PAD
    turned = jnp.zeros((2 * CLASS_HALF, LANE), F32)
    for k in range(2):
        grown = dot_nn(place(classes, 2 * CLASS_HALF, 0, turned=True), w_out_ref[:, k, :].astype(BF)).astype(BF)
        turned = turned + dot_nn(grown, place(share, LANE, k * share))
    turned = turned.astype(BF)
    for half in range(2):
        pack_ref[at : at + CLASS_HALF, half * LANE : (half + 1) * LANE] = turned[half * CLASS_HALF : (half + 1) * CLASS_HALF, :]


NORM_AT = FEAT_PAD - 6
CLASS_HALF = 32


def pack_rows(nodes, share):
    return nodes // HID * FEAT_PAD + 2 * share + 2 * FEAT_PAD + CLASS_HALF


def convert_kernel(adj_hbm, bound_hbm, keep_hbm, idx_hbm, adj_ref, edge_ref, row_ref, col_ref, sel_ref,
                   adj_buf, bound_buf, keep_ref, idx_ref, sems, small_sems):
    slots, nodes = sel_ref.shape
    parts, each = idx_ref.shape[1:]
    steps = nodes // CONVERT_TILE

    def fetch(step, slot):
        s = rows_of(step, CONVERT_TILE)
        return (pltpu.make_async_copy(adj_hbm.at[s], adj_buf.at[slot], sems.at[0, slot]),
                pltpu.make_async_copy(bound_hbm.at[s], bound_buf.at[slot], sems.at[1, slot]))

    small = (pltpu.make_async_copy(idx_hbm, idx_ref, small_sems.at[0]), pltpu.make_async_copy(keep_hbm, keep_ref, small_sems.at[1]))
    for copy in small:
        copy.start()
    for step in range(CONVERT_SLOTS):
        for copy in fetch(step, step):
            copy.start()
    for copy in small:
        copy.wait()
    eye = iota((each, each), 0) == iota((each, each), 1)
    for p in range(parts):
        column = jnp.sum(jnp.where(eye, idx_ref[0, p : p + 1, :].astype(F32), 0.0), 1, keepdims=True)
        hot = iota((each, nodes), 1) == column.astype(jnp.int32)
        sel_ref[p * each : (p + 1) * each, :] = hot.astype(F32).astype(BF)

    def body(step, _):
        slot = lax.rem(step, CONVERT_SLOTS)
        s = rows_of(step, CONVERT_TILE)
        for copy in fetch(step, slot):
            copy.wait()
        adj_ref[s, :] = adj_buf[slot].astype(F32).astype(BF)
        edge = (bound_buf[slot] * keep_ref[...]).astype(F32).astype(BF)
        edge_ref[s, :] = edge
        row_ref[s, :] = dot_nn(edge, jnp.ones((slots, LANE), BF))
        col_ref[...] += dot_tn(edge, jnp.ones((CONVERT_TILE, LANE), BF))

        @pl.when(step + CONVERT_SLOTS < steps)
        def _():
            for copy in fetch(step + CONVERT_SLOTS, slot):
                copy.start()

        return 0

    col_ref[...] = jnp.zeros(col_ref.shape, F32)
    lax.fori_loop(0, steps, body, 0)


CONVERT_SLOTS = 4


def spread_kernel(own_ref, core_ref, chip_ref, far_ref, sel_ref, after_ref, at_ref, ft_ref, send_ref):
    del after_ref
    row = iota((FEAT_PAD, HID), 0)
    keep = (row < NORM_AT) | (row == FEAT_PAD - 1)
    for k, packed_ref in enumerate((own_ref, core_ref, chip_ref, far_ref)):
        at = rows_of(at_ref[0] ^ k, FEAT_PAD)
        for b in range(ft_ref.shape[1] // HID):
            rows = widen(packed_ref[b * FEAT_PAD : (b + 1) * FEAT_PAD, :])
            ft_ref[at, b * HID : (b + 1) * HID] = jnp.where(keep, rows, 0.0).astype(BF)
    send_ref[...] = dot_nt(sel_ref[...], ft_ref[...]).astype(BF)


def unpack(packed_refs, at_ref, win_ref, wmid_ref, wout_ref, norm_ref):
    share = HID // len(packed_refs)
    norms = jnp.zeros((8, HID), F32)
    heads = [jnp.zeros((2 * CLASS_HALF, HID), F32) for _ in range(2)]
    for offset, packed_ref in enumerate(packed_refs):
        f = at_ref[0] ^ offset
        at = packed_ref.shape[0] - 2 * share - 2 * FEAT_PAD - CLASS_HALF
        for k in range(2):
            wmid_ref[k, rows_of(f, share), :] = packed_ref[at : at + share, :]
            at += share
        for k in range(2):
            win_ref[k, rows_of(f, FEAT_PAD), :] = packed_ref[at : at + FEAT_PAD, :]
            at += FEAT_PAD
        halves = [widen(packed_ref[at : at + CLASS_HALF, h * LANE : (h + 1) * LANE]) for h in range(2)]
        head = both(jnp.concatenate(halves, 0))
        lane = iota(head.shape, 1)
        heads[0] = heads[0] + pltpu.roll(jnp.where(lane < share, head, 0.0), f * share, 1)
        heads[1] = heads[1] + pltpu.roll(jnp.where((lane >= LANE + share) & (lane < LANE + 2 * share), head, 0.0),
                                         (f * share + LANE - share) & (HID - 1), 1)
        part = jnp.zeros((8, HID), F32)
        for p in range(3):
            part = part + widen(packed_ref[p * FEAT_PAD + 16 : (p + 1) * FEAT_PAD, :])[8:16, :]
        part = jnp.where((iota((8, HID), 0) >= NORM_AT - 24) & (iota((8, HID), 0) < NORM_AT - 20), part, 0.0)
        norms = norms + pltpu.roll(part, f * share, 1)
    for k in range(2):
        wout_ref[k, 0 : 2 * CLASS_HALF, :] = heads[k].astype(BF)
        wout_ref[k, 2 * CLASS_HALF :, :] = jnp.zeros((LANE - 2 * CLASS_HALF, HID), BF)
    norm_ref[...] = pltpu.roll(norms, 8 - (NORM_AT - 24), 0)


TILE = 1024


def loop(count, tile, body, carry=0):
    return lax.fori_loop(0, count // tile, lambda i, c: body(rows_of(i, tile), c), carry)


def norm_forward(joined, norm_ref, layer):
    center = jnp.sum(joined, 1, keepdims=True) * (1.0 / HID)
    spread = jnp.sum(joined * joined, 1, keepdims=True) * (1.0 / HID) - center * center
    inv_std = lax.rsqrt(spread + NORM_EPS)
    x_hat = (joined - center) * inv_std
    normed = x_hat * norm_ref[2 * layer : 2 * layer + 1, :] + norm_ref[2 * layer + 1 : 2 * layer + 2, :]
    gate = 0.5 * jnp.tanh(0.5 * normed) + 0.5
    return inv_std, x_hat, normed * gate, gate * (1.0 + normed * (1.0 - gate))


def keep_norm(s, parts, xhat_ref, slope_ref, istd_ref, h_ref):
    inv_std, x_hat, hidden, slope = parts
    xhat_ref[s, :] = x_hat
    slope_ref[s, :] = slope
    istd_ref[s, :] = jnp.broadcast_to(inv_std, (x_hat.shape[0], LANE))
    h_ref[s, :] = hidden.astype(BF)


def first_kernel(adj_ref, edge_ref, recv_ref, own_ref, core_ref, chip_ref, far_ref, ft_ref, sel_ref, at_ref,
                 wmid_ref, wout_ref, norm_ref,
                 mean_ref, xhat_ref, slope_ref, istd_ref, h_ref, invd_ref, send_ref, win_ref):
    nodes = edge_ref.shape[0]
    unpack((own_ref, core_ref, chip_ref, far_ref), at_ref, win_ref, wmid_ref, wout_ref, norm_ref)

    def gather(s, _):
        summed = dot_nt(adj_ref[s, :], ft_ref[...]) + dot_nn(edge_ref[s, :], recv_ref[...])
        inv_deg = 1.0 / jnp.maximum(summed[:, LANE - 1 : LANE], 1.0)
        invd_ref[s, :] = jnp.broadcast_to(inv_deg, summed.shape)
        mean_ref[s, :] = (summed * inv_deg).astype(BF)
        return 0

    loop(nodes, TILE, gather)

    def apply(s, _):
        joined = dot_tn(ft_ref[:, s], win_ref[0]) + dot_nn(mean_ref[s, :], win_ref[1])
        keep_norm(s, norm_forward(joined, norm_ref, 0), xhat_ref, slope_ref, istd_ref, h_ref)
        return 0

    loop(nodes, TILE, apply)
    send_ref[...] = dot_nn(sel_ref[...], h_ref[...]).astype(BF)


def gather_mean(adj_ref, hin_ref, edge_ref, halo_ref, invd_ref, mean_ref):
    def gather(s, _):
        summed = dot_nn(adj_ref[s, :], hin_ref[...]) + dot_nn(edge_ref[s, :], halo_ref[...])
        mean_ref[s, :] = (summed * both(invd_ref[s, :])).astype(BF)
        return 0

    loop(adj_ref.shape[0], TILE, gather)


def second_kernel(adj_ref, edge_ref, halo_ref, hin_ref, w_ref, norm_ref, invd_ref, sel_ref,
                  mean_ref, xhat_ref, slope_ref, istd_ref, h_ref, send_ref):
    gather_mean(adj_ref, hin_ref, edge_ref, halo_ref, invd_ref, mean_ref)

    def apply(s, _):
        joined = dot_nn(hin_ref[s, :], w_ref[0]) + dot_nn(mean_ref[s, :], w_ref[1])
        keep_norm(s, norm_forward(joined, norm_ref, 1), xhat_ref, slope_ref, istd_ref, h_ref)
        return 0

    loop(adj_ref.shape[0], TILE, apply)
    send_ref[...] = dot_nn(sel_ref[...], h_ref[...]).astype(BF)


def split_count(x):
    high = jnp.floor(x * (1.0 / 256.0))
    return high, x - 256.0 * high


def head_kernel(adj_ref, edge_ref, halo_ref, hin_ref, w_ref, invd_ref, sel_ref, mask_ref, col_ref,
                mean_ref, logit_ref, pred_ref, cross_ref, mine_ref, send_ref):
    gather_mean(adj_ref, hin_ref, edge_ref, halo_ref, invd_ref, mean_ref)

    def apply(s, _):
        logits = dot_nt(hin_ref[s, :], w_ref[0]) + dot_nt(mean_ref[s, :], w_ref[1])
        logit_ref[s, :] = logits
        pred_ref[s, :] = logits.astype(BF)
        return 0

    loop(adj_ref.shape[0], TILE, apply)
    mine = dot_nn(sel_ref[...], pred_ref[...])
    mine_ref[...] = mine
    cross = dot_tn(edge_ref[...], pred_ref[...])
    cross_ref[...] = cross
    high, low = bf_parts(cross, 2)
    count = jnp.sum(mask_ref[...].astype(F32), keepdims=True)
    lane = iota(mine.shape, 1)
    count_high, count_low = split_count(count)
    col_high, col_low = split_count(col_ref[...])
    extra = jnp.where(lane == 64, count_high, 0.0) + jnp.where(lane == 65, count_low, 0.0)
    extra = extra + jnp.where(lane == 66, col_high, 0.0) + jnp.where(lane == 67, col_low, 0.0)
    send_ref[:, 0:LANE] = (mine + pltpu.roll(widen(low), 64, 1)).astype(BF)
    send_ref[:, LANE:] = (widen(high) + extra).astype(BF)


def spread_row(values, row):
    pick = (iota(values.shape, 0) == row).astype(F32).astype(BF)
    return dot_tn(values.astype(F32).astype(BF), pick)


def logit_grad_kernel(logit_ref, label_ref, mask_ref, row_ref, pred_ref, edge_ref, recv_ref, mine_ref, cross_ref, col_ref,
                      sel_ref, w_ref, invd_ref,
                      grad_ref, gs_ref, send_ref, loss_ref, hp_ref, ret_ref, lab_ref, wgt_ref, *, classes, each):
    slots = mine_ref.shape[0]
    nodes = logit_ref.shape[0]
    first, second = widen(recv_ref[:, 0:LANE]), widen(recv_ref[:, LANE:])
    lane = iota((slots, LANE), 1)
    low_half = lane < 64
    halo_pred = jnp.where(low_half, first, 0.0)
    back_cross = jnp.where(low_half, second + pltpu.roll(first, 64, 1), 0.0)
    count = 256.0 * jnp.sum(jnp.where(lane == 64, second, 0.0), keepdims=True)
    count = (count + jnp.sum(jnp.where(lane == 65, second, 0.0), keepdims=True)) * (1.0 / each)
    col_back = 256.0 * second[:, 66:67] + second[:, 67:68]
    scale = 2.0 * PEN_WEIGHT / count
    inv_count = 1.0 / count
    hp_ref[...] = halo_pred.astype(BF)
    ret_ref[...] = (scale * (col_back * mine_ref[...] - back_cross)).astype(BF)
    pen = jnp.sum(col_ref[...] * (halo_pred * halo_pred), keepdims=True)
    pen = pen - 2.0 * jnp.sum(halo_pred * cross_ref[...], keepdims=True)
    for r in range(nodes // LANE):
        lab_ref[r * LANE : (r + 1) * LANE, :] = spread_row(label_ref[...], r)
        wgt_ref[r * LANE : (r + 1) * LANE, :] = spread_row(mask_ref[...], r)

    def body(s, carry):
        ce_sum, pen_sum = carry
        logits = logit_ref[s, :]
        lane = iota(logits.shape, 1)
        real = lane < classes
        top = jnp.max(jnp.where(real, logits, -jnp.inf), 1, keepdims=True)
        shifted = jnp.where(real, jnp.exp(jnp.where(real, logits - top, 0.0)), 0.0)
        total = jnp.sum(shifted, 1, keepdims=True)
        hot = (lane.astype(F32) == lab_ref[s, :]).astype(F32)
        target = jnp.sum(logits * hot, 1, keepdims=True)
        weight = wgt_ref[s, :]
        ce_sum = ce_sum + jnp.sum(weight[:, 0:1] * (top + jnp.log(total) - target), keepdims=True)
        pred = widen(pred_ref[s, :])
        drawn = row_ref[s, :] * pred
        pen_sum = pen_sum + jnp.sum(drawn * pred, keepdims=True)
        own = drawn - dot_nn(edge_ref[s, :], hp_ref[...])
        back = dot_tn(sel_ref[:, s], ret_ref[...])
        grad = ((inv_count * weight) * (shifted * (1.0 / total) - hot) + scale * own + back).astype(BF)
        grad_ref[s, :] = grad
        gs_ref[s, :] = (dot_nn(grad, w_ref[1]) * both(invd_ref[s, :])).astype(BF)
        return ce_sum, pen_sum

    zero = jnp.zeros((1, 1), F32)
    ce_sum, pen_sum = loop(nodes, TILE, body, (zero, zero))
    row = iota((8, LANE), 0)
    loss_ref[...] = (jnp.where(row == 0, ce_sum, 0.0) + jnp.where(row == 1, pen + pen_sum, 0.0)
                     + jnp.where(row == 2, count, 0.0))
    send_ref[...] = dot_tn(edge_ref[...], gs_ref[...]).astype(BF)


BACK_TILE = 1024


def layer_back(adj_ref, gs_ref, grad_ref, w_ref, sel_ref, halo_ref, slope_ref, xhat_ref, istd_ref, norm_ref, layer, own_ref, gj_ref, back):
    nodes = adj_ref.shape[0]

    def pull(s, _):
        own_ref[s, :] = (dot_tn(adj_ref[:, s], gs_ref[...]) + back(grad_ref[s, :], w_ref[0])
                         + dot_tn(sel_ref[:, s], halo_ref[...]))
        return 0

    loop(nodes, BACK_TILE, pull)

    def body(s, carry):
        gain_sum, bias_sum = carry
        grad_pre = own_ref[s, :] * slope_ref[s, :]
        x_hat = xhat_ref[s, :]
        grad_x = grad_pre * norm_ref[2 * layer : 2 * layer + 1, :]
        mean_one = jnp.sum(grad_x, 1, keepdims=True) * (1.0 / HID)
        mean_two = jnp.sum(grad_x * x_hat, 1, keepdims=True) * (1.0 / HID)
        gj_ref[s, :] = (both(istd_ref[s, :]) * (grad_x - mean_one - x_hat * mean_two)).astype(BF)
        gain_sum = gain_sum + jnp.sum(grad_pre * x_hat, 0, keepdims=True)
        bias_sum = bias_sum + jnp.sum(grad_pre, 0, keepdims=True)
        return gain_sum, bias_sum

    zero = jnp.zeros((1, HID), F32)
    return loop(nodes, TILE, body, (zero, zero))


def second_back_kernel(adj_ref, gsin_ref, grad_ref, wout_ref, recv_ref, sel_ref, slope_ref, xhat_ref, istd_ref, norm_ref, w_ref,
                       invd_ref, edge_ref, h_two_ref, mean_head_ref, h_one_ref, mean_two_ref, at_ref,
                       gj_ref, gs_ref, send_ref, sums_ref, own_ref, full_ref, head_ref, *, each):
    gain_sum, bias_sum = layer_back(
        adj_ref, gsin_ref, grad_ref, wout_ref, sel_ref, recv_ref, slope_ref, xhat_ref, istd_ref, norm_ref, 1, own_ref, gj_ref, dot_nn
    )
    row = iota((8, HID), 0)
    sums_ref[...] = jnp.where(row == 2, gain_sum, 0.0) + jnp.where(row == 3, bias_sum, 0.0)

    def body(s, _):
        gs_ref[s, :] = (dot_nt(gj_ref[s, :], w_ref[1]) * both(invd_ref[s, :])).astype(BF)
        return 0

    loop(adj_ref.shape[0], TILE, body)
    parts = send_ref.shape[0]
    send_ref[:, 0:each, :] = dot_tn(edge_ref[...], gs_ref[...]).astype(BF).reshape(parts, each, HID)
    share = HID // FEATS
    half = pl.ds(pl.multiple_of(at_ref[0] * share // LANE * LANE, LANE), LANE)
    start = at_ref[0] * share % LANE
    head_ref[:, 0:LANE] = dot_tn(h_two_ref[:, half], grad_ref[...])
    head_ref[:, LANE:] = dot_tn(mean_head_ref[:, half], grad_ref[...])
    full_ref[0] = dot_tn(h_one_ref[:, half], gj_ref[...])
    full_ref[1] = dot_tn(mean_two_ref[:, half], gj_ref[...])
    for q in range(parts):
        if q * 16 < 2 * share:
            k, r = divmod(q * 16, share)
            send_ref[q, each : each + 16, :] = full_ref[k, pl.ds(pl.multiple_of(start + r, 16), 16), :].astype(BF)
            rows = head_ref[pl.ds(pl.multiple_of(start + q * 8, 8), 8), :]
            high, low = bf_parts(rows, 2)
            send_ref[q, each + 16 : each + 32, :] = jnp.concatenate([widen(high), widen(low)], 0).astype(BF)
        else:
            send_ref[q, each : each + 32, :] = jnp.zeros((32, HID), BF)


FEATS = 4


def first_back_kernel(adj_ref, gsin_ref, grad_ref, w_ref, recv_ref, sel_ref, slope_ref, xhat_ref, istd_ref, norm_ref,
                      ft_ref, mean_ref, loss_ref, sums_ref, at_ref,
                      send_ref, gj_ref, own_ref, full_ref, halo_ref, *, each):
    parts = recv_ref.shape[0]
    halo_ref[...] = recv_ref[:, 0:each, :].reshape(halo_ref.shape)
    gain_sum, bias_sum = layer_back(
        adj_ref, gsin_ref, grad_ref, w_ref, sel_ref, halo_ref, slope_ref, xhat_ref, istd_ref, norm_ref, 0, own_ref, gj_ref, dot_nt
    )
    row = iota((8, HID), 0)
    sums = sums_ref[...] + jnp.where(row == 0, gain_sum, 0.0) + jnp.where(row == 1, bias_sum, 0.0)
    full_ref[0] = dot_nn(ft_ref[...], gj_ref[...])
    full_ref[1] = dot_tn(mean_ref[...], gj_ref[...])
    at = rows_of(at_ref[0], FEAT_PAD)
    mid = jnp.zeros((16, HID), F32)
    out = jnp.zeros((16, HID), F32)
    for q in range(parts):
        mid = mid + widen(recv_ref[q, each : each + 16, :])
        out = out + widen(recv_ref[q, each + 16 : each + 32, :])
    out = out + pltpu.roll(out, 8, 0)
    mid_high, mid_low = bf_parts(mid, 2)
    out_high, out_low = bf_parts(out, 2)
    out = jnp.where(iota((16, HID), 0) < 8, widen(out_high), widen(out_low))
    lane = iota((8, HID), 1)
    blocks = []
    for k, norm_part in enumerate(bf_parts(sums, 2)):
        tail = jnp.zeros((8, HID), F32)
        for p, part in enumerate(bf_parts(jnp.broadcast_to(loss_ref[k : k + 1, 0:1], (8, HID)), 3)):
            tail = tail + jnp.where(lane == p, widen(part), 0.0)
        rows = full_ref[k, at, :]
        last = jnp.where(row == 0, rows[FEAT_PAD - 8 :, :], jnp.where(row == 3, tail, 0.0))
        blocks += [rows[0 : FEAT_PAD - 8, :], jnp.where(row >= 4, pltpu.roll(widen(norm_part), 4, 0), last)]
    message = jnp.concatenate([*blocks, widen(mid_high), widen(mid_low), out], 0).astype(BF)
    for q in range(parts):
        send_ref[q] = message


CHUNK_ROW = 2 * FEAT_PAD
MESSAGE_ROWS = CHUNK_ROW + 48


def total_kernel(recv_ref, grads_ref, norm_ref, loss_ref, mid_ref, out_ref, square_ref, *, width):
    parts = recv_ref.shape[0]
    grads = jnp.zeros((CHUNK_ROW, HID), F32)
    for q in range(parts):
        grads = grads + widen(recv_ref[q, 0:CHUNK_ROW, :])
    grads_ref[...] = grads
    tails = [grads[FEAT_PAD - 8 : FEAT_PAD, :], grads[2 * FEAT_PAD - 8 :, :]]
    row = iota((8, HID), 0)
    norms = jnp.where(row < 4, pltpu.roll(tails[0] + tails[1], 4, 0), 0.0)
    norm_ref[...] = norms
    sums = [jnp.sum(tail[3:4, :], keepdims=True) for tail in tails]
    loss_ref[...] = jnp.broadcast_to(sums[0] + PEN_WEIGHT * sums[1], loss_ref.shape)
    for q in range(mid_ref.shape[0] // 16):
        at = CHUNK_ROW
        mid_ref[q * 16 : q * 16 + 16, :] = widen(recv_ref[q, at : at + 16, :]) + widen(recv_ref[q, at + 16 : at + 32, :])
        rows = widen(recv_ref[q, at + 32 : at + 48, :])
        out_ref[q * 8 : q * 8 + 8, :] = rows[0:8, :] + rows[8:16, :]
    weight_row = (iota((CHUNK_ROW, HID), 0) & (FEAT_PAD - 1)) < width
    first = jnp.where(weight_row, grads, 0.0)
    square = jnp.sum(first * first, keepdims=True)
    square = square + jnp.sum(mid_ref[...] * mid_ref[...], keepdims=True)
    square = square + jnp.sum(out_ref[...] * out_ref[...], keepdims=True)
    row = iota((8, LANE), 0)
    square_ref[...] = jnp.where(row == 1, jnp.sum(norms * norms, keepdims=True), square)


def adam(param, grad, first, second):
    first_new = BETA_ONE * first + (1.0 - BETA_ONE) * grad
    second_new = BETA_TWO * second + (1.0 - BETA_TWO) * grad * grad
    first_hat = first_new / (1.0 - BETA_ONE**STEP)
    second_hat = second_new / (1.0 - BETA_TWO**STEP)
    fresh = param - RATE * (first_hat / (jnp.sqrt(second_hat) + ADAM_EPS) + DECAY * param)
    return fresh, first_new, second_new


def update_kernel(grads_ref, gnorm_ref, total_ref, gmid_ref, gout_ref, sq0_ref, sq1_ref, sq2_ref, sq3_ref, loss_ref,
                  w_in, w_mid, w_out, norm, m_in, m_mid, m_out, m_norm, v_in, v_mid, v_out, v_norm, at_ref,
                  loss_out, count_out, gnorm_out,
                  nw_in, nw_mid, nw_out, nnorm, nm_in, nm_mid, nm_out, nm_norm, nv_in, nv_mid, nv_out, nv_norm,
                  c_in, c_mid, c_out):
    loss_out[...] = total_ref[0:1, 0:1]
    count_out[...] = loss_ref[2:3, 0:1]
    square = (sq0_ref[0:1, 0:1] + sq1_ref[0:1, 0:1]) + (sq2_ref[0:1, 0:1] + sq3_ref[0:1, 0:1])
    grad_norm = jnp.sqrt(square + sq0_ref[1:2, 0:1])
    gnorm_out[...] = grad_norm
    factor = jnp.minimum(1.0, CLIP_LEVEL / (grad_norm + 1e-06))

    def step(index, grad, w, m, v, nw, nm, nv, copy):
        fresh, first, second = adam(w[index], grad * factor, m[index], v[index])
        nw[index], nm[index], nv[index] = fresh, first, second
        if copy is not None:
            copy[index] = fresh.astype(BF)

    every = slice(None)
    width, _, share = w_in.shape[0], 2, w_mid.shape[1]
    classes = w_out.shape[0]
    for k in range(2):
        step((every, k, every), grads_ref[k * FEAT_PAD : k * FEAT_PAD + width, :], w_in, m_in, v_in, nw_in, nm_in, nv_in, c_in)
        step(k, gmid_ref[k * share : (k + 1) * share, :], w_mid, m_mid, v_mid, nw_mid, nm_mid, nv_mid, c_mid)
        turned = jnp.transpose(gout_ref[:, k * LANE : (k + 1) * LANE])[0:classes, :]
        step((every, k, every), turned, w_out, m_out, v_out, nw_out, nm_out, nv_out, c_out)
    whole = gnorm_ref[...]
    mine = jnp.zeros((8, share), F32)
    for f in range(HID // share):
        mine = mine + jnp.where(at_ref[0] == f, whole[:, f * share : (f + 1) * share], 0.0)
    for layer in range(2):
        step(layer, mine[2 * layer : 2 * layer + 2, :], norm, m_norm, v_norm, nnorm, nm_norm, nv_norm, None)


def exchange(x, parts):
    return lax.all_to_all(x.reshape(parts, -1, x.shape[-1]), "dom", split_axis=0, concat_axis=0, tiled=True)


def native(w_in, w_mid, w_out, norm):
    return (jnp.transpose(w_in, (1, 0, 2)), w_mid, jnp.transpose(w_out, (2, 0, 1)), norm)


def restore(w_in, w_mid, w_out, *norm):
    return (jnp.transpose(w_in, (1, 0, 2)), w_mid, jnp.transpose(w_out, (1, 2, 0)), *norm)


def shards(
    features,
    inner_adj,
    bound_adj,
    keep_slots,
    send_index,
    labels,
    train_mask,
    w_in,
    w_mid,
    w_out,
    norm_params,
    m_in,
    m_mid,
    m_out,
    m_norms,
    v_in,
    v_mid,
    v_out,
    v_norms,
    *,
    parts,
    feats,
):
    nodes = features.shape[0]
    each = send_index.shape[2]
    halo = parts * each
    classes = w_out.shape[2]
    share = w_mid.shape[1]
    width = features.shape[1]
    run = functools.partial(call, mib=16 if parts <= 16 else 48)
    labels = labels.reshape(nodes // LANE, LANE)
    mask = train_mask.reshape(nodes // LANE, LANE)
    params = native(w_in, w_mid, w_out, norm_params)
    firsts = native(m_in, m_mid, m_out, m_norms)
    seconds = native(v_in, v_mid, v_out, v_norms)
    feat_at = lax.axis_index("feat").astype(jnp.int32).reshape(1)

    def bf(*dims):
        return shape(*dims, dtype=BF)

    loads = tuple(pltpu.with_memory_space_constraint(a, pltpu.HBM) for a in (features.T, *params))
    own, at = run(
        pack_kernel, [bf(pack_rows(nodes, share), HID), shape(1, dtype=jnp.int32)],
        *loads, feat_at, smem_in=(5,), smem_out=(1,),  hbm_in=range(5),
        scratch=[pltpu.VMEM(a.shape, a.dtype) for a in loads] + [pltpu.SemaphoreType.DMA((5,))],
    )
    chip = lax.ppermute(own, "feat", [(s, s ^ 2) for s in range(feats)])
    core = lax.ppermute(own, "feat", [(s, s ^ 1) for s in range(feats)])
    graph = tuple(pltpu.with_memory_space_constraint(a, pltpu.HBM) for a in (inner_adj, bound_adj, keep_slots, send_index))
    adj, edge, row_deg, col_deg, sel = run(
        convert_kernel, [bf(nodes, nodes), bf(nodes, halo), shape(nodes, LANE), shape(halo, LANE), bf(halo, nodes)],
        *graph, hbm_in=range(4), flops=2 * nodes * nodes * HID,
        scratch=[pltpu.VMEM((CONVERT_SLOTS, CONVERT_TILE, nodes), jnp.int32), pltpu.VMEM((CONVERT_SLOTS, CONVERT_TILE, halo), jnp.int32),
                 pltpu.VMEM(keep_slots.shape, jnp.int32), pltpu.VMEM(send_index.shape, jnp.int32),
                 pltpu.SemaphoreType.DMA((2, CONVERT_SLOTS)), pltpu.SemaphoreType.DMA((2,))],
    )
    chip, adj = lax.optimization_barrier((chip, adj))
    far = lax.ppermute(chip, "feat", [(s, s ^ 1) for s in range(feats)])
    packed = (own, core, chip, far)
    ft, send = run(
        spread_kernel, [bf(feats * FEAT_PAD, nodes), bf(halo, LANE)], *packed, sel, adj, at, any_in=(5,), smem_in=(6,)
    )
    recv = exchange(send, parts).reshape(halo, LANE)
    (wmid, wout, norms,
     mean_one, xhat_one, slope_one, istd_one, h_one, inv_deg, send) = run(
        first_kernel,
        [bf(2, HID, HID), bf(2, LANE, HID), shape(8, HID),
         bf(nodes, LANE), shape(nodes, HID), shape(nodes, HID), shape(nodes, LANE), bf(nodes, HID), shape(nodes, LANE), bf(halo, HID)],
        adj, edge, recv, *packed, ft, sel, at, smem_in=(9,),
        scratch=[pltpu.VMEM((2, feats * FEAT_PAD, HID), BF)],
    )
    halo_one = exchange(send, parts).reshape(halo, HID)
    mean_two, xhat_two, slope_two, istd_two, h_two, send = run(
        second_kernel,
        [bf(nodes, HID), shape(nodes, HID), shape(nodes, HID), shape(nodes, LANE), bf(nodes, HID), bf(halo, HID)],
        adj, edge, halo_one, h_one, wmid, norms, inv_deg, sel,
    )
    halo_two = exchange(send, parts).reshape(halo, HID)
    mean_head, logits, pred, cross, mine, send = run(
        head_kernel,
        [bf(nodes, HID), shape(nodes, LANE), bf(nodes, LANE), shape(halo, LANE), shape(halo, LANE), bf(halo, HID)],
        adj, edge, halo_two, h_two, wout, inv_deg, sel, mask, col_deg,
    )
    recv = exchange(send, parts).reshape(halo, HID)
    grad, grad_sum, send, losses = run(
        functools.partial(logit_grad_kernel, classes=classes, each=each),
        [bf(nodes, LANE), bf(nodes, HID), bf(halo, HID), shape(8, LANE)],
        logits, labels, mask, row_deg, pred, edge, recv, mine, cross, col_deg, sel, wout, inv_deg,
        scratch=[pltpu.VMEM((halo, LANE), BF), pltpu.VMEM((halo, LANE), BF), pltpu.VMEM((nodes, LANE), F32), pltpu.VMEM((nodes, LANE), F32)],
    )
    recv = exchange(send, parts).reshape(halo, HID)
    joined_two, grad_sum, send, norm_sums = run(
        functools.partial(second_back_kernel, each=each),
        [bf(nodes, HID), bf(nodes, HID), bf(parts, each + 32, HID), shape(8, HID)],
        adj, grad_sum, grad, wout, recv, sel, slope_two, xhat_two, istd_two, norms, wmid, inv_deg, edge,
        h_two, mean_head, h_one, mean_two, at, smem_in=(17,),
        scratch=[pltpu.VMEM((nodes, HID), F32), pltpu.VMEM((2, LANE, HID), F32), pltpu.VMEM((LANE, HID), F32)],
    )
    recv = exchange(send, parts)
    send, = run(
        functools.partial(first_back_kernel, each=each), [bf(parts, MESSAGE_ROWS, HID)],
        adj, grad_sum, joined_two, wmid, recv, sel, slope_one, xhat_one, istd_one, norms, ft, mean_one, losses, norm_sums, at,
        smem_in=(14,),
        scratch=[pltpu.VMEM((nodes, HID), BF), pltpu.VMEM((nodes, HID), F32), pltpu.VMEM((2, feats * FEAT_PAD, HID), F32),
                 pltpu.VMEM((halo, HID), BF)],
    )
    recv = exchange(send, parts)
    *grads, square = run(
        functools.partial(total_kernel, width=width),
        [shape(CHUNK_ROW, HID), shape(8, HID), shape(8, LANE), shape(2 * share, HID), shape(share, HID), shape(8, LANE)], recv,
    )
    squares = [square]
    for k in range(1, feats):
        squares.append(lax.ppermute(square, "feat", [(s, s ^ k) for s in range(feats)]))
    outs = [shape(1, 1)] * 3 + [shape(*p.shape) for p in params] * 3 + [bf(*p.shape) for p in params[:3]]
    result = run(update_kernel, outs, *grads, *squares, losses, *params, *firsts, *seconds, at, smem_in=(22,))
    return (
        tuple(r.reshape(()) for r in result[:3])
        + restore(*result[3:7]) + restore(*result[7:11]) + restore(*result[11:15]) + restore(*result[15:])
    )


def solution(mesh):
    weight = P(None, "feat", None)
    norm = P(None, None, "feat")
    placed = (
        P("dom", "feat"), P("dom", None), P("dom", None), P("dom", None), P("dom", None, None), P("dom"), P("dom"),
    ) + (weight, weight, weight, norm) * 3
    return jax.shard_map(
        functools.partial(shards, parts=mesh.shape["dom"], feats=mesh.shape["feat"]),
        mesh=mesh,
        in_specs=placed,
        out_specs=(P(), P(), P()) + (weight, weight, weight, norm) * 3 + (weight,) * 3,
        check_vma=False,
    )
```

```python
import functools
import math

import jax
import jax.numpy as jnp
from jax import lax
from jax.experimental import pallas as pl
from jax.experimental.pallas import tpu as pltpu
from jax.sharding import PartitionSpec as P

HID = 256
STEP = 5

NORM_EPS = 1e-05
PEN_WEIGHT = 0.001
CLIP_LEVEL = 0.01
RATE = 0.05
BETA_ONE = 0.5
BETA_TWO = 0.5
ADAM_EPS = 1e-08
DECAY = 0.01

BF = jnp.bfloat16
F32 = jnp.float32
LANE = 128
FEAT_PAD = 32
MIB = 1 << 20
CONVERT_TILE = 256

VMEM = pl.BlockSpec(memory_space=pltpu.VMEM)
SMEM = pl.BlockSpec(memory_space=pltpu.SMEM)
ANY = pl.BlockSpec(memory_space=pl.ANY)
HBM = pl.BlockSpec(memory_space=pltpu.HBM)


def dot_nn(a, b):
    return jnp.dot(a, b, preferred_element_type=F32)


def dot_tn(a, b):
    return lax.dot_general(a, b, (((0,), (0,)), ((), ())), preferred_element_type=F32)


def dot_nt(a, b):
    return lax.dot_general(a, b, (((1,), (1,)), ((), ())), preferred_element_type=F32)


def iota(shape, axis):
    return lax.broadcasted_iota(jnp.int32, shape, axis)


def place(rows, cols, shift, turned=False):
    dims = (cols, rows) if turned else (rows, cols)
    return (iota(dims, int(turned)) + shift == iota(dims, int(not turned))).astype(F32).astype(BF)


def widen(x):
    return x.astype(F32)


def bf_parts(x, count):
    parts = []
    for _ in range(count):
        part = x.astype(BF)
        parts.append(part)
        x = x - widen(part)
    return parts


def both(x):
    return jnp.concatenate([x, x], 1)


def rows_of(i, tile):
    return pl.ds(pl.multiple_of(i * tile, tile), tile)


def call(kernel, outs, *args, mib=24, flops=0, smem_in=(), any_in=(), hbm_in=(), smem_out=(), hbm_out=(), scratch=()):
    size = sum(math.prod(a.shape) * a.dtype.itemsize for a in (*args, *outs))
    return pl.pallas_call(
        kernel,
        out_shape=outs,
        in_specs=[SMEM if i in smem_in else ANY if i in any_in else HBM if i in hbm_in else VMEM for i in range(len(args))],
        out_specs=[SMEM if i in smem_out else HBM if i in hbm_out else VMEM for i in range(len(outs))],
        scratch_shapes=list(scratch),
        cost_estimate=pl.CostEstimate(flops=flops, bytes_accessed=size // 4, transcendentals=0),
        compiler_params=pltpu.CompilerParams(vmem_limit_bytes=mib * MIB),
    )(*args)


def shape(*dims, dtype=F32):
    return jax.ShapeDtypeStruct(dims, dtype)


def select(idx_ref, sel_ref):
    nodes = sel_ref.shape[1]
    parts, each = idx_ref.shape[1:]
    eye = iota((each, each), 0) == iota((each, each), 1)
    for p in range(parts):
        column = jnp.sum(jnp.where(eye, idx_ref[0, p : p + 1, :].astype(F32), 0.0), 1, keepdims=True)
        hot = iota((each, nodes), 1) == column.astype(jnp.int32)
        sel_ref[p * each : (p + 1) * each, :] = hot.astype(F32).astype(BF)


def pack_kernel(idx_hbm, feat_hbm, w_in_hbm, w_mid_hbm, w_out_hbm, norm_hbm, at_ref, send_ref, pack_ref, at_out,
                sel_ref, idx_ref, feat_ref, w_in_ref, w_mid_ref, w_out_ref, norm_ref, sems):
    sources = (idx_hbm, feat_hbm, w_mid_hbm, w_in_hbm, w_out_hbm, norm_hbm)
    targets = (idx_ref, feat_ref, w_mid_ref, w_in_ref, w_out_ref, norm_ref)
    copies = [pltpu.make_async_copy(src, dst, sems.at[i]) for i, (src, dst) in enumerate(zip(sources, targets))]
    for copy in copies:
        copy.start()
    at_out[0] = at_ref[0]
    copies[0].wait()
    select(idx_ref, sel_ref)
    wait_all(copies[1:])
    nodes = feat_ref.shape[1]
    width, share = feat_ref.shape[0], w_mid_ref.shape[1]
    classes = w_out_ref.shape[0]
    rows = dot_nn(place(FEAT_PAD, width, 0), feat_ref[...].astype(BF))
    parts, copies, half, _ = send_ref.shape
    sent = dot_nt(sel_ref[...], rows.astype(BF)).astype(BF)
    left = dot_nn(sent, place(FEAT_PAD, LANE, 0)).reshape(parts, 2, half, LANE)[:, 0]
    right = dot_nn(sent, place(FEAT_PAD, LANE, LANE // 2)).reshape(parts, 2, half, LANE)[:, 1]
    for f in range(copies):
        send_ref[:, f] = (left + right).astype(BF)
    ones = iota((FEAT_PAD, nodes), 0) == FEAT_PAD - 1
    blocks = [jnp.zeros((FEAT_PAD, HID), F32) for _ in range(3)]
    for layer in range(2):
        for p, part in enumerate(bf_parts(norm_ref[layer], 3)):
            part = dot_nn(part, place(share, HID, 0)).astype(BF)
            blocks[p] = blocks[p] + dot_nn(place(2, FEAT_PAD, NORM_AT + 2 * layer, turned=True), part)
    blocks.append(jnp.zeros((FEAT_PAD, nodes - 3 * HID), F32))
    rows = (jnp.where(ones, 1.0, rows) + jnp.concatenate(blocks, 1)).astype(BF)
    at = 0
    for b in range(nodes // HID):
        pack_ref[at : at + FEAT_PAD, :] = rows[:, b * HID : (b + 1) * HID]
        at += FEAT_PAD
    for k in range(2):
        pack_ref[at : at + share, :] = w_mid_ref[k].astype(BF)
        at += share
    for k in range(2):
        pack_ref[at : at + FEAT_PAD, :] = dot_nn(place(FEAT_PAD, width, 0), w_in_ref[:, k, :].astype(BF)).astype(BF)
        at += FEAT_PAD
    turned = jnp.zeros((2 * CLASS_HALF, LANE), F32)
    for k in range(2):
        grown = dot_nn(place(classes, 2 * CLASS_HALF, 0, turned=True), w_out_ref[:, k, :].astype(BF)).astype(BF)
        turned = turned + dot_nn(grown, place(share, LANE, k * share))
    turned = turned.astype(BF)
    for half in range(2):
        pack_ref[at : at + CLASS_HALF, half * LANE : (half + 1) * LANE] = turned[half * CLASS_HALF : (half + 1) * CLASS_HALF, :]


NORM_AT = FEAT_PAD - 6
CLASS_HALF = 32


def pack_rows(nodes, share):
    return nodes // HID * FEAT_PAD + 2 * share + 2 * FEAT_PAD + CLASS_HALF


def spread(packed_refs, at_ref, ft_ref):
    row = iota((FEAT_PAD, HID), 0)
    keep = (row < NORM_AT) | (row == FEAT_PAD - 1)
    for k, packed_ref in enumerate(packed_refs):
        at = rows_of(at_ref[0] ^ k, FEAT_PAD)
        for b in range(ft_ref.shape[1] // HID):
            rows = widen(packed_ref[b * FEAT_PAD : (b + 1) * FEAT_PAD, :])
            ft_ref[at, b * HID : (b + 1) * HID] = jnp.where(keep, rows, 0.0).astype(BF)


def join_halo(recv_ref, halo_ref, width):
    parts, feats, half, _ = recv_ref.shape
    lane = iota((parts * half, LANE), 1)
    sides = [jnp.where(lane == LANE - 1, 1.0, 0.0)] * 2
    for f in range(feats):
        rows = widen(recv_ref[:, f]).reshape(parts * half, LANE)
        for g in range(2):
            at = g * (LANE // 2)
            side = jnp.where((lane >= at) & (lane < at + width), rows, 0.0)
            shift = (f * FEAT_PAD - at) % LANE
            sides[g] = sides[g] + (pltpu.roll(side, shift, 1) if shift else side)
    sides = [side.astype(BF).reshape(parts, half, LANE) for side in sides]
    halo_ref[...] = jnp.stack(sides, 1).reshape(halo_ref.shape)


def unpack(packed_refs, at_ref, win_ref, wmid_ref, wout_ref, norm_ref):
    share = HID // len(packed_refs)
    norms = jnp.zeros((8, HID), F32)
    heads = [jnp.zeros((2 * CLASS_HALF, HID), F32) for _ in range(2)]
    for offset, packed_ref in enumerate(packed_refs):
        f = at_ref[0] ^ offset
        at = packed_ref.shape[0] - 2 * share - 2 * FEAT_PAD - CLASS_HALF
        for k in range(2):
            wmid_ref[k, rows_of(f, share), :] = packed_ref[at : at + share, :]
            at += share
        for k in range(2):
            win_ref[k, rows_of(f, FEAT_PAD), :] = packed_ref[at : at + FEAT_PAD, :]
            at += FEAT_PAD
        halves = [widen(packed_ref[at : at + CLASS_HALF, h * LANE : (h + 1) * LANE]) for h in range(2)]
        head = both(jnp.concatenate(halves, 0))
        lane = iota(head.shape, 1)
        heads[0] = heads[0] + pltpu.roll(jnp.where(lane < share, head, 0.0), f * share, 1)
        heads[1] = heads[1] + pltpu.roll(jnp.where((lane >= LANE + share) & (lane < LANE + 2 * share), head, 0.0),
                                         (f * share + LANE - share) & (HID - 1), 1)
        part = jnp.zeros((8, HID), F32)
        for p in range(3):
            part = part + widen(packed_ref[p * FEAT_PAD + 16 : (p + 1) * FEAT_PAD, :])[8:16, :]
        part = jnp.where((iota((8, HID), 0) >= NORM_AT - 24) & (iota((8, HID), 0) < NORM_AT - 20), part, 0.0)
        norms = norms + pltpu.roll(part, f * share, 1)
    for k in range(2):
        wout_ref[k, 0 : 2 * CLASS_HALF, :] = heads[k].astype(BF)
        wout_ref[k, 2 * CLASS_HALF :, :] = jnp.zeros((LANE - 2 * CLASS_HALF, HID), BF)
    norm_ref[...] = pltpu.roll(norms, 8 - (NORM_AT - 24), 0)


TILE = 1024


def loop(count, tile, body, carry=0):
    return lax.fori_loop(0, count // tile, lambda i, c: body(rows_of(i, tile), c), carry)


def norm_forward(joined, norm_ref, layer):
    center = jnp.sum(joined, 1, keepdims=True) * (1.0 / HID)
    spread = jnp.sum(joined * joined, 1, keepdims=True) * (1.0 / HID) - center * center
    inv_std = lax.rsqrt(spread + NORM_EPS)
    x_hat = (joined - center) * inv_std
    normed = x_hat * norm_ref[2 * layer : 2 * layer + 1, :] + norm_ref[2 * layer + 1 : 2 * layer + 2, :]
    gate = 0.5 * jnp.tanh(0.5 * normed) + 0.5
    return inv_std, x_hat, normed * gate, gate * (1.0 + normed * (1.0 - gate))


def keep_norm(s, parts, xhat_ref, slope_ref, istd_ref, h_ref):
    inv_std, x_hat, hidden, slope = parts
    xhat_ref[s, :] = x_hat
    slope_ref[s, :] = slope
    istd_ref[s, :] = jnp.broadcast_to(inv_std, (x_hat.shape[0], LANE))
    h_ref[s, :] = hidden.astype(BF)


GATHER_PARTS = 2


def start_all(copies):
    for copy in copies:
        copy.start()
    return copies


def wait_all(copies):
    for copy in copies:
        copy.wait()


def side_kernel(own_hbm, chip_hbm, core_ref, far_ref, at_ref,
                ft_out, win_out, wmid_out, wout_out, norm_out,
                ft_ref, win_ref, wmid_ref, wout_ref, norm_ref, own_ref, chip_ref, in_sems, out_sems):
    packed_refs = (own_ref, core_ref, chip_ref, far_ref)
    loads = ((own_hbm, own_ref), (chip_hbm, chip_ref))
    wait_all(start_all([pltpu.make_async_copy(src, dst, in_sems.at[i]) for i, (src, dst) in enumerate(loads)]))
    pairs = ((ft_ref, ft_out), (win_ref, win_out), (wmid_ref, wmid_out), (wout_ref, wout_out), (norm_ref, norm_out))
    stores = [pltpu.make_async_copy(src, dst, out_sems.at[i]) for i, (src, dst) in enumerate(pairs)]
    spread(packed_refs, at_ref, ft_ref)
    stores[0].start()
    unpack(packed_refs, at_ref, win_ref, wmid_ref, wout_ref, norm_ref)
    start_all(stores[1:])
    wait_all(stores)


def first_kernel(adj_hbm, bound_hbm, keep_hbm, idx_hbm, ft_hbm, win_hbm, norm_hbm, recv_ref,
                 adj_ref, edge_ref, row_ref, sel_ref, mean_ref, xhat_ref, slope_ref, istd_ref, h_ref, invd_ref, send_ref,
                 halo_ref, keep_ref, idx_ref, ft_ref, win_ref, norm_ref, adj_buf, bound_buf, ring_sems, sems, *, width):
    nodes = edge_ref.shape[0]
    ring, tile = adj_buf.shape[0:2]

    def fetch(step, slot):
        return pltpu.make_async_copy(adj_hbm.at[rows_of(step, tile)], adj_buf.at[slot], ring_sems.at[0, slot])

    def fetch_bound(step, slot):
        return pltpu.make_async_copy(bound_hbm.at[rows_of(step, tile)], bound_buf.at[slot], ring_sems.at[1, slot])

    sources, targets = (keep_hbm, idx_hbm, ft_hbm, win_hbm, norm_hbm), (keep_ref, idx_ref, ft_ref, win_ref, norm_ref)
    small = [pltpu.make_async_copy(src, dst, sems.at[i]) for i, (src, dst) in enumerate(zip(sources, targets))]
    start_all(small[0:2])
    for step in range(bound_buf.shape[0]):
        fetch_bound(step, step).start()
    start_all(small[2:])
    for step in range(ring):
        fetch(step, step).start()
    join_halo(recv_ref, halo_ref, width)
    wait_all(small[0:2])
    select(idx_ref, sel_ref)

    def boundary(step, _):
        slot = lax.rem(step, bound_buf.shape[0])
        s = rows_of(step, tile)
        fetch_bound(step, slot).wait()
        edge_ref[s, :] = (bound_buf[slot] * keep_ref[...]).astype(F32).astype(BF)

        @pl.when(step + bound_buf.shape[0] < nodes // tile)
        def _():
            fetch_bound(step + bound_buf.shape[0], slot).start()

        return 0

    lax.fori_loop(0, nodes // tile, boundary, 0)
    wait_all(small[2:])

    def gather(step, _):
        for part in range(GATHER_PARTS):
            chunk = step * GATHER_PARTS + part
            slot = lax.rem(chunk, ring)
            fetch(chunk, slot).wait()
            adj_ref[rows_of(chunk, tile), :] = adj_buf[slot].astype(F32).astype(BF)

            @pl.when(chunk + ring < nodes // tile)
            def _():
                fetch(chunk + ring, slot).start()

        s = rows_of(step, GATHER_PARTS * tile)
        far = dot_nn(edge_ref[s, :], halo_ref[...])
        row_ref[s, :] = jnp.broadcast_to(far[:, LANE - 1 : LANE], far.shape)
        summed = dot_nt(adj_ref[s, :], ft_ref[...]) + far
        inv_deg = 1.0 / jnp.maximum(summed[:, LANE - 1 : LANE], 1.0)
        invd_ref[s, :] = jnp.broadcast_to(inv_deg, summed.shape)
        mean_ref[s, :] = (summed * inv_deg).astype(BF)
        return 0

    lax.fori_loop(0, nodes // (GATHER_PARTS * tile), gather, 0)

    def apply(s, _):
        joined = dot_tn(ft_ref[:, s], win_ref[0]) + dot_nn(mean_ref[s, :], win_ref[1])
        keep_norm(s, norm_forward(joined, norm_ref, 0), xhat_ref, slope_ref, istd_ref, h_ref)
        return 0

    loop(nodes, TILE, apply)
    send_ref[...] = dot_nn(sel_ref[...], h_ref[...]).astype(BF)


def gather_mean(adj_ref, hin_ref, edge_ref, halo_ref, invd_ref, mean_ref):
    def gather(s, _):
        summed = dot_nn(adj_ref[s, :], hin_ref[...]) + dot_nn(edge_ref[s, :], halo_ref[...])
        mean_ref[s, :] = (summed * both(invd_ref[s, :])).astype(BF)
        return 0

    loop(adj_ref.shape[0], TILE, gather)


def second_kernel(adj_ref, edge_ref, halo_ref, hin_ref, w_ref, norm_ref, invd_ref, sel_ref,
                  mean_ref, xhat_ref, slope_ref, istd_ref, h_ref, send_ref):
    gather_mean(adj_ref, hin_ref, edge_ref, halo_ref, invd_ref, mean_ref)

    def apply(s, _):
        joined = dot_nn(hin_ref[s, :], w_ref[0]) + dot_nn(mean_ref[s, :], w_ref[1])
        keep_norm(s, norm_forward(joined, norm_ref, 1), xhat_ref, slope_ref, istd_ref, h_ref)
        return 0

    loop(adj_ref.shape[0], TILE, apply)
    send_ref[...] = dot_nn(sel_ref[...], h_ref[...]).astype(BF)


def split_count(x):
    high = jnp.floor(x * (1.0 / 256.0))
    return high, x - 256.0 * high


def head_kernel(adj_ref, edge_ref, halo_ref, hin_ref, w_ref, invd_ref, sel_ref, mask_ref,
                mean_ref, logit_ref, pred_ref, cross_ref, mine_ref, send_ref):
    gather_mean(adj_ref, hin_ref, edge_ref, halo_ref, invd_ref, mean_ref)

    def apply(s, _):
        logits = dot_nt(hin_ref[s, :], w_ref[0]) + dot_nt(mean_ref[s, :], w_ref[1])
        logit_ref[s, :] = logits
        pred_ref[s, :] = jnp.where(iota(logits.shape, 1) == LANE - 1, 1.0, logits).astype(BF)
        return 0

    loop(adj_ref.shape[0], TILE, apply)
    mine = dot_nn(sel_ref[...], pred_ref[...])
    lane = iota(mine.shape, 1)
    mine = jnp.where(lane < 64, mine, 0.0)
    mine_ref[...] = mine
    cross = dot_tn(edge_ref[...], pred_ref[...])
    cross_ref[...] = cross
    high, low = bf_parts(jnp.where(lane < 64, cross, 0.0), 2)
    count = jnp.sum(mask_ref[...].astype(F32), keepdims=True)
    count_high, count_low = split_count(count)
    col_high, col_low = split_count(cross[:, LANE - 1 : LANE])
    extra = jnp.where(lane == 64, count_high, 0.0) + jnp.where(lane == 65, count_low, 0.0)
    extra = extra + jnp.where(lane == 66, col_high, 0.0) + jnp.where(lane == 67, col_low, 0.0)
    send_ref[:, 0:LANE] = (mine + pltpu.roll(widen(low), 64, 1)).astype(BF)
    send_ref[:, LANE:] = (widen(high) + extra).astype(BF)


def spread_row(values, row):
    pick = (iota(values.shape, 0) == row).astype(F32).astype(BF)
    return dot_tn(values.astype(F32).astype(BF), pick)


def logit_grad_kernel(logit_ref, label_ref, mask_ref, row_ref, pred_ref, edge_ref, recv_ref, mine_ref, cross_ref,
                      sel_ref, w_ref, invd_ref,
                      grad_ref, gs_ref, send_ref, loss_ref, hp_ref, ret_ref, lab_ref, wgt_ref, *, classes, each):
    slots = mine_ref.shape[0]
    nodes = logit_ref.shape[0]
    first, second = widen(recv_ref[:, 0:LANE]), widen(recv_ref[:, LANE:])
    lane = iota((slots, LANE), 1)
    low_half = lane < 64
    halo_pred = jnp.where(low_half, first, 0.0)
    back_cross = jnp.where(low_half, second + pltpu.roll(first, 64, 1), 0.0)
    count = 256.0 * jnp.sum(jnp.where(lane == 64, second, 0.0), keepdims=True)
    count = (count + jnp.sum(jnp.where(lane == 65, second, 0.0), keepdims=True)) * (1.0 / each)
    col_back = 256.0 * second[:, 66:67] + second[:, 67:68]
    scale = 2.0 * PEN_WEIGHT / count
    inv_count = 1.0 / count
    hp_ref[...] = halo_pred.astype(BF)
    ret_ref[...] = (scale * (col_back * mine_ref[...] - back_cross)).astype(BF)
    pen = jnp.sum(cross_ref[:, LANE - 1 : LANE] * (halo_pred * halo_pred), keepdims=True)
    pen = pen - 2.0 * jnp.sum(halo_pred * cross_ref[...], keepdims=True)
    for r in range(nodes // LANE):
        lab_ref[r * LANE : (r + 1) * LANE, :] = spread_row(label_ref[...], r)
        wgt_ref[r * LANE : (r + 1) * LANE, :] = spread_row(mask_ref[...], r)

    def body(s, carry):
        ce_sum, pen_sum = carry
        logits = logit_ref[s, :]
        lane = iota(logits.shape, 1)
        real = lane < classes
        top = jnp.max(jnp.where(real, logits, -jnp.inf), 1, keepdims=True)
        shifted = jnp.where(real, jnp.exp(jnp.where(real, logits - top, 0.0)), 0.0)
        total = jnp.sum(shifted, 1, keepdims=True)
        hot = (lane.astype(F32) == lab_ref[s, :]).astype(F32)
        target = jnp.sum(logits * hot, 1, keepdims=True)
        weight = wgt_ref[s, :]
        ce_sum = ce_sum + jnp.sum(weight[:, 0:1] * (top + jnp.log(total) - target), keepdims=True)
        pred = jnp.where(real, widen(pred_ref[s, :]), 0.0)
        drawn = row_ref[s, :] * pred
        pen_sum = pen_sum + jnp.sum(drawn * pred, keepdims=True)
        own = drawn - dot_nn(edge_ref[s, :], hp_ref[...])
        back = dot_tn(sel_ref[:, s], ret_ref[...])
        grad = ((inv_count * weight) * (shifted * (1.0 / total) - hot) + scale * own + back).astype(BF)
        grad_ref[s, :] = grad
        gs_ref[s, :] = (dot_nn(grad, w_ref[1]) * both(invd_ref[s, :])).astype(BF)
        return ce_sum, pen_sum

    zero = jnp.zeros((1, 1), F32)
    ce_sum, pen_sum = loop(nodes, TILE, body, (zero, zero))
    row = iota((8, LANE), 0)
    loss_ref[...] = (jnp.where(row == 0, ce_sum, 0.0) + jnp.where(row == 1, pen + pen_sum, 0.0)
                     + jnp.where(row == 2, count, 0.0))
    send_ref[...] = dot_tn(edge_ref[...], gs_ref[...]).astype(BF)


BACK_TILE = 1024


def layer_back(adj_ref, gs_ref, grad_ref, w_ref, sel_ref, halo_ref, slope_ref, xhat_ref, istd_ref, norm_ref, layer, own_ref, gj_ref, back):
    nodes = adj_ref.shape[0]

    def pull(s, _):
        own_ref[s, :] = (dot_tn(adj_ref[:, s], gs_ref[...]) + back(grad_ref[s, :], w_ref[0])
                         + dot_tn(sel_ref[:, s], halo_ref[...]))
        return 0

    loop(nodes, BACK_TILE, pull)

    def body(s, carry):
        gain_sum, bias_sum = carry
        grad_pre = own_ref[s, :] * slope_ref[s, :]
        x_hat = xhat_ref[s, :]
        grad_x = grad_pre * norm_ref[2 * layer : 2 * layer + 1, :]
        mean_one = jnp.sum(grad_x, 1, keepdims=True) * (1.0 / HID)
        mean_two = jnp.sum(grad_x * x_hat, 1, keepdims=True) * (1.0 / HID)
        gj_ref[s, :] = (both(istd_ref[s, :]) * (grad_x - mean_one - x_hat * mean_two)).astype(BF)
        gain_sum = gain_sum + jnp.sum(grad_pre * x_hat, 0, keepdims=True)
        bias_sum = bias_sum + jnp.sum(grad_pre, 0, keepdims=True)
        return gain_sum, bias_sum

    zero = jnp.zeros((1, HID), F32)
    return loop(nodes, TILE, body, (zero, zero))


def second_back_kernel(adj_ref, gsin_ref, grad_ref, wout_ref, recv_ref, sel_ref, slope_ref, xhat_ref, istd_ref, norm_ref, w_ref,
                       invd_ref, edge_ref, h_two_ref, mean_head_ref, h_one_ref, mean_two_ref, at_ref,
                       gj_ref, gs_ref, send_ref, sums_ref, own_ref, full_ref, head_ref, *, each):
    gain_sum, bias_sum = layer_back(
        adj_ref, gsin_ref, grad_ref, wout_ref, sel_ref, recv_ref, slope_ref, xhat_ref, istd_ref, norm_ref, 1, own_ref, gj_ref, dot_nn
    )
    row = iota((8, HID), 0)
    sums_ref[...] = jnp.where(row == 2, gain_sum, 0.0) + jnp.where(row == 3, bias_sum, 0.0)

    def body(s, _):
        gs_ref[s, :] = (dot_nt(gj_ref[s, :], w_ref[1]) * both(invd_ref[s, :])).astype(BF)
        return 0

    loop(adj_ref.shape[0], TILE, body)
    parts = send_ref.shape[0]
    send_ref[:, 0:each, :] = dot_tn(edge_ref[...], gs_ref[...]).astype(BF).reshape(parts, each, HID)
    share = HID // FEATS
    half = pl.ds(pl.multiple_of(at_ref[0] * share // LANE * LANE, LANE), LANE)
    start = at_ref[0] * share % LANE
    head_ref[:, 0:LANE] = dot_tn(h_two_ref[:, half], grad_ref[...])
    head_ref[:, LANE:] = dot_tn(mean_head_ref[:, half], grad_ref[...])
    full_ref[0] = dot_tn(h_one_ref[:, half], gj_ref[...])
    full_ref[1] = dot_tn(mean_two_ref[:, half], gj_ref[...])
    for q in range(parts):
        if q * 16 < 2 * share:
            k, r = divmod(q * 16, share)
            send_ref[q, each : each + 16, :] = full_ref[k, pl.ds(pl.multiple_of(start + r, 16), 16), :].astype(BF)
            rows = head_ref[pl.ds(pl.multiple_of(start + q * 8, 8), 8), :]
            high, low = bf_parts(rows, 2)
            send_ref[q, each + 16 : each + 32, :] = jnp.concatenate([widen(high), widen(low)], 0).astype(BF)
        else:
            send_ref[q, each : each + 32, :] = jnp.zeros((32, HID), BF)


FEATS = 4


def first_back_kernel(adj_ref, gsin_ref, grad_ref, w_ref, recv_ref, sel_ref, slope_ref, xhat_ref, istd_ref, norm_ref,
                      ft_ref, mean_ref, loss_ref, sums_ref, at_ref,
                      send_ref, gj_ref, own_ref, full_ref, halo_ref, *, each):
    parts = recv_ref.shape[0]
    halo_ref[...] = recv_ref[:, 0:each, :].reshape(halo_ref.shape)
    gain_sum, bias_sum = layer_back(
        adj_ref, gsin_ref, grad_ref, w_ref, sel_ref, halo_ref, slope_ref, xhat_ref, istd_ref, norm_ref, 0, own_ref, gj_ref, dot_nt
    )
    row = iota((8, HID), 0)
    sums = sums_ref[...] + jnp.where(row == 0, gain_sum, 0.0) + jnp.where(row == 1, bias_sum, 0.0)
    full_ref[0] = dot_nn(ft_ref[...], gj_ref[...])
    full_ref[1] = dot_tn(mean_ref[...], gj_ref[...])
    at = rows_of(at_ref[0], FEAT_PAD)
    mid = jnp.zeros((16, HID), F32)
    out = jnp.zeros((16, HID), F32)
    for q in range(parts):
        mid = mid + widen(recv_ref[q, each : each + 16, :])
        out = out + widen(recv_ref[q, each + 16 : each + 32, :])
    out = out + pltpu.roll(out, 8, 0)
    mid_high, mid_low = bf_parts(mid, 2)
    out_high, out_low = bf_parts(out, 2)
    out = jnp.where(iota((16, HID), 0) < 8, widen(out_high), widen(out_low))
    lane = iota((8, HID), 1)
    blocks = []
    for k, norm_part in enumerate(bf_parts(sums, 2)):
        tail = jnp.zeros((8, HID), F32)
        for p, part in enumerate(bf_parts(jnp.broadcast_to(loss_ref[k : k + 1, 0:1], (8, HID)), 3)):
            tail = tail + jnp.where(lane == p, widen(part), 0.0)
        rows = full_ref[k, at, :]
        last = jnp.where(row == 0, rows[FEAT_PAD - 8 :, :], jnp.where(row == 3, tail, 0.0))
        blocks += [rows[0 : FEAT_PAD - 8, :], jnp.where(row >= 4, pltpu.roll(widen(norm_part), 4, 0), last)]
    message = jnp.concatenate([*blocks, widen(mid_high), widen(mid_low), out], 0).astype(BF)
    for q in range(parts):
        send_ref[q] = message


CHUNK_ROW = 2 * FEAT_PAD
MESSAGE_ROWS = CHUNK_ROW + 48


def total_kernel(recv_ref, grads_ref, norm_ref, loss_ref, mid_ref, out_ref, square_ref, *, width):
    parts = recv_ref.shape[0]
    grads = jnp.zeros((CHUNK_ROW, HID), F32)
    for q in range(parts):
        grads = grads + widen(recv_ref[q, 0:CHUNK_ROW, :])
    grads_ref[...] = grads
    tails = [grads[FEAT_PAD - 8 : FEAT_PAD, :], grads[2 * FEAT_PAD - 8 :, :]]
    row = iota((8, HID), 0)
    norms = jnp.where(row < 4, pltpu.roll(tails[0] + tails[1], 4, 0), 0.0)
    norm_ref[...] = norms
    sums = [jnp.sum(tail[3:4, :], keepdims=True) for tail in tails]
    loss_ref[...] = jnp.broadcast_to(sums[0] + PEN_WEIGHT * sums[1], loss_ref.shape)
    for q in range(mid_ref.shape[0] // 16):
        at = CHUNK_ROW
        mid_ref[q * 16 : q * 16 + 16, :] = widen(recv_ref[q, at : at + 16, :]) + widen(recv_ref[q, at + 16 : at + 32, :])
        rows = widen(recv_ref[q, at + 32 : at + 48, :])
        out_ref[q * 8 : q * 8 + 8, :] = rows[0:8, :] + rows[8:16, :]
    weight_row = (iota((CHUNK_ROW, HID), 0) & (FEAT_PAD - 1)) < width
    first = jnp.where(weight_row, grads, 0.0)
    square = jnp.sum(first * first, keepdims=True)
    square = square + jnp.sum(mid_ref[...] * mid_ref[...], keepdims=True)
    square = square + jnp.sum(out_ref[...] * out_ref[...], keepdims=True)
    row = iota((8, LANE), 0)
    square_ref[...] = jnp.where(row == 1, jnp.sum(norms * norms, keepdims=True), square)


def adam(param, grad, first, second):
    first_new = BETA_ONE * first + (1.0 - BETA_ONE) * grad
    second_new = BETA_TWO * second + (1.0 - BETA_TWO) * grad * grad
    first_hat = first_new / (1.0 - BETA_ONE**STEP)
    second_hat = second_new / (1.0 - BETA_TWO**STEP)
    fresh = param - RATE * (first_hat / (jnp.sqrt(second_hat) + ADAM_EPS) + DECAY * param)
    return fresh, first_new, second_new


def update_kernel(grads_ref, gnorm_ref, total_ref, gmid_ref, gout_ref, sq0_ref, sq1_ref, sq2_ref, sq3_ref, loss_ref,
                  w_in, w_mid, w_out, norm, m_in, m_mid, m_out, m_norm, v_in, v_mid, v_out, v_norm, at_ref,
                  loss_out, count_out, gnorm_out,
                  nw_in, nw_mid, nw_out, nnorm, nm_in, nm_mid, nm_out, nm_norm, nv_in, nv_mid, nv_out, nv_norm,
                  c_in, c_mid, c_out):
    loss_out[...] = total_ref[0:1, 0:1]
    count_out[...] = loss_ref[2:3, 0:1]
    square = (sq0_ref[0:1, 0:1] + sq1_ref[0:1, 0:1]) + (sq2_ref[0:1, 0:1] + sq3_ref[0:1, 0:1])
    grad_norm = jnp.sqrt(square + sq0_ref[1:2, 0:1])
    gnorm_out[...] = grad_norm
    factor = jnp.minimum(1.0, CLIP_LEVEL / (grad_norm + 1e-06))

    def step(index, grad, w, m, v, nw, nm, nv, copy):
        fresh, first, second = adam(w[index], grad * factor, m[index], v[index])
        nw[index], nm[index], nv[index] = fresh, first, second
        if copy is not None:
            copy[index] = fresh.astype(BF)

    every = slice(None)
    width, _, share = w_in.shape[0], 2, w_mid.shape[1]
    classes = w_out.shape[0]
    for k in range(2):
        step((every, k, every), grads_ref[k * FEAT_PAD : k * FEAT_PAD + width, :], w_in, m_in, v_in, nw_in, nm_in, nv_in, c_in)
        step(k, gmid_ref[k * share : (k + 1) * share, :], w_mid, m_mid, v_mid, nw_mid, nm_mid, nv_mid, c_mid)
        turned = jnp.transpose(gout_ref[:, k * LANE : (k + 1) * LANE])[0:classes, :]
        step((every, k, every), turned, w_out, m_out, v_out, nw_out, nm_out, nv_out, c_out)
    whole = gnorm_ref[...]
    mine = jnp.zeros((8, share), F32)
    for f in range(HID // share):
        mine = mine + jnp.where(at_ref[0] == f, whole[:, f * share : (f + 1) * share], 0.0)
    for layer in range(2):
        step(layer, mine[2 * layer : 2 * layer + 2, :], norm, m_norm, v_norm, nnorm, nm_norm, nv_norm, None)


def exchange(x, parts):
    return lax.all_to_all(x.reshape(parts, -1, x.shape[-1]), "dom", split_axis=0, concat_axis=0, tiled=True)


def native(w_in, w_mid, w_out, norm):
    return (jnp.transpose(w_in, (1, 0, 2)), w_mid, jnp.transpose(w_out, (2, 0, 1)), norm)


def restore(w_in, w_mid, w_out, *norm):
    return (jnp.transpose(w_in, (1, 0, 2)), w_mid, jnp.transpose(w_out, (1, 2, 0)), *norm)


def shards(
    features,
    inner_adj,
    bound_adj,
    keep_slots,
    send_index,
    labels,
    train_mask,
    w_in,
    w_mid,
    w_out,
    norm_params,
    m_in,
    m_mid,
    m_out,
    m_norms,
    v_in,
    v_mid,
    v_out,
    v_norms,
    *,
    parts,
    feats,
):
    nodes = features.shape[0]
    each = send_index.shape[2]
    halo = parts * each
    classes = w_out.shape[2]
    share = w_mid.shape[1]
    width = features.shape[1]
    run = functools.partial(call, mib=16 if parts <= 16 else 52)
    labels = labels.reshape(nodes // LANE, LANE)
    mask = train_mask.reshape(nodes // LANE, LANE)
    params = native(w_in, w_mid, w_out, norm_params)
    firsts = native(m_in, m_mid, m_out, m_norms)
    seconds = native(v_in, v_mid, v_out, v_norms)
    feat_at = lax.axis_index("feat").astype(jnp.int32).reshape(1)

    def bf(*dims):
        return shape(*dims, dtype=BF)

    def in_hbm(*arrays):
        return tuple(pltpu.with_memory_space_constraint(a, pltpu.HBM) for a in arrays)

    loads = in_hbm(send_index, features.T, *params)
    send, own, at = run(
        pack_kernel, [bf(parts, feats, each // 2, LANE), bf(pack_rows(nodes, share), HID), shape(1, dtype=jnp.int32)],
        *loads, feat_at, smem_in=(6,), smem_out=(2,), hbm_in=range(6),
        scratch=[pltpu.VMEM((halo, nodes), BF)] + [pltpu.VMEM(a.shape, a.dtype) for a in loads] + [pltpu.SemaphoreType.DMA((6,))],
    )
    recv = lax.all_to_all(
        send.reshape(parts * feats, each // 2, LANE), ("dom", "feat"), split_axis=0, concat_axis=0, tiled=True
    ).reshape(parts, feats, each // 2, LANE)
    chip = lax.ppermute(own, "feat", [(s, s ^ 2) for s in range(feats)])
    core = lax.ppermute(own, "feat", [(s, s ^ 1) for s in range(feats)])
    far = lax.ppermute(chip, "feat", [(s, s ^ 1) for s in range(feats)])
    loads = in_hbm(own, chip)
    results = [((feats * FEAT_PAD, nodes), BF), ((2, feats * FEAT_PAD, HID), BF), ((2, HID, HID), BF), ((2, LANE, HID), BF), ((8, HID), F32)]
    ft, win, wmid, wout, norms = run(
        side_kernel, [pltpu.HBM(*r) for r in results], *loads, core, far, at, hbm_in=range(2), smem_in=(4,), hbm_out=range(5),
        scratch=[pltpu.VMEM(*r) for r in results] + [pltpu.VMEM(a.shape, a.dtype) for a in loads]
        + [pltpu.SemaphoreType.DMA((2,)), pltpu.SemaphoreType.DMA((5,))],
    )
    loads = in_hbm(inner_adj, bound_adj, keep_slots, send_index, ft, win, norms)
    ring, bound_ring = (4, 8) if parts <= 16 else (2, 2)
    adj, edge, row_deg, sel, mean_one, xhat_one, slope_one, istd_one, h_one, inv_deg, send = run(
        functools.partial(first_kernel, width=width),
        [bf(nodes, nodes), bf(nodes, halo), shape(nodes, LANE), bf(halo, nodes), bf(nodes, LANE),
         shape(nodes, HID), shape(nodes, HID), shape(nodes, LANE), bf(nodes, HID), shape(nodes, LANE), bf(halo, HID)],
        *loads, recv, hbm_in=range(7),
        scratch=[pltpu.VMEM((halo, LANE), BF), pltpu.VMEM(keep_slots.shape, jnp.int32), pltpu.VMEM(send_index.shape, jnp.int32)]
        + [pltpu.VMEM(a.shape, a.dtype) for a in loads[4:]]
        + [pltpu.VMEM((ring, CONVERT_TILE, nodes), jnp.int32), pltpu.VMEM((bound_ring, CONVERT_TILE, halo), jnp.int32),
           pltpu.SemaphoreType.DMA((2, max(ring, bound_ring))), pltpu.SemaphoreType.DMA((5,))],
    )
    halo_one = exchange(send, parts).reshape(halo, HID)
    mean_two, xhat_two, slope_two, istd_two, h_two, send = run(
        second_kernel,
        [bf(nodes, HID), shape(nodes, HID), shape(nodes, HID), shape(nodes, LANE), bf(nodes, HID), bf(halo, HID)],
        adj, edge, halo_one, h_one, wmid, norms, inv_deg, sel,
    )
    halo_two = exchange(send, parts).reshape(halo, HID)
    mean_head, logits, pred, cross, mine, send = run(
        head_kernel,
        [bf(nodes, HID), shape(nodes, LANE), bf(nodes, LANE), shape(halo, LANE), shape(halo, LANE), bf(halo, HID)],
        adj, edge, halo_two, h_two, wout, inv_deg, sel, mask,
    )
    recv = exchange(send, parts).reshape(halo, HID)
    grad, grad_sum, send, losses = run(
        functools.partial(logit_grad_kernel, classes=classes, each=each),
        [bf(nodes, LANE), bf(nodes, HID), bf(halo, HID), shape(8, LANE)],
        logits, labels, mask, row_deg, pred, edge, recv, mine, cross, sel, wout, inv_deg,
        scratch=[pltpu.VMEM((halo, LANE), BF), pltpu.VMEM((halo, LANE), BF), pltpu.VMEM((nodes, LANE), F32), pltpu.VMEM((nodes, LANE), F32)],
    )
    recv = exchange(send, parts).reshape(halo, HID)
    joined_two, grad_sum, send, norm_sums = run(
        functools.partial(second_back_kernel, each=each),
        [bf(nodes, HID), bf(nodes, HID), bf(parts, each + 32, HID), shape(8, HID)],
        adj, grad_sum, grad, wout, recv, sel, slope_two, xhat_two, istd_two, norms, wmid, inv_deg, edge,
        h_two, mean_head, h_one, mean_two, at, smem_in=(17,),
        scratch=[pltpu.VMEM((nodes, HID), F32), pltpu.VMEM((2, LANE, HID), F32), pltpu.VMEM((LANE, HID), F32)],
    )
    recv = exchange(send, parts)
    send, = run(
        functools.partial(first_back_kernel, each=each), [bf(parts, MESSAGE_ROWS, HID)],
        adj, grad_sum, joined_two, wmid, recv, sel, slope_one, xhat_one, istd_one, norms, ft, mean_one, losses, norm_sums, at,
        smem_in=(14,),
        scratch=[pltpu.VMEM((nodes, HID), BF), pltpu.VMEM((nodes, HID), F32), pltpu.VMEM((2, feats * FEAT_PAD, HID), F32),
                 pltpu.VMEM((halo, HID), BF)],
    )
    recv = exchange(send, parts)
    *grads, square = run(
        functools.partial(total_kernel, width=width),
        [shape(CHUNK_ROW, HID), shape(8, HID), shape(8, LANE), shape(2 * share, HID), shape(share, HID), shape(8, LANE)], recv,
    )
    squares = [square]
    for k in range(1, feats):
        squares.append(lax.ppermute(square, "feat", [(s, s ^ k) for s in range(feats)]))
    outs = [shape(1, 1)] * 3 + [shape(*p.shape) for p in params] * 3 + [bf(*p.shape) for p in params[:3]]
    result = run(update_kernel, outs, *grads, *squares, losses, *params, *firsts, *seconds, at, smem_in=(22,))
    return (
        tuple(r.reshape(()) for r in result[:3])
        + restore(*result[3:7]) + restore(*result[7:11]) + restore(*result[11:15]) + restore(*result[15:])
    )


def solution(mesh):
    weight = P(None, "feat", None)
    norm = P(None, None, "feat")
    placed = (
        P("dom", "feat"), P("dom", None), P("dom", None), P("dom", None), P("dom", None, None), P("dom"), P("dom"),
    ) + (weight, weight, weight, norm) * 3
    return jax.shard_map(
        functools.partial(shards, parts=mesh.shape["dom"], feats=mesh.shape["feat"]),
        mesh=mesh,
        in_specs=placed,
        out_specs=(P(), P(), P()) + (weight, weight, weight, norm) * 3 + (weight,) * 3,
        check_vma=False,
    )
```

```python
import functools
import math

import jax
import jax.numpy as jnp
from jax import lax
from jax.experimental import pallas as pl
from jax.experimental.pallas import tpu as pltpu
from jax.sharding import PartitionSpec as P

HID = 256
STEP = 5

NORM_EPS = 1e-05
PEN_WEIGHT = 0.001
CLIP_LEVEL = 0.01
RATE = 0.05
BETA_ONE = 0.5
BETA_TWO = 0.5
ADAM_EPS = 1e-08
DECAY = 0.01

BF = jnp.bfloat16
F32 = jnp.float32
LANE = 128
FEAT_PAD = 32
MIB = 1 << 20
CONVERT_TILE = 256

VMEM = pl.BlockSpec(memory_space=pltpu.VMEM)
SMEM = pl.BlockSpec(memory_space=pltpu.SMEM)
ANY = pl.BlockSpec(memory_space=pl.ANY)
HBM = pl.BlockSpec(memory_space=pltpu.HBM)


def dot_nn(a, b):
    return jnp.dot(a, b, preferred_element_type=F32)


def dot_tn(a, b):
    return lax.dot_general(a, b, (((0,), (0,)), ((), ())), preferred_element_type=F32)


def dot_nt(a, b):
    return lax.dot_general(a, b, (((1,), (1,)), ((), ())), preferred_element_type=F32)


def iota(shape, axis):
    return lax.broadcasted_iota(jnp.int32, shape, axis)


def place(rows, cols, shift, turned=False):
    dims = (cols, rows) if turned else (rows, cols)
    return (iota(dims, int(turned)) + shift == iota(dims, int(not turned))).astype(F32).astype(BF)


def widen(x):
    return x.astype(F32)


def bf_parts(x, count):
    parts = []
    for _ in range(count):
        part = x.astype(BF)
        parts.append(part)
        x = x - widen(part)
    return parts


def both(x):
    return jnp.concatenate([x, x], 1)


def rows_of(i, tile):
    return pl.ds(pl.multiple_of(i * tile, tile), tile)


def call(kernel, outs, *args, mib=24, flops=0, smem_in=(), any_in=(), hbm_in=(), smem_out=(), hbm_out=(), scratch=()):
    size = sum(math.prod(a.shape) * a.dtype.itemsize for a in (*args, *outs))
    return pl.pallas_call(
        kernel,
        out_shape=outs,
        in_specs=[SMEM if i in smem_in else ANY if i in any_in else HBM if i in hbm_in else VMEM for i in range(len(args))],
        out_specs=[SMEM if i in smem_out else HBM if i in hbm_out else VMEM for i in range(len(outs))],
        scratch_shapes=list(scratch),
        cost_estimate=pl.CostEstimate(flops=flops, bytes_accessed=size // 4, transcendentals=0),
        compiler_params=pltpu.CompilerParams(vmem_limit_bytes=mib * MIB),
    )(*args)


def shape(*dims, dtype=F32):
    return jax.ShapeDtypeStruct(dims, dtype)


def select(idx_ref, sel_ref):
    nodes = sel_ref.shape[1]
    parts, each = idx_ref.shape[1:]
    eye = iota((each, each), 0) == iota((each, each), 1)
    for p in range(parts):
        column = jnp.sum(jnp.where(eye, idx_ref[0, p : p + 1, :].astype(F32), 0.0), 1, keepdims=True)
        hot = iota((each, nodes), 1) == column.astype(jnp.int32)
        sel_ref[p * each : (p + 1) * each, :] = hot.astype(F32).astype(BF)


def pack_kernel(idx_hbm, feat_hbm, w_in_hbm, w_mid_hbm, w_out_hbm, norm_hbm, at_ref, send_ref, pack_ref, at_out,
                sel_ref, idx_ref, feat_ref, w_in_ref, w_mid_ref, w_out_ref, norm_ref, sems):
    sources = (idx_hbm, feat_hbm, w_mid_hbm, w_in_hbm, w_out_hbm, norm_hbm)
    targets = (idx_ref, feat_ref, w_mid_ref, w_in_ref, w_out_ref, norm_ref)
    copies = [pltpu.make_async_copy(src, dst, sems.at[i]) for i, (src, dst) in enumerate(zip(sources, targets))]
    for copy in copies:
        copy.start()
    at_out[0] = at_ref[0]
    copies[0].wait()
    select(idx_ref, sel_ref)
    wait_all(copies[1:])
    nodes = feat_ref.shape[1]
    width, share = feat_ref.shape[0], w_mid_ref.shape[1]
    classes = w_out_ref.shape[0]
    rows = dot_nn(place(FEAT_PAD, width, 0), feat_ref[...].astype(BF))
    parts, copies, half, _ = send_ref.shape
    sent = dot_nt(sel_ref[...], rows.astype(BF)).astype(BF)
    left = dot_nn(sent, place(FEAT_PAD, LANE, 0)).reshape(parts, 2, half, LANE)[:, 0]
    right = dot_nn(sent, place(FEAT_PAD, LANE, LANE // 2)).reshape(parts, 2, half, LANE)[:, 1]
    for f in range(copies):
        send_ref[:, f] = (left + right).astype(BF)
    ones = iota((FEAT_PAD, nodes), 0) == FEAT_PAD - 1
    blocks = [jnp.zeros((FEAT_PAD, HID), F32) for _ in range(3)]
    for layer in range(2):
        for p, part in enumerate(bf_parts(norm_ref[layer], 3)):
            part = dot_nn(part, place(share, HID, 0)).astype(BF)
            blocks[p] = blocks[p] + dot_nn(place(2, FEAT_PAD, NORM_AT + 2 * layer, turned=True), part)
    blocks.append(jnp.zeros((FEAT_PAD, nodes - 3 * HID), F32))
    rows = (jnp.where(ones, 1.0, rows) + jnp.concatenate(blocks, 1)).astype(BF)
    at = 0
    for b in range(nodes // HID):
        pack_ref[at : at + FEAT_PAD, :] = rows[:, b * HID : (b + 1) * HID]
        at += FEAT_PAD
    for k in range(2):
        pack_ref[at : at + share, :] = w_mid_ref[k].astype(BF)
        at += share
    for k in range(2):
        pack_ref[at : at + FEAT_PAD, :] = dot_nn(place(FEAT_PAD, width, 0), w_in_ref[:, k, :].astype(BF)).astype(BF)
        at += FEAT_PAD
    turned = jnp.zeros((2 * CLASS_HALF, LANE), F32)
    for k in range(2):
        grown = dot_nn(place(classes, 2 * CLASS_HALF, 0, turned=True), w_out_ref[:, k, :].astype(BF)).astype(BF)
        turned = turned + dot_nn(grown, place(share, LANE, k * share))
    turned = turned.astype(BF)
    for half in range(2):
        pack_ref[at : at + CLASS_HALF, half * LANE : (half + 1) * LANE] = turned[half * CLASS_HALF : (half + 1) * CLASS_HALF, :]


NORM_AT = FEAT_PAD - 6
CLASS_HALF = 32


def pack_rows(nodes, share):
    return nodes // HID * FEAT_PAD + 2 * share + 2 * FEAT_PAD + CLASS_HALF


def spread(packed_refs, at_ref, ft_ref):
    row = iota((FEAT_PAD, HID), 0)
    keep = (row < NORM_AT) | (row == FEAT_PAD - 1)
    for k, packed_ref in enumerate(packed_refs):
        at = rows_of(at_ref[0] ^ k, FEAT_PAD)
        for b in range(ft_ref.shape[1] // HID):
            rows = widen(packed_ref[b * FEAT_PAD : (b + 1) * FEAT_PAD, :])
            ft_ref[at, b * HID : (b + 1) * HID] = jnp.where(keep, rows, 0.0).astype(BF)


def join_halo(recv_ref, halo_ref, width):
    parts, feats, half, _ = recv_ref.shape
    lane = iota((parts * half, LANE), 1)
    sides = [jnp.where(lane == LANE - 1, 1.0, 0.0)] * 2
    for f in range(feats):
        rows = widen(recv_ref[:, f]).reshape(parts * half, LANE)
        for g in range(2):
            at = g * (LANE // 2)
            side = jnp.where((lane >= at) & (lane < at + width), rows, 0.0)
            shift = (f * FEAT_PAD - at) % LANE
            sides[g] = sides[g] + (pltpu.roll(side, shift, 1) if shift else side)
    sides = [side.astype(BF).reshape(parts, half, LANE) for side in sides]
    halo_ref[...] = jnp.stack(sides, 1).reshape(halo_ref.shape)


def unpack(packed_refs, at_ref, win_ref, wmid_ref, wout_ref, norm_ref):
    share = HID // len(packed_refs)
    norms = jnp.zeros((8, HID), F32)
    heads = [jnp.zeros((2 * CLASS_HALF, HID), F32) for _ in range(2)]
    for offset, packed_ref in enumerate(packed_refs):
        f = at_ref[0] ^ offset
        at = packed_ref.shape[0] - 2 * share - 2 * FEAT_PAD - CLASS_HALF
        for k in range(2):
            wmid_ref[k, rows_of(f, share), :] = packed_ref[at : at + share, :]
            at += share
        for k in range(2):
            win_ref[k, rows_of(f, FEAT_PAD), :] = packed_ref[at : at + FEAT_PAD, :]
            at += FEAT_PAD
        halves = [widen(packed_ref[at : at + CLASS_HALF, h * LANE : (h + 1) * LANE]) for h in range(2)]
        head = both(jnp.concatenate(halves, 0))
        lane = iota(head.shape, 1)
        heads[0] = heads[0] + pltpu.roll(jnp.where(lane < share, head, 0.0), f * share, 1)
        heads[1] = heads[1] + pltpu.roll(jnp.where((lane >= LANE + share) & (lane < LANE + 2 * share), head, 0.0),
                                         (f * share + LANE - share) & (HID - 1), 1)
        part = jnp.zeros((8, HID), F32)
        for p in range(3):
            part = part + widen(packed_ref[p * FEAT_PAD + 16 : (p + 1) * FEAT_PAD, :])[8:16, :]
        part = jnp.where((iota((8, HID), 0) >= NORM_AT - 24) & (iota((8, HID), 0) < NORM_AT - 20), part, 0.0)
        norms = norms + pltpu.roll(part, f * share, 1)
    for k in range(2):
        wout_ref[k, 0 : 2 * CLASS_HALF, :] = heads[k].astype(BF)
        wout_ref[k, 2 * CLASS_HALF :, :] = jnp.zeros((LANE - 2 * CLASS_HALF, HID), BF)
    norm_ref[...] = pltpu.roll(norms, 8 - (NORM_AT - 24), 0)


TILE = 1024


def loop(count, tile, body, carry=0):
    return lax.fori_loop(0, count // tile, lambda i, c: body(rows_of(i, tile), c), carry)


def norm_forward(joined, norm_ref, layer):
    center = jnp.sum(joined, 1, keepdims=True) * (1.0 / HID)
    spread = jnp.sum(joined * joined, 1, keepdims=True) * (1.0 / HID) - center * center
    inv_std = lax.rsqrt(spread + NORM_EPS)
    x_hat = (joined - center) * inv_std
    normed = x_hat * norm_ref[2 * layer : 2 * layer + 1, :] + norm_ref[2 * layer + 1 : 2 * layer + 2, :]
    gate = 0.5 * jnp.tanh(0.5 * normed) + 0.5
    hidden = normed * gate
    return inv_std, x_hat, hidden, gate + hidden * (1.0 - gate)


def keep_norm(s, parts, xhat_ref, slope_ref, istd_ref, h_ref):
    inv_std, x_hat, hidden, slope = parts
    xhat_ref[s, :] = x_hat
    slope_ref[s, :] = slope
    istd_ref[s, :] = jnp.broadcast_to(inv_std, (x_hat.shape[0], LANE))
    h_ref[s, :] = hidden.astype(BF)


GATHER_PARTS = 2


def start_all(copies):
    for copy in copies:
        copy.start()
    return copies


def wait_all(copies):
    for copy in copies:
        copy.wait()


def side_kernel(own_hbm, chip_hbm, core_ref, far_ref, at_ref,
                ft_out, win_out, wmid_out, wout_out, norm_out,
                ft_ref, win_ref, wmid_ref, wout_ref, norm_ref, own_ref, chip_ref, in_sems, out_sems):
    packed_refs = (own_ref, core_ref, chip_ref, far_ref)
    loads = ((own_hbm, own_ref), (chip_hbm, chip_ref))
    wait_all(start_all([pltpu.make_async_copy(src, dst, in_sems.at[i]) for i, (src, dst) in enumerate(loads)]))
    pairs = ((ft_ref, ft_out), (win_ref, win_out), (wmid_ref, wmid_out), (wout_ref, wout_out), (norm_ref, norm_out))
    stores = [pltpu.make_async_copy(src, dst, out_sems.at[i]) for i, (src, dst) in enumerate(pairs)]
    spread(packed_refs, at_ref, ft_ref)
    stores[0].start()
    unpack(packed_refs, at_ref, win_ref, wmid_ref, wout_ref, norm_ref)
    start_all(stores[1:])
    wait_all(stores)


def first_kernel(adj_hbm, bound_hbm, keep_hbm, idx_hbm, ft_hbm, win_hbm, norm_hbm, recv_ref,
                 adj_ref, edge_ref, row_ref, sel_ref, mean_ref, xhat_ref, slope_ref, istd_ref, h_ref, invd_ref, send_ref,
                 halo_ref, keep_ref, idx_ref, ft_ref, win_ref, norm_ref, adj_buf, bound_buf, ring_sems, sems, *, width):
    nodes = edge_ref.shape[0]
    ring, tile = adj_buf.shape[0:2]

    def fetch(step, slot):
        return pltpu.make_async_copy(adj_hbm.at[rows_of(step, tile)], adj_buf.at[slot], ring_sems.at[0, slot])

    def fetch_bound(step, slot):
        return pltpu.make_async_copy(bound_hbm.at[rows_of(step, tile)], bound_buf.at[slot], ring_sems.at[1, slot])

    sources, targets = (keep_hbm, idx_hbm, ft_hbm, win_hbm, norm_hbm), (keep_ref, idx_ref, ft_ref, win_ref, norm_ref)
    small = [pltpu.make_async_copy(src, dst, sems.at[i]) for i, (src, dst) in enumerate(zip(sources, targets))]
    start_all(small[0:2])
    for step in range(bound_buf.shape[0]):
        fetch_bound(step, step).start()
    start_all(small[2:])
    for step in range(ring):
        fetch(step, step).start()
    join_halo(recv_ref, halo_ref, width)
    wait_all(small[0:2])
    select(idx_ref, sel_ref)

    def boundary(step, _):
        slot = lax.rem(step, bound_buf.shape[0])
        s = rows_of(step, tile)
        fetch_bound(step, slot).wait()
        edge_ref[s, :] = (bound_buf[slot] * keep_ref[...]).astype(F32).astype(BF)

        @pl.when(step + bound_buf.shape[0] < nodes // tile)
        def _():
            fetch_bound(step + bound_buf.shape[0], slot).start()

        return 0

    lax.fori_loop(0, nodes // tile, boundary, 0)
    wait_all(small[2:])

    def gather(step, _):
        for part in range(GATHER_PARTS):
            chunk = step * GATHER_PARTS + part
            slot = lax.rem(chunk, ring)
            fetch(chunk, slot).wait()
            adj_ref[rows_of(chunk, tile), :] = adj_buf[slot].astype(F32).astype(BF)

            @pl.when(chunk + ring < nodes // tile)
            def _():
                fetch(chunk + ring, slot).start()

        s = rows_of(step, GATHER_PARTS * tile)
        far = dot_nn(edge_ref[s, :], halo_ref[...])
        row_ref[s, :] = jnp.broadcast_to(far[:, LANE - 1 : LANE], far.shape)
        summed = dot_nt(adj_ref[s, :], ft_ref[...]) + far
        inv_deg = 1.0 / jnp.maximum(summed[:, LANE - 1 : LANE], 1.0)
        invd_ref[s, :] = jnp.broadcast_to(inv_deg, summed.shape)
        mean_ref[s, :] = (summed * inv_deg).astype(BF)
        return 0

    lax.fori_loop(0, nodes // (GATHER_PARTS * tile), gather, 0)

    def apply(s, _):
        joined = dot_tn(ft_ref[:, s], win_ref[0]) + dot_nn(mean_ref[s, :], win_ref[1])
        keep_norm(s, norm_forward(joined, norm_ref, 0), xhat_ref, slope_ref, istd_ref, h_ref)
        return 0

    loop(nodes, TILE, apply)
    send_ref[...] = dot_nn(sel_ref[...], h_ref[...]).astype(BF)


def gather_mean(adj_ref, hin_ref, edge_ref, halo_ref, invd_ref, mean_ref):
    def gather(s, _):
        summed = dot_nn(adj_ref[s, :], hin_ref[...]) + dot_nn(edge_ref[s, :], halo_ref[...])
        mean_ref[s, :] = (summed * both(invd_ref[s, :])).astype(BF)
        return 0

    loop(adj_ref.shape[0], 2 * TILE, gather)


def second_kernel(adj_ref, edge_ref, halo_ref, hin_ref, w_ref, norm_ref, invd_ref, sel_ref,
                  mean_ref, xhat_ref, slope_ref, istd_ref, h_ref, send_ref):
    gather_mean(adj_ref, hin_ref, edge_ref, halo_ref, invd_ref, mean_ref)

    def apply(s, _):
        joined = dot_nn(hin_ref[s, :], w_ref[0]) + dot_nn(mean_ref[s, :], w_ref[1])
        keep_norm(s, norm_forward(joined, norm_ref, 1), xhat_ref, slope_ref, istd_ref, h_ref)
        return 0

    loop(adj_ref.shape[0], TILE, apply)
    send_ref[...] = dot_nn(sel_ref[...], h_ref[...]).astype(BF)


def split_count(x):
    high = jnp.floor(x * (1.0 / 256.0))
    return high, x - 256.0 * high


def head_kernel(adj_ref, edge_ref, halo_ref, hin_ref, w_ref, invd_ref, sel_ref, mask_ref,
                mean_ref, logit_ref, pred_ref, cross_ref, mine_ref, send_ref):
    gather_mean(adj_ref, hin_ref, edge_ref, halo_ref, invd_ref, mean_ref)

    def apply(s, _):
        logits = dot_nt(hin_ref[s, :], w_ref[0]) + dot_nt(mean_ref[s, :], w_ref[1])
        logit_ref[s, :] = logits
        pred_ref[s, :] = jnp.where(iota(logits.shape, 1) == LANE - 1, 1.0, logits).astype(BF)
        return 0

    loop(adj_ref.shape[0], TILE, apply)
    mine = dot_nn(sel_ref[...], pred_ref[...])
    lane = iota(mine.shape, 1)
    mine = jnp.where(lane < 64, mine, 0.0)
    mine_ref[...] = mine
    cross = dot_tn(edge_ref[...], pred_ref[...])
    cross_ref[...] = cross
    high, low = bf_parts(jnp.where(lane < 64, cross, 0.0), 2)
    count = jnp.sum(mask_ref[...].astype(F32), keepdims=True)
    count_high, count_low = split_count(count)
    col_high, col_low = split_count(cross[:, LANE - 1 : LANE])
    extra = jnp.where(lane == 64, count_high, 0.0) + jnp.where(lane == 65, count_low, 0.0)
    extra = extra + jnp.where(lane == 66, col_high, 0.0) + jnp.where(lane == 67, col_low, 0.0)
    send_ref[:, 0:LANE] = (mine + pltpu.roll(widen(low), 64, 1)).astype(BF)
    send_ref[:, LANE:] = (widen(high) + extra).astype(BF)


def spread_row(values, row):
    pick = (iota(values.shape, 0) == row).astype(F32).astype(BF)
    return dot_tn(values.astype(F32).astype(BF), pick)


def logit_grad_kernel(logit_ref, label_ref, mask_ref, row_ref, pred_ref, edge_ref, recv_ref, mine_ref, cross_ref,
                      sel_ref, w_ref, invd_ref,
                      grad_ref, gs_ref, send_ref, loss_ref, hp_ref, ret_ref, lab_ref, wgt_ref, *, classes, each):
    slots = mine_ref.shape[0]
    nodes = logit_ref.shape[0]
    first, second = widen(recv_ref[:, 0:LANE]), widen(recv_ref[:, LANE:])
    lane = iota((slots, LANE), 1)
    low_half = lane < 64
    halo_pred = jnp.where(low_half, first, 0.0)
    back_cross = jnp.where(low_half, second + pltpu.roll(first, 64, 1), 0.0)
    count = 256.0 * jnp.sum(jnp.where(lane == 64, second, 0.0), keepdims=True)
    count = (count + jnp.sum(jnp.where(lane == 65, second, 0.0), keepdims=True)) * (1.0 / each)
    col_back = 256.0 * second[:, 66:67] + second[:, 67:68]
    scale = 2.0 * PEN_WEIGHT / count
    inv_count = 1.0 / count
    hp_ref[...] = halo_pred.astype(BF)
    ret_ref[...] = (scale * (col_back * mine_ref[...] - back_cross)).astype(BF)
    pen = jnp.sum(cross_ref[:, LANE - 1 : LANE] * (halo_pred * halo_pred), keepdims=True)
    pen = pen - 2.0 * jnp.sum(halo_pred * cross_ref[...], keepdims=True)
    for r in range(nodes // LANE):
        lab_ref[r * LANE : (r + 1) * LANE, :] = spread_row(label_ref[...], r)
        wgt_ref[r * LANE : (r + 1) * LANE, :] = spread_row(mask_ref[...], r)

    def body(s, carry):
        ce_sum, pen_sum = carry
        logits = logit_ref[s, :]
        lane = iota(logits.shape, 1)
        real = lane < classes
        top = jnp.max(jnp.where(real, logits, -jnp.inf), 1, keepdims=True)
        shifted = jnp.where(real, jnp.exp(jnp.where(real, logits - top, 0.0)), 0.0)
        total = jnp.sum(shifted, 1, keepdims=True)
        hot = (lane.astype(F32) == lab_ref[s, :]).astype(F32)
        target = jnp.sum(logits * hot, 1, keepdims=True)
        weight = wgt_ref[s, :]
        ce_sum = ce_sum + jnp.sum(weight[:, 0:1] * (top + jnp.log(total) - target), keepdims=True)
        pred = jnp.where(real, widen(pred_ref[s, :]), 0.0)
        drawn = row_ref[s, :] * pred
        pen_sum = pen_sum + jnp.sum(drawn * pred, keepdims=True)
        own = drawn - dot_nn(edge_ref[s, :], hp_ref[...])
        back = dot_tn(sel_ref[:, s], ret_ref[...])
        grad = ((inv_count * weight) * (shifted * (1.0 / total) - hot) + scale * own + back).astype(BF)
        grad_ref[s, :] = grad
        gs_ref[s, :] = (dot_nn(grad, w_ref[1]) * both(invd_ref[s, :])).astype(BF)
        return ce_sum, pen_sum

    zero = jnp.zeros((1, 1), F32)
    ce_sum, pen_sum = loop(nodes, TILE, body, (zero, zero))
    row = iota((8, LANE), 0)
    loss_ref[...] = (jnp.where(row == 0, ce_sum, 0.0) + jnp.where(row == 1, pen + pen_sum, 0.0)
                     + jnp.where(row == 2, count, 0.0))
    send_ref[...] = dot_tn(edge_ref[...], gs_ref[...]).astype(BF)


BACK_TILE = 1024


def layer_back(adj_ref, gs_ref, grad_ref, w_ref, sel_ref, halo_ref, slope_ref, xhat_ref, istd_ref, norm_ref, layer, own_ref, gj_ref, back):
    nodes = adj_ref.shape[0]

    def pull(s, _):
        own_ref[s, :] = (dot_tn(adj_ref[:, s], gs_ref[...]) + back(grad_ref[s, :], w_ref[0])
                         + dot_tn(sel_ref[:, s], halo_ref[...]))
        return 0

    loop(nodes, BACK_TILE, pull)

    def body(s, carry):
        gain_sum, bias_sum = carry
        grad_pre = own_ref[s, :] * slope_ref[s, :]
        x_hat = xhat_ref[s, :]
        grad_x = grad_pre * norm_ref[2 * layer : 2 * layer + 1, :]
        mean_one = jnp.sum(grad_x, 1, keepdims=True) * (1.0 / HID)
        mean_two = jnp.sum(grad_x * x_hat, 1, keepdims=True) * (1.0 / HID)
        gj_ref[s, :] = (both(istd_ref[s, :]) * (grad_x - mean_one - x_hat * mean_two)).astype(BF)
        gain_sum = gain_sum + jnp.sum(grad_pre * x_hat, 0, keepdims=True)
        bias_sum = bias_sum + jnp.sum(grad_pre, 0, keepdims=True)
        return gain_sum, bias_sum

    zero = jnp.zeros((1, HID), F32)
    return loop(nodes, TILE, body, (zero, zero))


def second_back_kernel(adj_ref, gsin_ref, grad_ref, wout_ref, recv_ref, sel_ref, slope_ref, xhat_ref, istd_ref, norm_ref, w_ref,
                       invd_ref, edge_ref, h_two_ref, mean_head_ref, h_one_ref, mean_two_ref, at_ref,
                       gj_ref, gs_ref, send_ref, sums_ref, own_ref, full_ref, head_ref, *, each):
    gain_sum, bias_sum = layer_back(
        adj_ref, gsin_ref, grad_ref, wout_ref, sel_ref, recv_ref, slope_ref, xhat_ref, istd_ref, norm_ref, 1, own_ref, gj_ref, dot_nn
    )
    row = iota((8, HID), 0)
    sums_ref[...] = jnp.where(row == 2, gain_sum, 0.0) + jnp.where(row == 3, bias_sum, 0.0)

    def body(s, _):
        gs_ref[s, :] = (dot_nt(gj_ref[s, :], w_ref[1]) * both(invd_ref[s, :])).astype(BF)
        return 0

    loop(adj_ref.shape[0], TILE, body)
    parts = send_ref.shape[0]
    send_ref[:, 0:each, :] = dot_tn(edge_ref[...], gs_ref[...]).astype(BF).reshape(parts, each, HID)
    share = HID // FEATS
    half = pl.ds(pl.multiple_of(at_ref[0] * share // LANE * LANE, LANE), LANE)
    start = at_ref[0] * share % LANE
    head_ref[:, 0:LANE] = dot_tn(h_two_ref[:, half], grad_ref[...])
    head_ref[:, LANE:] = dot_tn(mean_head_ref[:, half], grad_ref[...])
    full_ref[0] = dot_tn(h_one_ref[:, half], gj_ref[...])
    full_ref[1] = dot_tn(mean_two_ref[:, half], gj_ref[...])
    for q in range(parts):
        if q * 16 < 2 * share:
            k, r = divmod(q * 16, share)
            send_ref[q, each : each + 16, :] = full_ref[k, pl.ds(pl.multiple_of(start + r, 16), 16), :].astype(BF)
            rows = head_ref[pl.ds(pl.multiple_of(start + q * 8, 8), 8), :]
            high, low = bf_parts(rows, 2)
            send_ref[q, each + 16 : each + 32, :] = jnp.concatenate([widen(high), widen(low)], 0).astype(BF)
        else:
            send_ref[q, each : each + 32, :] = jnp.zeros((32, HID), BF)


FEATS = 4


def first_back_kernel(adj_ref, gsin_ref, grad_ref, w_ref, recv_ref, sel_ref, slope_ref, xhat_ref, istd_ref, norm_ref,
                      ft_ref, mean_ref, loss_ref, sums_ref, at_ref,
                      send_ref, gj_ref, own_ref, full_ref, halo_ref, *, each):
    parts = recv_ref.shape[0]
    halo_ref[...] = recv_ref[:, 0:each, :].reshape(halo_ref.shape)
    gain_sum, bias_sum = layer_back(
        adj_ref, gsin_ref, grad_ref, w_ref, sel_ref, halo_ref, slope_ref, xhat_ref, istd_ref, norm_ref, 0, own_ref, gj_ref, dot_nt
    )
    row = iota((8, HID), 0)
    sums = sums_ref[...] + jnp.where(row == 0, gain_sum, 0.0) + jnp.where(row == 1, bias_sum, 0.0)
    full_ref[0] = dot_nn(ft_ref[...], gj_ref[...])
    full_ref[1] = dot_tn(mean_ref[...], gj_ref[...])
    at = rows_of(at_ref[0], FEAT_PAD)
    mid = jnp.zeros((16, HID), F32)
    out = jnp.zeros((16, HID), F32)
    for q in range(parts):
        mid = mid + widen(recv_ref[q, each : each + 16, :])
        out = out + widen(recv_ref[q, each + 16 : each + 32, :])
    out = out + pltpu.roll(out, 8, 0)
    mid_high, mid_low = bf_parts(mid, 2)
    out_high, out_low = bf_parts(out, 2)
    out = jnp.where(iota((16, HID), 0) < 8, widen(out_high), widen(out_low))
    lane = iota((8, HID), 1)
    blocks = []
    for k, norm_part in enumerate(bf_parts(sums, 2)):
        tail = jnp.zeros((8, HID), F32)
        for p, part in enumerate(bf_parts(jnp.broadcast_to(loss_ref[k : k + 1, 0:1], (8, HID)), 3)):
            tail = tail + jnp.where(lane == p, widen(part), 0.0)
        rows = full_ref[k, at, :]
        last = jnp.where(row == 0, rows[FEAT_PAD - 8 :, :], jnp.where(row == 3, tail, 0.0))
        blocks += [rows[0 : FEAT_PAD - 8, :], jnp.where(row >= 4, pltpu.roll(widen(norm_part), 4, 0), last)]
    message = jnp.concatenate([*blocks, widen(mid_high), widen(mid_low), out], 0).astype(BF)
    for q in range(parts):
        send_ref[q] = message


CHUNK_ROW = 2 * FEAT_PAD
MESSAGE_ROWS = CHUNK_ROW + 48


def total_kernel(recv_ref, grads_ref, norm_ref, loss_ref, mid_ref, out_ref, square_ref, *, width):
    parts = recv_ref.shape[0]
    grads = jnp.zeros((CHUNK_ROW, HID), F32)
    for q in range(parts):
        grads = grads + widen(recv_ref[q, 0:CHUNK_ROW, :])
    grads_ref[...] = grads
    tails = [grads[FEAT_PAD - 8 : FEAT_PAD, :], grads[2 * FEAT_PAD - 8 :, :]]
    row = iota((8, HID), 0)
    norms = jnp.where(row < 4, pltpu.roll(tails[0] + tails[1], 4, 0), 0.0)
    norm_ref[...] = norms
    sums = [jnp.sum(tail[3:4, :], keepdims=True) for tail in tails]
    loss_ref[...] = jnp.broadcast_to(sums[0] + PEN_WEIGHT * sums[1], loss_ref.shape)
    for q in range(mid_ref.shape[0] // 16):
        at = CHUNK_ROW
        mid_ref[q * 16 : q * 16 + 16, :] = widen(recv_ref[q, at : at + 16, :]) + widen(recv_ref[q, at + 16 : at + 32, :])
        rows = widen(recv_ref[q, at + 32 : at + 48, :])
        out_ref[q * 8 : q * 8 + 8, :] = rows[0:8, :] + rows[8:16, :]
    weight_row = (iota((CHUNK_ROW, HID), 0) & (FEAT_PAD - 1)) < width
    first = jnp.where(weight_row, grads, 0.0)
    square = jnp.sum(first * first, keepdims=True)
    square = square + jnp.sum(mid_ref[...] * mid_ref[...], keepdims=True)
    square = square + jnp.sum(out_ref[...] * out_ref[...], keepdims=True)
    row = iota((8, LANE), 0)
    square_ref[...] = jnp.where(row == 1, jnp.sum(norms * norms, keepdims=True), square)


def adam(param, grad, first, second):
    first_new = BETA_ONE * first + (1.0 - BETA_ONE) * grad
    second_new = BETA_TWO * second + (1.0 - BETA_TWO) * grad * grad
    first_hat = first_new / (1.0 - BETA_ONE**STEP)
    second_hat = second_new / (1.0 - BETA_TWO**STEP)
    fresh = param - RATE * (first_hat / (jnp.sqrt(second_hat) + ADAM_EPS) + DECAY * param)
    return fresh, first_new, second_new


def turn_kernel(grads_ref, gnorm_ref, gmid_ref, gout_ref, at_ref, in_ref, mid_ref, out_ref, norm_ref):
    width, classes, share = in_ref.shape[0], out_ref.shape[0], mid_ref.shape[1]
    whole = gnorm_ref[...]
    mine = jnp.zeros((8, share), F32)
    for f in range(HID // share):
        mine = mine + jnp.where(at_ref[0] == f, whole[:, f * share : (f + 1) * share], 0.0)
    for k in range(2):
        in_ref[:, k, :] = grads_ref[k * FEAT_PAD : k * FEAT_PAD + width, :]
        mid_ref[k] = gmid_ref[k * share : (k + 1) * share, :]
        out_ref[:, k, :] = jnp.transpose(gout_ref[:, k * LANE : (k + 1) * LANE])[0:classes, :]
        norm_ref[k] = mine[2 * k : 2 * k + 2, :]


def update_kernel(total_ref, sq0_ref, sq1_ref, sq2_ref, sq3_ref, loss_ref, *refs):
    grads, params, firsts, seconds = (refs[i : i + 4] for i in range(0, 16, 4))
    loss_out, count_out, gnorm_out, *results = refs[16:]
    loss_out[...] = total_ref[0:1, 0:1]
    count_out[...] = loss_ref[2:3, 0:1]
    square = (sq0_ref[0:1, 0:1] + sq1_ref[0:1, 0:1]) + (sq2_ref[0:1, 0:1] + sq3_ref[0:1, 0:1])
    grad_norm = jnp.sqrt(square + sq0_ref[1:2, 0:1])
    gnorm_out[...] = grad_norm
    factor = jnp.minimum(1.0, CLIP_LEVEL / (grad_norm + 1e-06)).reshape(1, 1, 1)
    for i in range(4):
        fresh, first, second = adam(params[i][...], grads[i][...] * factor, firsts[i][...], seconds[i][...])
        results[i][...], results[4 + i][...], results[8 + i][...] = fresh, first, second
        if i < 3:
            results[12 + i][...] = fresh.astype(BF)


def exchange(x, parts):
    return lax.all_to_all(x.reshape(parts, -1, x.shape[-1]), "dom", split_axis=0, concat_axis=0, tiled=True)


def native(w_in, w_mid, w_out, norm):
    return (jnp.transpose(w_in, (1, 0, 2)), w_mid, jnp.transpose(w_out, (2, 0, 1)), norm)


def restore(w_in, w_mid, w_out, *norm):
    return (jnp.transpose(w_in, (1, 0, 2)), w_mid, jnp.transpose(w_out, (1, 2, 0)), *norm)


def shards(
    features,
    inner_adj,
    bound_adj,
    keep_slots,
    send_index,
    labels,
    train_mask,
    w_in,
    w_mid,
    w_out,
    norm_params,
    m_in,
    m_mid,
    m_out,
    m_norms,
    v_in,
    v_mid,
    v_out,
    v_norms,
    *,
    parts,
    feats,
):
    nodes = features.shape[0]
    each = send_index.shape[2]
    halo = parts * each
    classes = w_out.shape[2]
    share = w_mid.shape[1]
    width = features.shape[1]
    run = functools.partial(call, mib=16 if parts <= 16 else 52)
    labels = labels.reshape(nodes // LANE, LANE)
    mask = train_mask.reshape(nodes // LANE, LANE)
    params = native(w_in, w_mid, w_out, norm_params)
    firsts = native(m_in, m_mid, m_out, m_norms)
    seconds = native(v_in, v_mid, v_out, v_norms)
    feat_at = lax.axis_index("feat").astype(jnp.int32).reshape(1)

    def bf(*dims):
        return shape(*dims, dtype=BF)

    def in_hbm(*arrays):
        return tuple(pltpu.with_memory_space_constraint(a, pltpu.HBM) for a in arrays)

    loads = in_hbm(send_index, features.T, *params)
    send, own, at = run(
        pack_kernel, [bf(parts, feats, each // 2, LANE), bf(pack_rows(nodes, share), HID), shape(1, dtype=jnp.int32)],
        *loads, feat_at, smem_in=(6,), smem_out=(2,), hbm_in=range(6),
        scratch=[pltpu.VMEM((halo, nodes), BF)] + [pltpu.VMEM(a.shape, a.dtype) for a in loads] + [pltpu.SemaphoreType.DMA((6,))],
    )
    recv = lax.all_to_all(
        send.reshape(parts * feats, each // 2, LANE), ("dom", "feat"), split_axis=0, concat_axis=0, tiled=True
    ).reshape(parts, feats, each // 2, LANE)
    chip = lax.ppermute(own, "feat", [(s, s ^ 2) for s in range(feats)])
    core = lax.ppermute(own, "feat", [(s, s ^ 1) for s in range(feats)])
    far = lax.ppermute(chip, "feat", [(s, s ^ 1) for s in range(feats)])
    loads = in_hbm(own, chip)
    results = [((feats * FEAT_PAD, nodes), BF), ((2, feats * FEAT_PAD, HID), BF), ((2, HID, HID), BF), ((2, LANE, HID), BF), ((8, HID), F32)]
    ft, win, wmid, wout, norms = run(
        side_kernel, [pltpu.HBM(*r) for r in results], *loads, core, far, at, hbm_in=range(2), smem_in=(4,), hbm_out=range(5),
        scratch=[pltpu.VMEM(*r) for r in results] + [pltpu.VMEM(a.shape, a.dtype) for a in loads]
        + [pltpu.SemaphoreType.DMA((2,)), pltpu.SemaphoreType.DMA((5,))],
    )
    loads = in_hbm(inner_adj, bound_adj, keep_slots, send_index, ft, win, norms)
    ring, bound_ring = (4, 8) if parts <= 16 else (2, 2)
    adj, edge, row_deg, sel, mean_one, xhat_one, slope_one, istd_one, h_one, inv_deg, send = run(
        functools.partial(first_kernel, width=width),
        [bf(nodes, nodes), bf(nodes, halo), shape(nodes, LANE), bf(halo, nodes), bf(nodes, LANE),
         shape(nodes, HID), shape(nodes, HID), shape(nodes, LANE), bf(nodes, HID), shape(nodes, LANE), bf(halo, HID)],
        *loads, recv, hbm_in=range(7),
        scratch=[pltpu.VMEM((halo, LANE), BF), pltpu.VMEM(keep_slots.shape, jnp.int32), pltpu.VMEM(send_index.shape, jnp.int32)]
        + [pltpu.VMEM(a.shape, a.dtype) for a in loads[4:]]
        + [pltpu.VMEM((ring, CONVERT_TILE, nodes), jnp.int32), pltpu.VMEM((bound_ring, CONVERT_TILE, halo), jnp.int32),
           pltpu.SemaphoreType.DMA((2, max(ring, bound_ring))), pltpu.SemaphoreType.DMA((5,))],
    )
    halo_one = exchange(send, parts).reshape(halo, HID)
    mean_two, xhat_two, slope_two, istd_two, h_two, send = run(
        second_kernel,
        [bf(nodes, HID), shape(nodes, HID), shape(nodes, HID), shape(nodes, LANE), bf(nodes, HID), bf(halo, HID)],
        adj, edge, halo_one, h_one, wmid, norms, inv_deg, sel,
    )
    halo_two = exchange(send, parts).reshape(halo, HID)
    mean_head, logits, pred, cross, mine, send = run(
        head_kernel,
        [bf(nodes, HID), shape(nodes, LANE), bf(nodes, LANE), shape(halo, LANE), shape(halo, LANE), bf(halo, HID)],
        adj, edge, halo_two, h_two, wout, inv_deg, sel, mask,
    )
    recv = exchange(send, parts).reshape(halo, HID)
    grad, grad_sum, send, losses = run(
        functools.partial(logit_grad_kernel, classes=classes, each=each),
        [bf(nodes, LANE), bf(nodes, HID), bf(halo, HID), shape(8, LANE)],
        logits, labels, mask, row_deg, pred, edge, recv, mine, cross, sel, wout, inv_deg,
        scratch=[pltpu.VMEM((halo, LANE), BF), pltpu.VMEM((halo, LANE), BF), pltpu.VMEM((nodes, LANE), F32), pltpu.VMEM((nodes, LANE), F32)],
    )
    recv = exchange(send, parts).reshape(halo, HID)
    joined_two, grad_sum, send, norm_sums = run(
        functools.partial(second_back_kernel, each=each),
        [bf(nodes, HID), bf(nodes, HID), bf(parts, each + 32, HID), shape(8, HID)],
        adj, grad_sum, grad, wout, recv, sel, slope_two, xhat_two, istd_two, norms, wmid, inv_deg, edge,
        h_two, mean_head, h_one, mean_two, at, smem_in=(17,),
        scratch=[pltpu.VMEM((nodes, HID), F32), pltpu.VMEM((2, LANE, HID), F32), pltpu.VMEM((LANE, HID), F32)],
    )
    recv = exchange(send, parts)
    send, = run(
        functools.partial(first_back_kernel, each=each), [bf(parts, MESSAGE_ROWS, HID)],
        adj, grad_sum, joined_two, wmid, recv, sel, slope_one, xhat_one, istd_one, norms, ft, mean_one, losses, norm_sums, at,
        smem_in=(14,),
        scratch=[pltpu.VMEM((nodes, HID), BF), pltpu.VMEM((nodes, HID), F32), pltpu.VMEM((2, feats * FEAT_PAD, HID), F32),
                 pltpu.VMEM((halo, HID), BF)],
    )
    recv = exchange(send, parts)
    grads, gnorm, total, gmid, gout, square = run(
        functools.partial(total_kernel, width=width),
        [shape(CHUNK_ROW, HID), shape(8, HID), shape(8, LANE), shape(2 * share, HID), shape(share, HID), shape(8, LANE)], recv,
    )
    squares = [square]
    for k in range(1, feats):
        squares.append(lax.ppermute(square, "feat", [(s, s ^ k) for s in range(feats)]))
    outs = [shape(1, 1)] * 3 + [shape(*p.shape) for p in params] * 3 + [bf(*p.shape) for p in params[:3]]
    grads = run(turn_kernel, [shape(*p.shape) for p in params], grads, gnorm, gmid, gout, at, smem_in=(4,))
    result = run(update_kernel, outs, total, *squares, losses, *grads, *params, *firsts, *seconds)
    return (
        tuple(r.reshape(()) for r in result[:3])
        + restore(*result[3:7]) + restore(*result[7:11]) + restore(*result[11:15]) + restore(*result[15:])
    )


def solution(mesh):
    weight = P(None, "feat", None)
    norm = P(None, None, "feat")
    placed = (
        P("dom", "feat"), P("dom", None), P("dom", None), P("dom", None), P("dom", None, None), P("dom"), P("dom"),
    ) + (weight, weight, weight, norm) * 3
    return jax.shard_map(
        functools.partial(shards, parts=mesh.shape["dom"], feats=mesh.shape["feat"]),
        mesh=mesh,
        in_specs=placed,
        out_specs=(P(), P(), P()) + (weight, weight, weight, norm) * 3 + (weight,) * 3,
        check_vma=False,
    )
```

```python
import functools
import math

import jax
import jax.numpy as jnp
from jax import lax
from jax.experimental import pallas as pl
from jax.experimental.pallas import tpu as pltpu
from jax.sharding import PartitionSpec as P

HID = 256
STEP = 5

NORM_EPS = 1e-05
PEN_WEIGHT = 0.001
CLIP_LEVEL = 0.01
RATE = 0.05
BETA_ONE = 0.5
BETA_TWO = 0.5
ADAM_EPS = 1e-08
DECAY = 0.01

BF = jnp.bfloat16
F32 = jnp.float32
LANE = 128
FEAT_PAD = 32
MIB = 1 << 20

VMEM = pl.BlockSpec(memory_space=pltpu.VMEM)
SMEM = pl.BlockSpec(memory_space=pltpu.SMEM)
ANY = pl.BlockSpec(memory_space=pl.ANY)
HBM = pl.BlockSpec(memory_space=pltpu.HBM)


def dot_nn(a, b):
    return jnp.dot(a, b, preferred_element_type=F32)


def dot_tn(a, b):
    return lax.dot_general(a, b, (((0,), (0,)), ((), ())), preferred_element_type=F32)


def dot_nt(a, b):
    return lax.dot_general(a, b, (((1,), (1,)), ((), ())), preferred_element_type=F32)


def iota(shape, axis):
    return lax.broadcasted_iota(jnp.int32, shape, axis)


def place(rows, cols, shift, turned=False):
    dims = (cols, rows) if turned else (rows, cols)
    return (iota(dims, int(turned)) + shift == iota(dims, int(not turned))).astype(F32).astype(BF)


def widen(x):
    return x.astype(F32)


def bf_parts(x, count):
    parts = []
    for _ in range(count):
        part = x.astype(BF)
        parts.append(part)
        x = x - widen(part)
    return parts


def both(x):
    return jnp.concatenate([x, x], 1)


def rows_of(i, tile):
    return pl.ds(pl.multiple_of(i * tile, tile), tile)


def call(kernel, outs, *args, mib=24, flops=0, smem_in=(), any_in=(), hbm_in=(), smem_out=(), hbm_out=(), scratch=()):
    size = sum(math.prod(a.shape) * a.dtype.itemsize for a in (*args, *outs))
    return pl.pallas_call(
        kernel,
        out_shape=outs,
        in_specs=[SMEM if i in smem_in else ANY if i in any_in else HBM if i in hbm_in else VMEM for i in range(len(args))],
        out_specs=[SMEM if i in smem_out else HBM if i in hbm_out else VMEM for i in range(len(outs))],
        scratch_shapes=list(scratch),
        cost_estimate=pl.CostEstimate(flops=flops, bytes_accessed=size // 4, transcendentals=0),
        compiler_params=pltpu.CompilerParams(vmem_limit_bytes=mib * MIB),
    )(*args)


def shape(*dims, dtype=F32):
    return jax.ShapeDtypeStruct(dims, dtype)


def select(idx_ref, sel_ref):
    nodes = sel_ref.shape[1]
    parts, each = idx_ref.shape[1:]
    eye = iota((each, each), 0) == iota((each, each), 1)
    for p in range(parts):
        column = jnp.sum(jnp.where(eye, idx_ref[0, p : p + 1, :].astype(F32), 0.0), 1, keepdims=True)
        hot = iota((each, nodes), 1) == column.astype(jnp.int32)
        sel_ref[p * each : (p + 1) * each, :] = hot.astype(F32).astype(BF)


def pack_kernel(idx_hbm, feat_hbm, w_in_hbm, w_mid_hbm, w_out_hbm, norm_hbm, at_ref, send_ref, pack_ref, at_out,
                sel_ref, idx_ref, feat_ref, w_in_ref, w_mid_ref, w_out_ref, norm_ref, sems):
    sources = (idx_hbm, feat_hbm, w_mid_hbm, w_in_hbm, w_out_hbm, norm_hbm)
    targets = (idx_ref, feat_ref, w_mid_ref, w_in_ref, w_out_ref, norm_ref)
    copies = [pltpu.make_async_copy(src, dst, sems.at[i]) for i, (src, dst) in enumerate(zip(sources, targets))]
    for copy in copies:
        copy.start()
    at_out[0] = at_ref[0]
    copies[0].wait()
    select(idx_ref, sel_ref)
    wait_all(copies[1:])
    nodes = feat_ref.shape[1]
    width, share = feat_ref.shape[0], w_mid_ref.shape[1]
    classes = w_out_ref.shape[0]
    rows = dot_nn(place(FEAT_PAD, width, 0), feat_ref[...].astype(BF))
    parts, copies, half, _ = send_ref.shape
    sent = dot_nt(sel_ref[...], rows.astype(BF)).astype(BF)
    left = dot_nn(sent, place(FEAT_PAD, LANE, 0)).reshape(parts, 2, half, LANE)[:, 0]
    right = dot_nn(sent, place(FEAT_PAD, LANE, LANE // 2)).reshape(parts, 2, half, LANE)[:, 1]
    for f in range(copies):
        send_ref[:, f] = (left + right).astype(BF)
    ones = iota((FEAT_PAD, nodes), 0) == FEAT_PAD - 1
    blocks = [jnp.zeros((FEAT_PAD, HID), F32) for _ in range(3)]
    for layer in range(2):
        for p, part in enumerate(bf_parts(norm_ref[layer], 3)):
            part = dot_nn(part, place(share, HID, 0)).astype(BF)
            blocks[p] = blocks[p] + dot_nn(place(2, FEAT_PAD, NORM_AT + 2 * layer, turned=True), part)
    blocks.append(jnp.zeros((FEAT_PAD, nodes - 3 * HID), F32))
    rows = (jnp.where(ones, 1.0, rows) + jnp.concatenate(blocks, 1)).astype(BF)
    at = 0
    for b in range(nodes // HID):
        pack_ref[at : at + FEAT_PAD, :] = rows[:, b * HID : (b + 1) * HID]
        at += FEAT_PAD
    for k in range(2):
        pack_ref[at : at + share, :] = w_mid_ref[k].astype(BF)
        at += share
    for k in range(2):
        pack_ref[at : at + FEAT_PAD, :] = dot_nn(place(FEAT_PAD, width, 0), w_in_ref[:, k, :].astype(BF)).astype(BF)
        at += FEAT_PAD
    turned = jnp.zeros((2 * CLASS_HALF, LANE), F32)
    for k in range(2):
        grown = dot_nn(place(classes, 2 * CLASS_HALF, 0, turned=True), w_out_ref[:, k, :].astype(BF)).astype(BF)
        turned = turned + dot_nn(grown, place(share, LANE, k * share))
    turned = turned.astype(BF)
    for half in range(2):
        pack_ref[at : at + CLASS_HALF, half * LANE : (half + 1) * LANE] = turned[half * CLASS_HALF : (half + 1) * CLASS_HALF, :]


NORM_AT = FEAT_PAD - 6
CLASS_HALF = 32


def pack_rows(nodes, share):
    return nodes // HID * FEAT_PAD + 2 * share + 2 * FEAT_PAD + CLASS_HALF


def spread(packed_refs, at_ref, ft_ref):
    row = iota((FEAT_PAD, HID), 0)
    keep = (row < NORM_AT) | (row == FEAT_PAD - 1)
    for k, packed_ref in enumerate(packed_refs):
        at = rows_of(at_ref[0] ^ k, FEAT_PAD)
        for b in range(ft_ref.shape[1] // HID):
            rows = widen(packed_ref[b * FEAT_PAD : (b + 1) * FEAT_PAD, :])
            ft_ref[at, b * HID : (b + 1) * HID] = jnp.where(keep, rows, 0.0).astype(BF)


def join_halo(recv_ref, halo_ref, width):
    parts, feats, half, _ = recv_ref.shape
    lane = iota((parts * half, LANE), 1)
    sides = [jnp.where(lane == LANE - 1, 1.0, 0.0)] * 2
    for f in range(feats):
        rows = widen(recv_ref[:, f]).reshape(parts * half, LANE)
        for g in range(2):
            at = g * (LANE // 2)
            side = jnp.where((lane >= at) & (lane < at + width), rows, 0.0)
            shift = (f * FEAT_PAD - at) % LANE
            sides[g] = sides[g] + (pltpu.roll(side, shift, 1) if shift else side)
    sides = [side.astype(BF).reshape(parts, half, LANE) for side in sides]
    halo_ref[...] = jnp.stack(sides, 1).reshape(halo_ref.shape)


def unpack(packed_refs, at_ref, win_ref, wmid_ref, wout_ref, norm_ref):
    share = HID // len(packed_refs)
    norms = jnp.zeros((8, HID), F32)
    heads = [jnp.zeros((2 * CLASS_HALF, HID), F32) for _ in range(2)]
    for offset, packed_ref in enumerate(packed_refs):
        f = at_ref[0] ^ offset
        at = packed_ref.shape[0] - 2 * share - 2 * FEAT_PAD - CLASS_HALF
        for k in range(2):
            wmid_ref[k, rows_of(f, share), :] = packed_ref[at : at + share, :]
            at += share
        for k in range(2):
            win_ref[k, rows_of(f, FEAT_PAD), :] = packed_ref[at : at + FEAT_PAD, :]
            at += FEAT_PAD
        halves = [widen(packed_ref[at : at + CLASS_HALF, h * LANE : (h + 1) * LANE]) for h in range(2)]
        head = both(jnp.concatenate(halves, 0))
        lane = iota(head.shape, 1)
        heads[0] = heads[0] + pltpu.roll(jnp.where(lane < share, head, 0.0), f * share, 1)
        heads[1] = heads[1] + pltpu.roll(jnp.where((lane >= LANE + share) & (lane < LANE + 2 * share), head, 0.0),
                                         (f * share + LANE - share) & (HID - 1), 1)
        part = jnp.zeros((8, HID), F32)
        for p in range(3):
            part = part + widen(packed_ref[p * FEAT_PAD + 16 : (p + 1) * FEAT_PAD, :])[8:16, :]
        part = jnp.where((iota((8, HID), 0) >= NORM_AT - 24) & (iota((8, HID), 0) < NORM_AT - 20), part, 0.0)
        norms = norms + pltpu.roll(part, f * share, 1)
    for k in range(2):
        wout_ref[k, 0 : 2 * CLASS_HALF, :] = heads[k].astype(BF)
        wout_ref[k, 2 * CLASS_HALF :, :] = jnp.zeros((LANE - 2 * CLASS_HALF, HID), BF)
    norm_ref[...] = pltpu.roll(norms, 8 - (NORM_AT - 24), 0)


TILE = 1024


def loop(count, tile, body, carry=0):
    return lax.fori_loop(0, count // tile, lambda i, c: body(rows_of(i, tile), c), carry)


def norm_forward(joined, norm_ref, layer):
    center = jnp.sum(joined, 1, keepdims=True) * (1.0 / HID)
    spread = jnp.sum(joined * joined, 1, keepdims=True) * (1.0 / HID) - center * center
    inv_std = lax.rsqrt(spread + NORM_EPS)
    x_hat = (joined - center) * inv_std
    normed = x_hat * norm_ref[2 * layer : 2 * layer + 1, :] + norm_ref[2 * layer + 1 : 2 * layer + 2, :]
    gate = 0.5 * jnp.tanh(0.5 * normed) + 0.5
    hidden = normed * gate
    return inv_std, x_hat, hidden, gate + hidden * (1.0 - gate)


def keep_norm(s, parts, xhat_ref, slope_ref, istd_ref, h_ref):
    inv_std, x_hat, hidden, slope = parts
    xhat_ref[s, :] = x_hat
    slope_ref[s, :] = slope
    istd_ref[s, :] = jnp.broadcast_to(inv_std, (x_hat.shape[0], LANE))
    h_ref[s, :] = hidden.astype(BF)


GATHER_ROWS = 512


def start_all(copies):
    for copy in copies:
        copy.start()
    return copies


def wait_all(copies):
    for copy in copies:
        copy.wait()


def side_kernel(own_hbm, chip_hbm, core_ref, far_ref, at_ref,
                ft_out, win_out, wmid_out, wout_out, norm_out,
                ft_ref, win_ref, wmid_ref, wout_ref, norm_ref, own_ref, chip_ref, in_sems, out_sems):
    packed_refs = (own_ref, core_ref, chip_ref, far_ref)
    loads = ((own_hbm, own_ref), (chip_hbm, chip_ref))
    wait_all(start_all([pltpu.make_async_copy(src, dst, in_sems.at[i]) for i, (src, dst) in enumerate(loads)]))
    pairs = ((ft_ref, ft_out), (win_ref, win_out), (wmid_ref, wmid_out), (wout_ref, wout_out), (norm_ref, norm_out))
    stores = [pltpu.make_async_copy(src, dst, out_sems.at[i]) for i, (src, dst) in enumerate(pairs)]
    spread(packed_refs, at_ref, ft_ref)
    stores[0].start()
    unpack(packed_refs, at_ref, win_ref, wmid_ref, wout_ref, norm_ref)
    start_all(stores[1:])
    wait_all(stores)


def first_kernel(adj_hbm, bound_hbm, keep_hbm, idx_hbm, ft_hbm, win_hbm, norm_hbm, recv_ref,
                 adj_ref, edge_ref, row_ref, sel_ref, mean_ref, xhat_ref, slope_ref, istd_ref, h_ref, invd_ref, send_ref,
                 halo_ref, keep_ref, idx_ref, ft_ref, win_ref, norm_ref, adj_buf, bound_buf, ring_sems, sems, *, width):
    nodes = edge_ref.shape[0]
    ring, tile = adj_buf.shape[0:2]

    def fetch(step, slot):
        return pltpu.make_async_copy(adj_hbm.at[rows_of(step, tile)], adj_buf.at[slot], ring_sems.at[0, slot])

    def fetch_bound(step, slot):
        return pltpu.make_async_copy(bound_hbm.at[rows_of(step, tile)], bound_buf.at[slot], ring_sems.at[1, slot])

    sources, targets = (keep_hbm, idx_hbm, ft_hbm, win_hbm, norm_hbm), (keep_ref, idx_ref, ft_ref, win_ref, norm_ref)
    small = [pltpu.make_async_copy(src, dst, sems.at[i]) for i, (src, dst) in enumerate(zip(sources, targets))]
    start_all(small[0:2])
    for step in range(bound_buf.shape[0]):
        fetch_bound(step, step).start()
    start_all(small[2:])
    for step in range(ring):
        fetch(step, step).start()
    join_halo(recv_ref, halo_ref, width)
    wait_all(small[0:2])
    select(idx_ref, sel_ref)

    def boundary(step, _):
        slot = lax.rem(step, bound_buf.shape[0])
        s = rows_of(step, tile)
        fetch_bound(step, slot).wait()
        edge_ref[s, :] = (bound_buf[slot] * keep_ref[...]).astype(F32).astype(BF)

        @pl.when(step + bound_buf.shape[0] < nodes // tile)
        def _():
            fetch_bound(step + bound_buf.shape[0], slot).start()

        return 0

    lax.fori_loop(0, nodes // tile, boundary, 0)
    wait_all(small[2:])

    def gather(step, _):
        for part in range(GATHER_ROWS // tile):
            chunk = step * (GATHER_ROWS // tile) + part
            slot = lax.rem(chunk, ring)
            fetch(chunk, slot).wait()
            adj_ref[rows_of(chunk, tile), :] = adj_buf[slot].astype(F32).astype(BF)

            @pl.when(chunk + ring < nodes // tile)
            def _():
                fetch(chunk + ring, slot).start()

        s = rows_of(step, GATHER_ROWS)
        far = dot_nn(edge_ref[s, :], halo_ref[...])
        row_ref[s, :] = jnp.broadcast_to(far[:, LANE - 1 : LANE], far.shape)
        summed = dot_nt(adj_ref[s, :], ft_ref[...]) + far
        inv_deg = 1.0 / jnp.maximum(summed[:, LANE - 1 : LANE], 1.0)
        invd_ref[s, :] = jnp.broadcast_to(inv_deg, summed.shape)
        mean_ref[s, :] = (summed * inv_deg).astype(BF)
        return 0

    lax.fori_loop(0, nodes // GATHER_ROWS, gather, 0)

    def apply(s, _):
        joined = dot_tn(ft_ref[:, s], win_ref[0]) + dot_nn(mean_ref[s, :], win_ref[1])
        keep_norm(s, norm_forward(joined, norm_ref, 0), xhat_ref, slope_ref, istd_ref, h_ref)
        return 0

    loop(nodes, TILE, apply)
    send_ref[...] = dot_nn(sel_ref[...], h_ref[...]).astype(BF)


def gather_mean(adj_ref, hin_ref, edge_ref, halo_ref, invd_ref, mean_ref):
    def gather(s, _):
        summed = dot_nn(adj_ref[s, :], hin_ref[...]) + dot_nn(edge_ref[s, :], halo_ref[...])
        mean_ref[s, :] = (summed * both(invd_ref[s, :])).astype(BF)
        return 0

    loop(adj_ref.shape[0], 2 * TILE, gather)


def second_kernel(adj_ref, edge_ref, halo_ref, hin_ref, w_ref, norm_ref, invd_ref, sel_ref,
                  mean_ref, xhat_ref, slope_ref, istd_ref, h_ref, send_ref):
    gather_mean(adj_ref, hin_ref, edge_ref, halo_ref, invd_ref, mean_ref)

    def apply(s, _):
        joined = dot_nn(hin_ref[s, :], w_ref[0]) + dot_nn(mean_ref[s, :], w_ref[1])
        keep_norm(s, norm_forward(joined, norm_ref, 1), xhat_ref, slope_ref, istd_ref, h_ref)
        return 0

    loop(adj_ref.shape[0], TILE, apply)
    send_ref[...] = dot_nn(sel_ref[...], h_ref[...]).astype(BF)


def split_count(x):
    high = jnp.floor(x * (1.0 / 256.0))
    return high, x - 256.0 * high


def head_kernel(adj_ref, edge_ref, halo_ref, hin_ref, w_ref, invd_ref, sel_ref, mask_ref,
                mean_ref, logit_ref, pred_ref, cross_ref, mine_ref, send_ref):
    gather_mean(adj_ref, hin_ref, edge_ref, halo_ref, invd_ref, mean_ref)

    def apply(s, _):
        logits = dot_nt(hin_ref[s, :], w_ref[0]) + dot_nt(mean_ref[s, :], w_ref[1])
        logit_ref[s, :] = logits
        pred_ref[s, :] = jnp.where(iota(logits.shape, 1) == LANE - 1, 1.0, logits).astype(BF)
        return 0

    loop(adj_ref.shape[0], TILE, apply)
    mine = dot_nn(sel_ref[...], pred_ref[...])
    lane = iota(mine.shape, 1)
    mine = jnp.where(lane < 64, mine, 0.0)
    mine_ref[...] = mine
    cross = dot_tn(edge_ref[...], pred_ref[...])
    cross_ref[...] = cross
    high, low = bf_parts(jnp.where(lane < 64, cross, 0.0), 2)
    count = jnp.sum(mask_ref[...].astype(F32), keepdims=True)
    count_high, count_low = split_count(count)
    col_high, col_low = split_count(cross[:, LANE - 1 : LANE])
    extra = jnp.where(lane == 64, count_high, 0.0) + jnp.where(lane == 65, count_low, 0.0)
    extra = extra + jnp.where(lane == 66, col_high, 0.0) + jnp.where(lane == 67, col_low, 0.0)
    send_ref[:, 0:LANE] = (mine + pltpu.roll(widen(low), 64, 1)).astype(BF)
    send_ref[:, LANE:] = (widen(high) + extra).astype(BF)


def spread_row(values, row):
    pick = (iota(values.shape, 0) == row).astype(F32).astype(BF)
    return dot_tn(values.astype(F32).astype(BF), pick)


def logit_grad_kernel(logit_ref, label_ref, mask_ref, row_ref, pred_ref, edge_ref, recv_ref, mine_ref, cross_ref,
                      sel_ref, w_ref, invd_ref,
                      grad_ref, gs_ref, send_ref, loss_ref, hp_ref, ret_ref, lab_ref, wgt_ref, *, classes, each):
    slots = mine_ref.shape[0]
    nodes = logit_ref.shape[0]
    first, second = widen(recv_ref[:, 0:LANE]), widen(recv_ref[:, LANE:])
    lane = iota((slots, LANE), 1)
    low_half = lane < 64
    halo_pred = jnp.where(low_half, first, 0.0)
    back_cross = jnp.where(low_half, second + pltpu.roll(first, 64, 1), 0.0)
    count = 256.0 * jnp.sum(jnp.where(lane == 64, second, 0.0), keepdims=True)
    count = (count + jnp.sum(jnp.where(lane == 65, second, 0.0), keepdims=True)) * (1.0 / each)
    col_back = 256.0 * second[:, 66:67] + second[:, 67:68]
    scale = 2.0 * PEN_WEIGHT / count
    inv_count = 1.0 / count
    hp_ref[...] = halo_pred.astype(BF)
    ret_ref[...] = (scale * (col_back * mine_ref[...] - back_cross)).astype(BF)
    pen = jnp.sum(cross_ref[:, LANE - 1 : LANE] * (halo_pred * halo_pred), keepdims=True)
    pen = pen - 2.0 * jnp.sum(halo_pred * cross_ref[...], keepdims=True)
    for r in range(nodes // LANE):
        lab_ref[r * LANE : (r + 1) * LANE, :] = spread_row(label_ref[...], r)
        wgt_ref[r * LANE : (r + 1) * LANE, :] = spread_row(mask_ref[...], r)

    def body(s, carry):
        ce_sum, pen_sum = carry
        logits = logit_ref[s, :]
        lane = iota(logits.shape, 1)
        real = lane < classes
        top = jnp.max(jnp.where(real, logits, -jnp.inf), 1, keepdims=True)
        shifted = jnp.where(real, jnp.exp(jnp.where(real, logits - top, 0.0)), 0.0)
        total = jnp.sum(shifted, 1, keepdims=True)
        hot = (lane.astype(F32) == lab_ref[s, :]).astype(F32)
        target = jnp.sum(logits * hot, 1, keepdims=True)
        weight = wgt_ref[s, :]
        ce_sum = ce_sum + jnp.sum(weight[:, 0:1] * (top + jnp.log(total) - target), keepdims=True)
        pred = jnp.where(real, widen(pred_ref[s, :]), 0.0)
        drawn = row_ref[s, :] * pred
        pen_sum = pen_sum + jnp.sum(drawn * pred, keepdims=True)
        own = drawn - dot_nn(edge_ref[s, :], hp_ref[...])
        back = dot_tn(sel_ref[:, s], ret_ref[...])
        grad = ((inv_count * weight) * (shifted * (1.0 / total) - hot) + scale * own + back).astype(BF)
        grad_ref[s, :] = grad
        gs_ref[s, :] = (dot_nn(grad, w_ref[1]) * both(invd_ref[s, :])).astype(BF)
        return ce_sum, pen_sum

    zero = jnp.zeros((1, 1), F32)
    ce_sum, pen_sum = loop(nodes, TILE, body, (zero, zero))
    row = iota((8, LANE), 0)
    loss_ref[...] = (jnp.where(row == 0, ce_sum, 0.0) + jnp.where(row == 1, pen + pen_sum, 0.0)
                     + jnp.where(row == 2, count, 0.0))
    send_ref[...] = dot_tn(edge_ref[...], gs_ref[...]).astype(BF)


BACK_TILE = 1024


def layer_back(adj_ref, gs_ref, grad_ref, w_ref, sel_ref, halo_ref, slope_ref, xhat_ref, istd_ref, norm_ref, layer, own_ref, gj_ref, back):
    nodes = adj_ref.shape[0]

    def pull(s, _):
        own_ref[s, :] = (dot_tn(adj_ref[:, s], gs_ref[...]) + back(grad_ref[s, :], w_ref[0])
                         + dot_tn(sel_ref[:, s], halo_ref[...]))
        return 0

    loop(nodes, BACK_TILE, pull)

    def body(s, carry):
        gain_sum, bias_sum = carry
        grad_pre = own_ref[s, :] * slope_ref[s, :]
        x_hat = xhat_ref[s, :]
        grad_x = grad_pre * norm_ref[2 * layer : 2 * layer + 1, :]
        mean_one = jnp.sum(grad_x, 1, keepdims=True) * (1.0 / HID)
        mean_two = jnp.sum(grad_x * x_hat, 1, keepdims=True) * (1.0 / HID)
        gj_ref[s, :] = (both(istd_ref[s, :]) * (grad_x - mean_one - x_hat * mean_two)).astype(BF)
        gain_sum = gain_sum + jnp.sum(grad_pre * x_hat, 0, keepdims=True)
        bias_sum = bias_sum + jnp.sum(grad_pre, 0, keepdims=True)
        return gain_sum, bias_sum

    zero = jnp.zeros((1, HID), F32)
    return loop(nodes, TILE, body, (zero, zero))


def second_back_kernel(adj_ref, gsin_ref, grad_ref, wout_ref, recv_ref, sel_ref, slope_ref, xhat_ref, istd_ref, norm_ref, w_ref,
                       invd_ref, edge_ref, h_two_ref, mean_head_ref, h_one_ref, mean_two_ref, at_ref,
                       gj_ref, gs_ref, send_ref, sums_ref, own_ref, full_ref, head_ref, *, each):
    gain_sum, bias_sum = layer_back(
        adj_ref, gsin_ref, grad_ref, wout_ref, sel_ref, recv_ref, slope_ref, xhat_ref, istd_ref, norm_ref, 1, own_ref, gj_ref, dot_nn
    )
    row = iota((8, HID), 0)
    sums_ref[...] = jnp.where(row == 2, gain_sum, 0.0) + jnp.where(row == 3, bias_sum, 0.0)

    def body(s, _):
        gs_ref[s, :] = (dot_nt(gj_ref[s, :], w_ref[1]) * both(invd_ref[s, :])).astype(BF)
        return 0

    loop(adj_ref.shape[0], TILE, body)
    parts = send_ref.shape[0]
    send_ref[:, 0:each, :] = dot_tn(edge_ref[...], gs_ref[...]).astype(BF).reshape(parts, each, HID)
    share = HID // FEATS
    half = pl.ds(pl.multiple_of(at_ref[0] * share // LANE * LANE, LANE), LANE)
    start = at_ref[0] * share % LANE
    head_ref[:, 0:LANE] = dot_tn(h_two_ref[:, half], grad_ref[...])
    head_ref[:, LANE:] = dot_tn(mean_head_ref[:, half], grad_ref[...])
    full_ref[0] = dot_tn(h_one_ref[:, half], gj_ref[...])
    full_ref[1] = dot_tn(mean_two_ref[:, half], gj_ref[...])
    for q in range(parts):
        if q * 16 < 2 * share:
            k, r = divmod(q * 16, share)
            send_ref[q, each : each + 16, :] = full_ref[k, pl.ds(pl.multiple_of(start + r, 16), 16), :].astype(BF)
            rows = head_ref[pl.ds(pl.multiple_of(start + q * 8, 8), 8), :]
            high, low = bf_parts(rows, 2)
            send_ref[q, each + 16 : each + 32, :] = jnp.concatenate([widen(high), widen(low)], 0).astype(BF)
        else:
            send_ref[q, each : each + 32, :] = jnp.zeros((32, HID), BF)


FEATS = 4


def first_back_kernel(adj_ref, gsin_ref, grad_ref, w_ref, recv_ref, sel_ref, slope_ref, xhat_ref, istd_ref, norm_ref,
                      ft_ref, mean_ref, loss_ref, sums_ref, at_ref,
                      send_ref, gj_ref, own_ref, full_ref, halo_ref, *, each):
    parts = recv_ref.shape[0]
    halo_ref[...] = recv_ref[:, 0:each, :].reshape(halo_ref.shape)
    gain_sum, bias_sum = layer_back(
        adj_ref, gsin_ref, grad_ref, w_ref, sel_ref, halo_ref, slope_ref, xhat_ref, istd_ref, norm_ref, 0, own_ref, gj_ref, dot_nt
    )
    row = iota((8, HID), 0)
    sums = sums_ref[...] + jnp.where(row == 0, gain_sum, 0.0) + jnp.where(row == 1, bias_sum, 0.0)
    full_ref[0] = dot_nn(ft_ref[...], gj_ref[...])
    full_ref[1] = dot_tn(mean_ref[...], gj_ref[...])
    at = rows_of(at_ref[0], FEAT_PAD)
    mid = jnp.zeros((16, HID), F32)
    out = jnp.zeros((16, HID), F32)
    for q in range(parts):
        mid = mid + widen(recv_ref[q, each : each + 16, :])
        out = out + widen(recv_ref[q, each + 16 : each + 32, :])
    out = out + pltpu.roll(out, 8, 0)
    mid_high, mid_low = bf_parts(mid, 2)
    out_high, out_low = bf_parts(out, 2)
    out = jnp.where(iota((16, HID), 0) < 8, widen(out_high), widen(out_low))
    lane = iota((8, HID), 1)
    blocks = []
    for k, norm_part in enumerate(bf_parts(sums, 2)):
        tail = jnp.zeros((8, HID), F32)
        for p, part in enumerate(bf_parts(jnp.broadcast_to(loss_ref[k : k + 1, 0:1], (8, HID)), 3)):
            tail = tail + jnp.where(lane == p, widen(part), 0.0)
        rows = full_ref[k, at, :]
        last = jnp.where(row == 0, rows[FEAT_PAD - 8 :, :], jnp.where(row == 3, tail, 0.0))
        blocks += [rows[0 : FEAT_PAD - 8, :], jnp.where(row >= 4, pltpu.roll(widen(norm_part), 4, 0), last)]
    message = jnp.concatenate([*blocks, widen(mid_high), widen(mid_low), out], 0).astype(BF)
    for q in range(parts):
        send_ref[q] = message


CHUNK_ROW = 2 * FEAT_PAD
MESSAGE_ROWS = CHUNK_ROW + 48


def total_kernel(recv_ref, grads_ref, norm_ref, loss_ref, mid_ref, out_ref, square_ref, *, width):
    parts = recv_ref.shape[0]
    grads = jnp.zeros((CHUNK_ROW, HID), F32)
    for q in range(parts):
        grads = grads + widen(recv_ref[q, 0:CHUNK_ROW, :])
    grads_ref[...] = grads
    tails = [grads[FEAT_PAD - 8 : FEAT_PAD, :], grads[2 * FEAT_PAD - 8 :, :]]
    row = iota((8, HID), 0)
    norms = jnp.where(row < 4, pltpu.roll(tails[0] + tails[1], 4, 0), 0.0)
    norm_ref[...] = norms
    sums = [jnp.sum(tail[3:4, :], keepdims=True) for tail in tails]
    loss_ref[...] = jnp.broadcast_to(sums[0] + PEN_WEIGHT * sums[1], loss_ref.shape)
    for q in range(mid_ref.shape[0] // 16):
        at = CHUNK_ROW
        mid_ref[q * 16 : q * 16 + 16, :] = widen(recv_ref[q, at : at + 16, :]) + widen(recv_ref[q, at + 16 : at + 32, :])
        rows = widen(recv_ref[q, at + 32 : at + 48, :])
        out_ref[q * 8 : q * 8 + 8, :] = rows[0:8, :] + rows[8:16, :]
    weight_row = (iota((CHUNK_ROW, HID), 0) & (FEAT_PAD - 1)) < width
    first = jnp.where(weight_row, grads, 0.0)
    square = jnp.sum(first * first, keepdims=True)
    square = square + jnp.sum(mid_ref[...] * mid_ref[...], keepdims=True)
    square = square + jnp.sum(out_ref[...] * out_ref[...], keepdims=True)
    row = iota((8, LANE), 0)
    square_ref[...] = jnp.where(row == 1, jnp.sum(norms * norms, keepdims=True), square)


def adam(param, grad, first, second):
    first_new = BETA_ONE * first + (1.0 - BETA_ONE) * grad
    second_new = BETA_TWO * second + (1.0 - BETA_TWO) * grad * grad
    first_hat = first_new / (1.0 - BETA_ONE**STEP)
    second_hat = second_new / (1.0 - BETA_TWO**STEP)
    fresh = param - RATE * (first_hat / (jnp.sqrt(second_hat) + ADAM_EPS) + DECAY * param)
    return fresh, first_new, second_new


def turn_kernel(grads_ref, gnorm_ref, gmid_ref, gout_ref, at_ref, in_ref, mid_ref, out_ref, norm_ref):
    width, classes, share = in_ref.shape[0], out_ref.shape[0], mid_ref.shape[1]
    whole = gnorm_ref[...]
    mine = jnp.zeros((8, share), F32)
    for f in range(HID // share):
        mine = mine + jnp.where(at_ref[0] == f, whole[:, f * share : (f + 1) * share], 0.0)
    for k in range(2):
        in_ref[:, k, :] = grads_ref[k * FEAT_PAD : k * FEAT_PAD + width, :]
        mid_ref[k] = gmid_ref[k * share : (k + 1) * share, :]
        out_ref[:, k, :] = jnp.transpose(gout_ref[:, k * LANE : (k + 1) * LANE])[0:classes, :]
        norm_ref[k] = mine[2 * k : 2 * k + 2, :]


def update_kernel(total_ref, sq0_ref, sq1_ref, sq2_ref, sq3_ref, loss_ref, *refs):
    grads, params, firsts, seconds = (refs[i : i + 4] for i in range(0, 16, 4))
    loss_out, count_out, gnorm_out, *results = refs[16:]
    loss_out[...] = total_ref[0:1, 0:1]
    count_out[...] = loss_ref[2:3, 0:1]
    square = (sq0_ref[0:1, 0:1] + sq1_ref[0:1, 0:1]) + (sq2_ref[0:1, 0:1] + sq3_ref[0:1, 0:1])
    grad_norm = jnp.sqrt(square + sq0_ref[1:2, 0:1])
    gnorm_out[...] = grad_norm
    factor = jnp.minimum(1.0, CLIP_LEVEL / (grad_norm + 1e-06)).reshape(1, 1, 1)
    for i in range(4):
        fresh, first, second = adam(params[i][...], grads[i][...] * factor, firsts[i][...], seconds[i][...])
        results[i][...], results[4 + i][...], results[8 + i][...] = fresh, first, second
        if i < 3:
            results[12 + i][...] = fresh.astype(BF)


def exchange(x, parts):
    return lax.all_to_all(x.reshape(parts, -1, x.shape[-1]), "dom", split_axis=0, concat_axis=0, tiled=True)


def native(w_in, w_mid, w_out, norm):
    return (jnp.transpose(w_in, (1, 0, 2)), w_mid, jnp.transpose(w_out, (2, 0, 1)), norm)


def restore(w_in, w_mid, w_out, *norm):
    return (jnp.transpose(w_in, (1, 0, 2)), w_mid, jnp.transpose(w_out, (1, 2, 0)), *norm)


def shards(
    features,
    inner_adj,
    bound_adj,
    keep_slots,
    send_index,
    labels,
    train_mask,
    w_in,
    w_mid,
    w_out,
    norm_params,
    m_in,
    m_mid,
    m_out,
    m_norms,
    v_in,
    v_mid,
    v_out,
    v_norms,
    *,
    parts,
    feats,
):
    nodes = features.shape[0]
    each = send_index.shape[2]
    halo = parts * each
    classes = w_out.shape[2]
    share = w_mid.shape[1]
    width = features.shape[1]
    run = functools.partial(call, mib=16 if parts <= 16 else 52)
    labels = labels.reshape(nodes // LANE, LANE)
    mask = train_mask.reshape(nodes // LANE, LANE)
    params = native(w_in, w_mid, w_out, norm_params)
    firsts = native(m_in, m_mid, m_out, m_norms)
    seconds = native(v_in, v_mid, v_out, v_norms)
    feat_at = lax.axis_index("feat").astype(jnp.int32).reshape(1)

    def bf(*dims):
        return shape(*dims, dtype=BF)

    def in_hbm(*arrays):
        return tuple(pltpu.with_memory_space_constraint(a, pltpu.HBM) for a in arrays)

    loads = in_hbm(send_index, features.T, *params)
    send, own, at = run(
        pack_kernel, [bf(parts, feats, each // 2, LANE), bf(pack_rows(nodes, share), HID), shape(1, dtype=jnp.int32)],
        *loads, feat_at, smem_in=(6,), smem_out=(2,), hbm_in=range(6),
        scratch=[pltpu.VMEM((halo, nodes), BF)] + [pltpu.VMEM(a.shape, a.dtype) for a in loads] + [pltpu.SemaphoreType.DMA((6,))],
    )
    recv = lax.all_to_all(
        send.reshape(parts * feats, each // 2, LANE), ("dom", "feat"), split_axis=0, concat_axis=0, tiled=True
    ).reshape(parts, feats, each // 2, LANE)
    chip = lax.ppermute(own, "feat", [(s, s ^ 2) for s in range(feats)])
    core = lax.ppermute(own, "feat", [(s, s ^ 1) for s in range(feats)])
    far = lax.ppermute(chip, "feat", [(s, s ^ 1) for s in range(feats)])
    loads = in_hbm(own, chip)
    results = [((feats * FEAT_PAD, nodes), BF), ((2, feats * FEAT_PAD, HID), BF), ((2, HID, HID), BF), ((2, LANE, HID), BF), ((8, HID), F32)]
    ft, win, wmid, wout, norms = run(
        side_kernel, [pltpu.HBM(*r) for r in results], *loads, core, far, at, hbm_in=range(2), smem_in=(4,), hbm_out=range(5),
        scratch=[pltpu.VMEM(*r) for r in results] + [pltpu.VMEM(a.shape, a.dtype) for a in loads]
        + [pltpu.SemaphoreType.DMA((2,)), pltpu.SemaphoreType.DMA((5,))],
    )
    loads = in_hbm(inner_adj, bound_adj, keep_slots, send_index, ft, win, norms)
    tile, ring, bound_ring = (512, 3, 4) if parts <= 16 else (256, 2, 2)
    adj, edge, row_deg, sel, mean_one, xhat_one, slope_one, istd_one, h_one, inv_deg, send = run(
        functools.partial(first_kernel, width=width),
        [bf(nodes, nodes), bf(nodes, halo), shape(nodes, LANE), bf(halo, nodes), bf(nodes, LANE),
         shape(nodes, HID), shape(nodes, HID), shape(nodes, LANE), bf(nodes, HID), shape(nodes, LANE), bf(halo, HID)],
        *loads, recv, hbm_in=range(7), mib=24 if parts <= 16 else 52,
        scratch=[pltpu.VMEM((halo, LANE), BF), pltpu.VMEM(keep_slots.shape, jnp.int32), pltpu.VMEM(send_index.shape, jnp.int32)]
        + [pltpu.VMEM(a.shape, a.dtype) for a in loads[4:]]
        + [pltpu.VMEM((ring, tile, nodes), jnp.int32), pltpu.VMEM((bound_ring, tile, halo), jnp.int32),
           pltpu.SemaphoreType.DMA((2, max(ring, bound_ring))), pltpu.SemaphoreType.DMA((5,))],
    )
    halo_one = exchange(send, parts).reshape(halo, HID)
    mean_two, xhat_two, slope_two, istd_two, h_two, send = run(
        second_kernel,
        [bf(nodes, HID), shape(nodes, HID), shape(nodes, HID), shape(nodes, LANE), bf(nodes, HID), bf(halo, HID)],
        adj, edge, halo_one, h_one, wmid, norms, inv_deg, sel,
    )
    halo_two = exchange(send, parts).reshape(halo, HID)
    mean_head, logits, pred, cross, mine, send = run(
        head_kernel,
        [bf(nodes, HID), shape(nodes, LANE), bf(nodes, LANE), shape(halo, LANE), shape(halo, LANE), bf(halo, HID)],
        adj, edge, halo_two, h_two, wout, inv_deg, sel, mask,
    )
    recv = exchange(send, parts).reshape(halo, HID)
    grad, grad_sum, send, losses = run(
        functools.partial(logit_grad_kernel, classes=classes, each=each),
        [bf(nodes, LANE), bf(nodes, HID), bf(halo, HID), shape(8, LANE)],
        logits, labels, mask, row_deg, pred, edge, recv, mine, cross, sel, wout, inv_deg,
        scratch=[pltpu.VMEM((halo, LANE), BF), pltpu.VMEM((halo, LANE), BF), pltpu.VMEM((nodes, LANE), F32), pltpu.VMEM((nodes, LANE), F32)],
    )
    recv = exchange(send, parts).reshape(halo, HID)
    joined_two, grad_sum, send, norm_sums = run(
        functools.partial(second_back_kernel, each=each),
        [bf(nodes, HID), bf(nodes, HID), bf(parts, each + 32, HID), shape(8, HID)],
        adj, grad_sum, grad, wout, recv, sel, slope_two, xhat_two, istd_two, norms, wmid, inv_deg, edge,
        h_two, mean_head, h_one, mean_two, at, smem_in=(17,),
        scratch=[pltpu.VMEM((nodes, HID), F32), pltpu.VMEM((2, LANE, HID), F32), pltpu.VMEM((LANE, HID), F32)],
    )
    recv = exchange(send, parts)
    send, = run(
        functools.partial(first_back_kernel, each=each), [bf(parts, MESSAGE_ROWS, HID)],
        adj, grad_sum, joined_two, wmid, recv, sel, slope_one, xhat_one, istd_one, norms, ft, mean_one, losses, norm_sums, at,
        smem_in=(14,),
        scratch=[pltpu.VMEM((nodes, HID), BF), pltpu.VMEM((nodes, HID), F32), pltpu.VMEM((2, feats * FEAT_PAD, HID), F32),
                 pltpu.VMEM((halo, HID), BF)],
    )
    recv = exchange(send, parts)
    grads, gnorm, total, gmid, gout, square = run(
        functools.partial(total_kernel, width=width),
        [shape(CHUNK_ROW, HID), shape(8, HID), shape(8, LANE), shape(2 * share, HID), shape(share, HID), shape(8, LANE)], recv,
    )
    squares = [square]
    for k in range(1, feats):
        squares.append(lax.ppermute(square, "feat", [(s, s ^ k) for s in range(feats)]))
    outs = [shape(1, 1)] * 3 + [shape(*p.shape) for p in params] * 3 + [bf(*p.shape) for p in params[:3]]
    grads = run(turn_kernel, [shape(*p.shape) for p in params], grads, gnorm, gmid, gout, at, smem_in=(4,))
    result = run(update_kernel, outs, total, *squares, losses, *grads, *params, *firsts, *seconds)
    return (
        tuple(r.reshape(()) for r in result[:3])
        + restore(*result[3:7]) + restore(*result[7:11]) + restore(*result[11:15]) + restore(*result[15:])
    )


def solution(mesh):
    weight = P(None, "feat", None)
    norm = P(None, None, "feat")
    placed = (
        P("dom", "feat"), P("dom", None), P("dom", None), P("dom", None), P("dom", None, None), P("dom"), P("dom"),
    ) + (weight, weight, weight, norm) * 3
    return jax.shard_map(
        functools.partial(shards, parts=mesh.shape["dom"], feats=mesh.shape["feat"]),
        mesh=mesh,
        in_specs=placed,
        out_specs=(P(), P(), P()) + (weight, weight, weight, norm) * 3 + (weight,) * 3,
        check_vma=False,
    )
```

```python
import functools
import math

import jax
import jax.numpy as jnp
from jax import lax
from jax.experimental import pallas as pl
from jax.experimental.pallas import tpu as pltpu
from jax.sharding import PartitionSpec as P

HID = 256
STEP = 5

NORM_EPS = 1e-05
PEN_WEIGHT = 0.001
CLIP_LEVEL = 0.01
RATE = 0.05
BETA_ONE = 0.5
BETA_TWO = 0.5
ADAM_EPS = 1e-08
DECAY = 0.01

BF = jnp.bfloat16
F32 = jnp.float32
LANE = 128
FEAT_PAD = 32
MIB = 1 << 20

VMEM = pl.BlockSpec(memory_space=pltpu.VMEM)
SMEM = pl.BlockSpec(memory_space=pltpu.SMEM)
ANY = pl.BlockSpec(memory_space=pl.ANY)
HBM = pl.BlockSpec(memory_space=pltpu.HBM)


def dot_nn(a, b):
    return jnp.dot(a, b, preferred_element_type=F32)


def dot_tn(a, b):
    return lax.dot_general(a, b, (((0,), (0,)), ((), ())), preferred_element_type=F32)


def dot_nt(a, b):
    return lax.dot_general(a, b, (((1,), (1,)), ((), ())), preferred_element_type=F32)


def iota(shape, axis):
    return lax.broadcasted_iota(jnp.int32, shape, axis)


def place(rows, cols, shift, turned=False):
    dims = (cols, rows) if turned else (rows, cols)
    return (iota(dims, int(turned)) + shift == iota(dims, int(not turned))).astype(F32).astype(BF)


def widen(x):
    return x.astype(F32)


def bf_parts(x, count):
    parts = []
    for _ in range(count):
        part = x.astype(BF)
        parts.append(part)
        x = x - widen(part)
    return parts


def both(x):
    return jnp.concatenate([x, x], 1)


def rows_of(i, tile):
    return pl.ds(pl.multiple_of(i * tile, tile), tile)


def call(kernel, outs, *args, mib=24, flops=0, smem_in=(), any_in=(), hbm_in=(), smem_out=(), hbm_out=(), scratch=()):
    size = sum(math.prod(a.shape) * a.dtype.itemsize for a in (*args, *outs))
    return pl.pallas_call(
        kernel,
        out_shape=outs,
        in_specs=[SMEM if i in smem_in else ANY if i in any_in else HBM if i in hbm_in else VMEM for i in range(len(args))],
        out_specs=[SMEM if i in smem_out else HBM if i in hbm_out else VMEM for i in range(len(outs))],
        scratch_shapes=list(scratch),
        cost_estimate=pl.CostEstimate(flops=flops, bytes_accessed=size // 4, transcendentals=0),
        compiler_params=pltpu.CompilerParams(vmem_limit_bytes=mib * MIB),
    )(*args)


def shape(*dims, dtype=F32):
    return jax.ShapeDtypeStruct(dims, dtype)


def select(idx_ref, sel_ref):
    nodes = sel_ref.shape[1]
    parts, each = idx_ref.shape[1:]
    eye = iota((each, each), 0) == iota((each, each), 1)
    for p in range(parts):
        column = jnp.sum(jnp.where(eye, idx_ref[0, p : p + 1, :].astype(F32), 0.0), 1, keepdims=True)
        hot = iota((each, nodes), 1) == column.astype(jnp.int32)
        sel_ref[p * each : (p + 1) * each, :] = hot.astype(F32).astype(BF)


def pack_kernel(idx_hbm, feat_hbm, w_in_hbm, w_mid_hbm, w_out_hbm, norm_hbm, at_ref, send_ref, pack_ref, at_out,
                sel_ref, idx_ref, feat_ref, w_in_ref, w_mid_ref, w_out_ref, norm_ref, sems):
    sources = (idx_hbm, feat_hbm, w_mid_hbm, w_in_hbm, w_out_hbm, norm_hbm)
    targets = (idx_ref, feat_ref, w_mid_ref, w_in_ref, w_out_ref, norm_ref)
    copies = [pltpu.make_async_copy(src, dst, sems.at[i]) for i, (src, dst) in enumerate(zip(sources, targets))]
    for copy in copies:
        copy.start()
    at_out[0] = at_ref[0]
    copies[0].wait()
    select(idx_ref, sel_ref)
    wait_all(copies[1:])
    nodes = feat_ref.shape[1]
    width, share = feat_ref.shape[0], w_mid_ref.shape[1]
    classes = w_out_ref.shape[0]
    rows = dot_nn(place(FEAT_PAD, width, 0), feat_ref[...].astype(BF))
    parts, copies, half, _ = send_ref.shape
    sent = dot_nt(sel_ref[...], rows.astype(BF)).astype(BF)
    left = dot_nn(sent, place(FEAT_PAD, LANE, 0)).reshape(parts, 2, half, LANE)[:, 0]
    right = dot_nn(sent, place(FEAT_PAD, LANE, LANE // 2)).reshape(parts, 2, half, LANE)[:, 1]
    for f in range(copies):
        send_ref[:, f] = (left + right).astype(BF)
    ones = iota((FEAT_PAD, nodes), 0) == FEAT_PAD - 1
    blocks = [jnp.zeros((FEAT_PAD, HID), F32) for _ in range(3)]
    for layer in range(2):
        for p, part in enumerate(bf_parts(norm_ref[layer], 3)):
            part = dot_nn(part, place(share, HID, 0)).astype(BF)
            blocks[p] = blocks[p] + dot_nn(place(2, FEAT_PAD, NORM_AT + 2 * layer, turned=True), part)
    blocks.append(jnp.zeros((FEAT_PAD, nodes - 3 * HID), F32))
    rows = (jnp.where(ones, 1.0, rows) + jnp.concatenate(blocks, 1)).astype(BF)
    at = 0
    for b in range(nodes // HID):
        pack_ref[at : at + FEAT_PAD, :] = rows[:, b * HID : (b + 1) * HID]
        at += FEAT_PAD
    for k in range(2):
        pack_ref[at : at + share, :] = w_mid_ref[k].astype(BF)
        at += share
    for k in range(2):
        pack_ref[at : at + FEAT_PAD, :] = dot_nn(place(FEAT_PAD, width, 0), w_in_ref[:, k, :].astype(BF)).astype(BF)
        at += FEAT_PAD
    turned = jnp.zeros((2 * CLASS_HALF, LANE), F32)
    for k in range(2):
        grown = dot_nn(place(classes, 2 * CLASS_HALF, 0, turned=True), w_out_ref[:, k, :].astype(BF)).astype(BF)
        turned = turned + dot_nn(grown, place(share, LANE, k * share))
    turned = turned.astype(BF)
    for half in range(2):
        pack_ref[at : at + CLASS_HALF, half * LANE : (half + 1) * LANE] = turned[half * CLASS_HALF : (half + 1) * CLASS_HALF, :]


NORM_AT = FEAT_PAD - 6
CLASS_HALF = 32


def pack_rows(nodes, share):
    return nodes // HID * FEAT_PAD + 2 * share + 2 * FEAT_PAD + CLASS_HALF


def spread(packed_refs, at_ref, ft_ref):
    row = iota((FEAT_PAD, HID), 0)
    keep = (row < NORM_AT) | (row == FEAT_PAD - 1)
    for k, packed_ref in enumerate(packed_refs):
        at = rows_of(at_ref[0] ^ k, FEAT_PAD)
        for b in range(ft_ref.shape[1] // HID):
            rows = widen(packed_ref[b * FEAT_PAD : (b + 1) * FEAT_PAD, :])
            ft_ref[at, b * HID : (b + 1) * HID] = jnp.where(keep, rows, 0.0).astype(BF)


def join_halo(recv_ref, halo_ref, width):
    parts, feats, half, _ = recv_ref.shape
    lane = iota((parts * half, LANE), 1)
    sides = [jnp.where(lane == LANE - 1, 1.0, 0.0)] * 2
    for f in range(feats):
        rows = widen(recv_ref[:, f]).reshape(parts * half, LANE)
        for g in range(2):
            at = g * (LANE // 2)
            side = jnp.where((lane >= at) & (lane < at + width), rows, 0.0)
            shift = (f * FEAT_PAD - at) % LANE
            sides[g] = sides[g] + (pltpu.roll(side, shift, 1) if shift else side)
    sides = [side.astype(BF).reshape(parts, half, LANE) for side in sides]
    halo_ref[...] = jnp.stack(sides, 1).reshape(halo_ref.shape)


def unpack(packed_refs, at_ref, win_ref, wmid_ref, wout_ref, norm_ref):
    share = HID // len(packed_refs)
    norms = jnp.zeros((8, HID), F32)
    heads = [jnp.zeros((2 * CLASS_HALF, HID), F32) for _ in range(2)]
    for offset, packed_ref in enumerate(packed_refs):
        f = at_ref[0] ^ offset
        at = packed_ref.shape[0] - 2 * share - 2 * FEAT_PAD - CLASS_HALF
        for k in range(2):
            wmid_ref[k, rows_of(f, share), :] = packed_ref[at : at + share, :]
            at += share
        for k in range(2):
            win_ref[k, rows_of(f, FEAT_PAD), :] = packed_ref[at : at + FEAT_PAD, :]
            at += FEAT_PAD
        halves = [widen(packed_ref[at : at + CLASS_HALF, h * LANE : (h + 1) * LANE]) for h in range(2)]
        head = both(jnp.concatenate(halves, 0))
        lane = iota(head.shape, 1)
        heads[0] = heads[0] + pltpu.roll(jnp.where(lane < share, head, 0.0), f * share, 1)
        heads[1] = heads[1] + pltpu.roll(jnp.where((lane >= LANE + share) & (lane < LANE + 2 * share), head, 0.0),
                                         (f * share + LANE - share) & (HID - 1), 1)
        part = jnp.zeros((8, HID), F32)
        for p in range(3):
            part = part + widen(packed_ref[p * FEAT_PAD + 16 : (p + 1) * FEAT_PAD, :])[8:16, :]
        part = jnp.where((iota((8, HID), 0) >= NORM_AT - 24) & (iota((8, HID), 0) < NORM_AT - 20), part, 0.0)
        norms = norms + pltpu.roll(part, f * share, 1)
    for k in range(2):
        wout_ref[k, 0 : 2 * CLASS_HALF, :] = heads[k].astype(BF)
        wout_ref[k, 2 * CLASS_HALF :, :] = jnp.zeros((LANE - 2 * CLASS_HALF, HID), BF)
    norm_ref[...] = pltpu.roll(norms, 8 - (NORM_AT - 24), 0)


TILE = 2048


def loop(count, tile, body, carry=0):
    return lax.fori_loop(0, count // tile, lambda i, c: body(rows_of(i, tile), c), carry)


def norm_forward(joined, norm_ref, layer):
    center = jnp.sum(joined, 1, keepdims=True) * (1.0 / HID)
    spread = jnp.sum(joined * joined, 1, keepdims=True) * (1.0 / HID) - center * center
    inv_std = lax.rsqrt(spread + NORM_EPS)
    x_hat = (joined - center) * inv_std
    normed = x_hat * norm_ref[2 * layer : 2 * layer + 1, :] + norm_ref[2 * layer + 1 : 2 * layer + 2, :]
    gate = 0.5 * jnp.tanh(0.5 * normed) + 0.5
    hidden = normed * gate
    return inv_std, x_hat, hidden, gate + hidden * (1.0 - gate)


def keep_norm(s, parts, xhat_ref, slope_ref, istd_ref, h_ref):
    inv_std, x_hat, hidden, slope = parts
    xhat_ref[s, :] = x_hat
    slope_ref[s, :] = slope
    istd_ref[s, :] = jnp.broadcast_to(inv_std, (x_hat.shape[0], LANE))
    h_ref[s, :] = hidden.astype(BF)


GATHER_ROWS = 512


def start_all(copies):
    for copy in copies:
        copy.start()
    return copies


def wait_all(copies):
    for copy in copies:
        copy.wait()


def side_kernel(own_hbm, chip_hbm, core_ref, far_ref, at_ref,
                ft_out, win_out, wmid_out, wout_out, norm_out,
                ft_ref, win_ref, wmid_ref, wout_ref, norm_ref, own_ref, chip_ref, in_sems, out_sems):
    packed_refs = (own_ref, core_ref, chip_ref, far_ref)
    loads = ((own_hbm, own_ref), (chip_hbm, chip_ref))
    wait_all(start_all([pltpu.make_async_copy(src, dst, in_sems.at[i]) for i, (src, dst) in enumerate(loads)]))
    pairs = ((ft_ref, ft_out), (win_ref, win_out), (wmid_ref, wmid_out), (wout_ref, wout_out), (norm_ref, norm_out))
    stores = [pltpu.make_async_copy(src, dst, out_sems.at[i]) for i, (src, dst) in enumerate(pairs)]
    spread(packed_refs, at_ref, ft_ref)
    stores[0].start()
    unpack(packed_refs, at_ref, win_ref, wmid_ref, wout_ref, norm_ref)
    start_all(stores[1:])
    wait_all(stores)


def first_kernel(adj_hbm, bound_hbm, keep_hbm, idx_hbm, ft_hbm, win_hbm, norm_hbm, recv_ref,
                 adj_ref, edge_ref, row_ref, sel_ref, mean_ref, xhat_ref, slope_ref, istd_ref, h_ref, invd_ref, send_ref,
                 halo_ref, keep_ref, idx_ref, ft_ref, win_ref, norm_ref, adj_buf, bound_buf, ring_sems, sems, *, width):
    nodes = edge_ref.shape[0]
    ring, tile = adj_buf.shape[0:2]

    def fetch(step, slot):
        return pltpu.make_async_copy(adj_hbm.at[rows_of(step, tile)], adj_buf.at[slot], ring_sems.at[0, slot])

    def fetch_bound(step, slot):
        return pltpu.make_async_copy(bound_hbm.at[rows_of(step, tile)], bound_buf.at[slot], ring_sems.at[1, slot])

    sources, targets = (keep_hbm, idx_hbm, ft_hbm, win_hbm, norm_hbm), (keep_ref, idx_ref, ft_ref, win_ref, norm_ref)
    small = [pltpu.make_async_copy(src, dst, sems.at[i]) for i, (src, dst) in enumerate(zip(sources, targets))]
    start_all(small[0:2])
    for step in range(bound_buf.shape[0]):
        fetch_bound(step, step).start()
    start_all(small[2:])
    for step in range(ring):
        fetch(step, step).start()
    join_halo(recv_ref, halo_ref, width)
    wait_all(small[0:2])
    select(idx_ref, sel_ref)

    def boundary(step, _):
        slot = lax.rem(step, bound_buf.shape[0])
        s = rows_of(step, tile)
        fetch_bound(step, slot).wait()
        edge_ref[s, :] = (bound_buf[slot] * keep_ref[...]).astype(F32).astype(BF)

        @pl.when(step + bound_buf.shape[0] < nodes // tile)
        def _():
            fetch_bound(step + bound_buf.shape[0], slot).start()

        return 0

    lax.fori_loop(0, nodes // tile, boundary, 0)
    wait_all(small[2:])

    def gather(step, _):
        for part in range(GATHER_ROWS // tile):
            chunk = step * (GATHER_ROWS // tile) + part
            slot = lax.rem(chunk, ring)
            fetch(chunk, slot).wait()
            adj_ref[rows_of(chunk, tile), :] = adj_buf[slot].astype(F32).astype(BF)

            @pl.when(chunk + ring < nodes // tile)
            def _():
                fetch(chunk + ring, slot).start()

        s = rows_of(step, GATHER_ROWS)
        far = dot_nn(edge_ref[s, :], halo_ref[...])
        row_ref[s, :] = jnp.broadcast_to(far[:, LANE - 1 : LANE], far.shape)
        summed = dot_nt(adj_ref[s, :], ft_ref[...]) + far
        inv_deg = 1.0 / jnp.maximum(summed[:, LANE - 1 : LANE], 1.0)
        invd_ref[s, :] = jnp.broadcast_to(inv_deg, summed.shape)
        mean_ref[s, :] = (summed * inv_deg).astype(BF)
        return 0

    lax.fori_loop(0, nodes // GATHER_ROWS, gather, 0)

    def apply(s, _):
        joined = dot_tn(ft_ref[:, s], win_ref[0]) + dot_nn(mean_ref[s, :], win_ref[1])
        keep_norm(s, norm_forward(joined, norm_ref, 0), xhat_ref, slope_ref, istd_ref, h_ref)
        return 0

    loop(nodes, TILE, apply)
    send_ref[...] = dot_nn(sel_ref[...], h_ref[...]).astype(BF)


def gather_mean(adj_ref, hin_ref, edge_ref, halo_ref, invd_ref, mean_ref):
    def gather(s, _):
        summed = dot_nn(adj_ref[s, :], hin_ref[...]) + dot_nn(edge_ref[s, :], halo_ref[...])
        mean_ref[s, :] = (summed * both(invd_ref[s, :])).astype(BF)
        return 0

    loop(adj_ref.shape[0], TILE, gather)


def second_kernel(adj_ref, edge_ref, halo_ref, hin_ref, w_ref, norm_ref, invd_ref, sel_ref,
                  mean_ref, xhat_ref, slope_ref, istd_ref, h_ref, send_ref):
    gather_mean(adj_ref, hin_ref, edge_ref, halo_ref, invd_ref, mean_ref)

    def apply(s, _):
        joined = dot_nn(hin_ref[s, :], w_ref[0]) + dot_nn(mean_ref[s, :], w_ref[1])
        keep_norm(s, norm_forward(joined, norm_ref, 1), xhat_ref, slope_ref, istd_ref, h_ref)
        return 0

    loop(adj_ref.shape[0], TILE, apply)
    send_ref[...] = dot_nn(sel_ref[...], h_ref[...]).astype(BF)


def split_count(x):
    high = jnp.floor(x * (1.0 / 256.0))
    return high, x - 256.0 * high


def head_kernel(adj_ref, edge_ref, halo_ref, hin_ref, w_ref, invd_ref, sel_ref, mask_ref,
                mean_ref, logit_ref, pred_ref, cross_ref, mine_ref, send_ref):
    gather_mean(adj_ref, hin_ref, edge_ref, halo_ref, invd_ref, mean_ref)

    def apply(s, _):
        logits = dot_nt(hin_ref[s, :], w_ref[0]) + dot_nt(mean_ref[s, :], w_ref[1])
        logit_ref[s, :] = logits
        pred_ref[s, :] = jnp.where(iota(logits.shape, 1) == LANE - 1, 1.0, logits).astype(BF)
        return 0

    loop(adj_ref.shape[0], TILE, apply)
    mine = dot_nn(sel_ref[...], pred_ref[...])
    lane = iota(mine.shape, 1)
    mine = jnp.where(lane < 64, mine, 0.0)
    mine_ref[...] = mine
    cross = dot_tn(edge_ref[...], pred_ref[...])
    cross_ref[...] = cross
    high, low = bf_parts(jnp.where(lane < 64, cross, 0.0), 2)
    count = jnp.sum(mask_ref[...].astype(F32), keepdims=True)
    count_high, count_low = split_count(count)
    col_high, col_low = split_count(cross[:, LANE - 1 : LANE])
    extra = jnp.where(lane == 64, count_high, 0.0) + jnp.where(lane == 65, count_low, 0.0)
    extra = extra + jnp.where(lane == 66, col_high, 0.0) + jnp.where(lane == 67, col_low, 0.0)
    send_ref[:, 0:LANE] = (mine + pltpu.roll(widen(low), 64, 1)).astype(BF)
    send_ref[:, LANE:] = (widen(high) + extra).astype(BF)


def spread_row(values, row):
    pick = (iota(values.shape, 0) == row).astype(F32).astype(BF)
    return dot_tn(values.astype(F32).astype(BF), pick)


def logit_grad_kernel(logit_ref, label_ref, mask_ref, row_ref, pred_ref, edge_ref, recv_ref, mine_ref, cross_ref,
                      sel_ref, w_ref, invd_ref,
                      grad_ref, gs_ref, send_ref, loss_ref, hp_ref, ret_ref, lab_ref, wgt_ref, *, classes, each):
    slots = mine_ref.shape[0]
    nodes = logit_ref.shape[0]
    first, second = widen(recv_ref[:, 0:LANE]), widen(recv_ref[:, LANE:])
    lane = iota((slots, LANE), 1)
    low_half = lane < 64
    halo_pred = jnp.where(low_half, first, 0.0)
    back_cross = jnp.where(low_half, second + pltpu.roll(first, 64, 1), 0.0)
    count = 256.0 * jnp.sum(jnp.where(lane == 64, second, 0.0), keepdims=True)
    count = (count + jnp.sum(jnp.where(lane == 65, second, 0.0), keepdims=True)) * (1.0 / each)
    col_back = 256.0 * second[:, 66:67] + second[:, 67:68]
    scale = 2.0 * PEN_WEIGHT / count
    inv_count = 1.0 / count
    hp_ref[...] = halo_pred.astype(BF)
    ret_ref[...] = (scale * (col_back * mine_ref[...] - back_cross)).astype(BF)
    pen = jnp.sum(cross_ref[:, LANE - 1 : LANE] * (halo_pred * halo_pred), keepdims=True)
    pen = pen - 2.0 * jnp.sum(halo_pred * cross_ref[...], keepdims=True)
    for r in range(nodes // LANE):
        lab_ref[r * LANE : (r + 1) * LANE, :] = spread_row(label_ref[...], r)
        wgt_ref[r * LANE : (r + 1) * LANE, :] = spread_row(mask_ref[...], r)

    def body(s, carry):
        ce_sum, pen_sum = carry
        logits = logit_ref[s, :]
        lane = iota(logits.shape, 1)
        real = lane < classes
        top = jnp.max(jnp.where(real, logits, -jnp.inf), 1, keepdims=True)
        shifted = jnp.where(real, jnp.exp(jnp.where(real, logits - top, 0.0)), 0.0)
        total = jnp.sum(shifted, 1, keepdims=True)
        hot = (lane.astype(F32) == lab_ref[s, :]).astype(F32)
        target = jnp.sum(logits * hot, 1, keepdims=True)
        weight = wgt_ref[s, :]
        ce_sum = ce_sum + jnp.sum(weight[:, 0:1] * (top + jnp.log(total) - target), keepdims=True)
        pred = jnp.where(real, widen(pred_ref[s, :]), 0.0)
        drawn = row_ref[s, :] * pred
        pen_sum = pen_sum + jnp.sum(drawn * pred, keepdims=True)
        own = drawn - dot_nn(edge_ref[s, :], hp_ref[...])
        back = dot_tn(sel_ref[:, s], ret_ref[...])
        grad = ((inv_count * weight) * (shifted * (1.0 / total) - hot) + scale * own + back).astype(BF)
        grad_ref[s, :] = grad
        gs_ref[s, :] = (dot_nn(grad, w_ref[1]) * both(invd_ref[s, :])).astype(BF)
        return ce_sum, pen_sum

    zero = jnp.zeros((1, 1), F32)
    ce_sum, pen_sum = loop(nodes, TILE, body, (zero, zero))
    row = iota((8, LANE), 0)
    loss_ref[...] = (jnp.where(row == 0, ce_sum, 0.0) + jnp.where(row == 1, pen + pen_sum, 0.0)
                     + jnp.where(row == 2, count, 0.0))
    send_ref[...] = dot_tn(edge_ref[...], gs_ref[...]).astype(BF)


BACK_TILE = 1024


def layer_back(adj_ref, gs_ref, grad_ref, w_ref, sel_ref, halo_ref, slope_ref, xhat_ref, istd_ref, norm_ref, layer, own_ref, gj_ref, back):
    nodes = adj_ref.shape[0]

    def pull(s, _):
        own_ref[s, :] = (dot_tn(adj_ref[:, s], gs_ref[...]) + back(grad_ref[s, :], w_ref[0])
                         + dot_tn(sel_ref[:, s], halo_ref[...]))
        return 0

    loop(nodes, BACK_TILE, pull)

    def body(s, carry):
        gain_sum, bias_sum = carry
        grad_pre = own_ref[s, :] * slope_ref[s, :]
        x_hat = xhat_ref[s, :]
        grad_x = grad_pre * norm_ref[2 * layer : 2 * layer + 1, :]
        mean_one = jnp.sum(grad_x, 1, keepdims=True) * (1.0 / HID)
        mean_two = jnp.sum(grad_x * x_hat, 1, keepdims=True) * (1.0 / HID)
        gj_ref[s, :] = (both(istd_ref[s, :]) * (grad_x - mean_one - x_hat * mean_two)).astype(BF)
        gain_sum = gain_sum + jnp.sum(grad_pre * x_hat, 0, keepdims=True)
        bias_sum = bias_sum + jnp.sum(grad_pre, 0, keepdims=True)
        return gain_sum, bias_sum

    zero = jnp.zeros((1, HID), F32)
    return loop(nodes, TILE, body, (zero, zero))


def second_back_kernel(adj_ref, gsin_ref, grad_ref, wout_ref, recv_ref, sel_ref, slope_ref, xhat_ref, istd_ref, norm_ref, w_ref,
                       invd_ref, edge_ref, h_two_ref, mean_head_ref, h_one_ref, mean_two_ref, at_ref,
                       gj_ref, gs_ref, send_ref, sums_ref, own_ref, full_ref, head_ref, *, each):
    gain_sum, bias_sum = layer_back(
        adj_ref, gsin_ref, grad_ref, wout_ref, sel_ref, recv_ref, slope_ref, xhat_ref, istd_ref, norm_ref, 1, own_ref, gj_ref, dot_nn
    )
    row = iota((8, HID), 0)
    sums_ref[...] = jnp.where(row == 2, gain_sum, 0.0) + jnp.where(row == 3, bias_sum, 0.0)

    def body(s, _):
        gs_ref[s, :] = (dot_nt(gj_ref[s, :], w_ref[1]) * both(invd_ref[s, :])).astype(BF)
        return 0

    loop(adj_ref.shape[0], TILE, body)
    parts = send_ref.shape[0]
    send_ref[:, 0:each, :] = dot_tn(edge_ref[...], gs_ref[...]).astype(BF).reshape(parts, each, HID)
    share = HID // FEATS
    half = pl.ds(pl.multiple_of(at_ref[0] * share // LANE * LANE, LANE), LANE)
    start = at_ref[0] * share % LANE
    head_ref[:, 0:LANE] = dot_tn(h_two_ref[:, half], grad_ref[...])
    head_ref[:, LANE:] = dot_tn(mean_head_ref[:, half], grad_ref[...])
    full_ref[0] = dot_tn(h_one_ref[:, half], gj_ref[...])
    full_ref[1] = dot_tn(mean_two_ref[:, half], gj_ref[...])
    for q in range(parts):
        if q * 16 < 2 * share:
            k, r = divmod(q * 16, share)
            send_ref[q, each : each + 16, :] = full_ref[k, pl.ds(pl.multiple_of(start + r, 16), 16), :].astype(BF)
            rows = head_ref[pl.ds(pl.multiple_of(start + q * 8, 8), 8), :]
            high, low = bf_parts(rows, 2)
            send_ref[q, each + 16 : each + 32, :] = jnp.concatenate([widen(high), widen(low)], 0).astype(BF)
        else:
            send_ref[q, each : each + 32, :] = jnp.zeros((32, HID), BF)


FEATS = 4


def first_back_kernel(adj_ref, gsin_ref, grad_ref, w_ref, recv_ref, sel_ref, slope_ref, xhat_ref, istd_ref, norm_ref,
                      ft_ref, mean_ref, loss_ref, sums_ref, at_ref,
                      send_ref, gj_ref, own_ref, full_ref, halo_ref, *, each):
    parts = recv_ref.shape[0]
    halo_ref[...] = recv_ref[:, 0:each, :].reshape(halo_ref.shape)
    gain_sum, bias_sum = layer_back(
        adj_ref, gsin_ref, grad_ref, w_ref, sel_ref, halo_ref, slope_ref, xhat_ref, istd_ref, norm_ref, 0, own_ref, gj_ref, dot_nt
    )
    row = iota((8, HID), 0)
    sums = sums_ref[...] + jnp.where(row == 0, gain_sum, 0.0) + jnp.where(row == 1, bias_sum, 0.0)
    full_ref[0] = dot_nn(ft_ref[...], gj_ref[...])
    full_ref[1] = dot_tn(mean_ref[...], gj_ref[...])
    at = rows_of(at_ref[0], FEAT_PAD)
    mid = jnp.zeros((16, HID), F32)
    out = jnp.zeros((16, HID), F32)
    for q in range(parts):
        mid = mid + widen(recv_ref[q, each : each + 16, :])
        out = out + widen(recv_ref[q, each + 16 : each + 32, :])
    out = out + pltpu.roll(out, 8, 0)
    mid_high, mid_low = bf_parts(mid, 2)
    out_high, out_low = bf_parts(out, 2)
    out = jnp.where(iota((16, HID), 0) < 8, widen(out_high), widen(out_low))
    lane = iota((8, HID), 1)
    blocks = []
    for k, norm_part in enumerate(bf_parts(sums, 2)):
        tail = jnp.zeros((8, HID), F32)
        for p, part in enumerate(bf_parts(jnp.broadcast_to(loss_ref[k : k + 1, 0:1], (8, HID)), 3)):
            tail = tail + jnp.where(lane == p, widen(part), 0.0)
        rows = full_ref[k, at, :]
        last = jnp.where(row == 0, rows[FEAT_PAD - 8 :, :], jnp.where(row == 3, tail, 0.0))
        blocks += [rows[0 : FEAT_PAD - 8, :], jnp.where(row >= 4, pltpu.roll(widen(norm_part), 4, 0), last)]
    message = jnp.concatenate([*blocks, widen(mid_high), widen(mid_low), out], 0).astype(BF)
    for q in range(parts):
        send_ref[q] = message


CHUNK_ROW = 2 * FEAT_PAD
MESSAGE_ROWS = CHUNK_ROW + 48


def total_kernel(recv_ref, grads_ref, norm_ref, loss_ref, mid_ref, out_ref, square_ref, *, width):
    parts = recv_ref.shape[0]
    grads = jnp.zeros((CHUNK_ROW, HID), F32)
    for q in range(parts):
        grads = grads + widen(recv_ref[q, 0:CHUNK_ROW, :])
    grads_ref[...] = grads
    tails = [grads[FEAT_PAD - 8 : FEAT_PAD, :], grads[2 * FEAT_PAD - 8 :, :]]
    row = iota((8, HID), 0)
    norms = jnp.where(row < 4, pltpu.roll(tails[0] + tails[1], 4, 0), 0.0)
    norm_ref[...] = norms
    sums = [jnp.sum(tail[3:4, :], keepdims=True) for tail in tails]
    loss_ref[...] = jnp.broadcast_to(sums[0] + PEN_WEIGHT * sums[1], loss_ref.shape)
    for q in range(mid_ref.shape[0] // 16):
        at = CHUNK_ROW
        mid_ref[q * 16 : q * 16 + 16, :] = widen(recv_ref[q, at : at + 16, :]) + widen(recv_ref[q, at + 16 : at + 32, :])
        rows = widen(recv_ref[q, at + 32 : at + 48, :])
        out_ref[q * 8 : q * 8 + 8, :] = rows[0:8, :] + rows[8:16, :]
    weight_row = (iota((CHUNK_ROW, HID), 0) & (FEAT_PAD - 1)) < width
    first = jnp.where(weight_row, grads, 0.0)
    square = jnp.sum(first * first, keepdims=True)
    square = square + jnp.sum(mid_ref[...] * mid_ref[...], keepdims=True)
    square = square + jnp.sum(out_ref[...] * out_ref[...], keepdims=True)
    row = iota((8, LANE), 0)
    square_ref[...] = jnp.where(row == 1, jnp.sum(norms * norms, keepdims=True), square)


def adam(param, grad, first, second):
    first_new = BETA_ONE * first + (1.0 - BETA_ONE) * grad
    second_new = BETA_TWO * second + (1.0 - BETA_TWO) * grad * grad
    first_hat = first_new / (1.0 - BETA_ONE**STEP)
    second_hat = second_new / (1.0 - BETA_TWO**STEP)
    fresh = param - RATE * (first_hat / (jnp.sqrt(second_hat) + ADAM_EPS) + DECAY * param)
    return fresh, first_new, second_new


def turn_kernel(grads_ref, gnorm_ref, gmid_ref, gout_ref, at_ref, in_ref, mid_ref, out_ref, norm_ref):
    width, classes, share = in_ref.shape[0], out_ref.shape[0], mid_ref.shape[1]
    whole = gnorm_ref[...]
    mine = jnp.zeros((8, share), F32)
    for f in range(HID // share):
        mine = mine + jnp.where(at_ref[0] == f, whole[:, f * share : (f + 1) * share], 0.0)
    for k in range(2):
        in_ref[:, k, :] = grads_ref[k * FEAT_PAD : k * FEAT_PAD + width, :]
        mid_ref[k] = gmid_ref[k * share : (k + 1) * share, :]
        out_ref[:, k, :] = jnp.transpose(gout_ref[:, k * LANE : (k + 1) * LANE])[0:classes, :]
        norm_ref[k] = mine[2 * k : 2 * k + 2, :]


def update_kernel(total_ref, sq0_ref, sq1_ref, sq2_ref, sq3_ref, loss_ref, *refs):
    grads, params, firsts, seconds = (refs[i : i + 4] for i in range(0, 16, 4))
    loss_out, count_out, gnorm_out, *results = refs[16:]
    loss_out[...] = total_ref[0:1, 0:1]
    count_out[...] = loss_ref[2:3, 0:1]
    square = (sq0_ref[0:1, 0:1] + sq1_ref[0:1, 0:1]) + (sq2_ref[0:1, 0:1] + sq3_ref[0:1, 0:1])
    grad_norm = jnp.sqrt(square + sq0_ref[1:2, 0:1])
    gnorm_out[...] = grad_norm
    factor = jnp.minimum(1.0, CLIP_LEVEL / (grad_norm + 1e-06)).reshape(1, 1, 1)
    for i in range(4):
        fresh, first, second = adam(params[i][...], grads[i][...] * factor, firsts[i][...], seconds[i][...])
        results[i][...], results[4 + i][...], results[8 + i][...] = fresh, first, second
        if i < 3:
            results[12 + i][...] = fresh.astype(BF)


def exchange(x, parts):
    return lax.all_to_all(x.reshape(parts, -1, x.shape[-1]), "dom", split_axis=0, concat_axis=0, tiled=True)


def native(w_in, w_mid, w_out, norm):
    return (jnp.transpose(w_in, (1, 0, 2)), w_mid, jnp.transpose(w_out, (2, 0, 1)), norm)


def restore(w_in, w_mid, w_out, *norm):
    return (jnp.transpose(w_in, (1, 0, 2)), w_mid, jnp.transpose(w_out, (1, 2, 0)), *norm)


def shards(
    features,
    inner_adj,
    bound_adj,
    keep_slots,
    send_index,
    labels,
    train_mask,
    w_in,
    w_mid,
    w_out,
    norm_params,
    m_in,
    m_mid,
    m_out,
    m_norms,
    v_in,
    v_mid,
    v_out,
    v_norms,
    *,
    parts,
    feats,
):
    nodes = features.shape[0]
    each = send_index.shape[2]
    halo = parts * each
    classes = w_out.shape[2]
    share = w_mid.shape[1]
    width = features.shape[1]
    run = functools.partial(call, mib=16 if parts <= 16 else 52)
    labels = labels.reshape(nodes // LANE, LANE)
    mask = train_mask.reshape(nodes // LANE, LANE)
    params = native(w_in, w_mid, w_out, norm_params)
    firsts = native(m_in, m_mid, m_out, m_norms)
    seconds = native(v_in, v_mid, v_out, v_norms)
    feat_at = lax.axis_index("feat").astype(jnp.int32).reshape(1)

    def bf(*dims):
        return shape(*dims, dtype=BF)

    def in_hbm(*arrays):
        return tuple(pltpu.with_memory_space_constraint(a, pltpu.HBM) for a in arrays)

    loads = in_hbm(send_index, features.T, *params)
    send, own, at = run(
        pack_kernel, [bf(parts, feats, each // 2, LANE), bf(pack_rows(nodes, share), HID), shape(1, dtype=jnp.int32)],
        *loads, feat_at, smem_in=(6,), smem_out=(2,), hbm_in=range(6),
        scratch=[pltpu.VMEM((halo, nodes), BF)] + [pltpu.VMEM(a.shape, a.dtype) for a in loads] + [pltpu.SemaphoreType.DMA((6,))],
    )
    recv = lax.all_to_all(
        send.reshape(parts * feats, each // 2, LANE), ("dom", "feat"), split_axis=0, concat_axis=0, tiled=True
    ).reshape(parts, feats, each // 2, LANE)
    chip = lax.ppermute(own, "feat", [(s, s ^ 2) for s in range(feats)])
    core = lax.ppermute(own, "feat", [(s, s ^ 1) for s in range(feats)])
    far = lax.ppermute(chip, "feat", [(s, s ^ 1) for s in range(feats)])
    loads = in_hbm(own, chip)
    results = [((feats * FEAT_PAD, nodes), BF), ((2, feats * FEAT_PAD, HID), BF), ((2, HID, HID), BF), ((2, LANE, HID), BF), ((8, HID), F32)]
    ft, win, wmid, wout, norms = run(
        side_kernel, [pltpu.HBM(*r) for r in results], *loads, core, far, at, hbm_in=range(2), smem_in=(4,), hbm_out=range(5),
        scratch=[pltpu.VMEM(*r) for r in results] + [pltpu.VMEM(a.shape, a.dtype) for a in loads]
        + [pltpu.SemaphoreType.DMA((2,)), pltpu.SemaphoreType.DMA((5,))],
    )
    loads = in_hbm(inner_adj, bound_adj, keep_slots, send_index, ft, win, norms)
    tile, ring, bound_ring = (512, 3, 4) if parts <= 16 else (256, 2, 2)
    adj, edge, row_deg, sel, mean_one, xhat_one, slope_one, istd_one, h_one, inv_deg, send = run(
        functools.partial(first_kernel, width=width),
        [bf(nodes, nodes), bf(nodes, halo), shape(nodes, LANE), bf(halo, nodes), bf(nodes, LANE),
         shape(nodes, HID), shape(nodes, HID), shape(nodes, LANE), bf(nodes, HID), shape(nodes, LANE), bf(halo, HID)],
        *loads, recv, hbm_in=range(7), mib=24 if parts <= 16 else 52,
        scratch=[pltpu.VMEM((halo, LANE), BF), pltpu.VMEM(keep_slots.shape, jnp.int32), pltpu.VMEM(send_index.shape, jnp.int32)]
        + [pltpu.VMEM(a.shape, a.dtype) for a in loads[4:]]
        + [pltpu.VMEM((ring, tile, nodes), jnp.int32), pltpu.VMEM((bound_ring, tile, halo), jnp.int32),
           pltpu.SemaphoreType.DMA((2, max(ring, bound_ring))), pltpu.SemaphoreType.DMA((5,))],
    )
    halo_one = exchange(send, parts).reshape(halo, HID)
    mean_two, xhat_two, slope_two, istd_two, h_two, send = run(
        second_kernel,
        [bf(nodes, HID), shape(nodes, HID), shape(nodes, HID), shape(nodes, LANE), bf(nodes, HID), bf(halo, HID)],
        adj, edge, halo_one, h_one, wmid, norms, inv_deg, sel,
    )
    halo_two = exchange(send, parts).reshape(halo, HID)
    mean_head, logits, pred, cross, mine, send = run(
        head_kernel,
        [bf(nodes, HID), shape(nodes, LANE), bf(nodes, LANE), shape(halo, LANE), shape(halo, LANE), bf(halo, HID)],
        adj, edge, halo_two, h_two, wout, inv_deg, sel, mask,
    )
    recv = exchange(send, parts).reshape(halo, HID)
    grad, grad_sum, send, losses = run(
        functools.partial(logit_grad_kernel, classes=classes, each=each),
        [bf(nodes, LANE), bf(nodes, HID), bf(halo, HID), shape(8, LANE)],
        logits, labels, mask, row_deg, pred, edge, recv, mine, cross, sel, wout, inv_deg,
        scratch=[pltpu.VMEM((halo, LANE), BF), pltpu.VMEM((halo, LANE), BF), pltpu.VMEM((nodes, LANE), F32), pltpu.VMEM((nodes, LANE), F32)],
    )
    recv = exchange(send, parts).reshape(halo, HID)
    joined_two, grad_sum, send, norm_sums = run(
        functools.partial(second_back_kernel, each=each),
        [bf(nodes, HID), bf(nodes, HID), bf(parts, each + 32, HID), shape(8, HID)],
        adj, grad_sum, grad, wout, recv, sel, slope_two, xhat_two, istd_two, norms, wmid, inv_deg, edge,
        h_two, mean_head, h_one, mean_two, at, smem_in=(17,),
        scratch=[pltpu.VMEM((nodes, HID), F32), pltpu.VMEM((2, LANE, HID), F32), pltpu.VMEM((LANE, HID), F32)],
    )
    recv = exchange(send, parts)
    send, = run(
        functools.partial(first_back_kernel, each=each), [bf(parts, MESSAGE_ROWS, HID)],
        adj, grad_sum, joined_two, wmid, recv, sel, slope_one, xhat_one, istd_one, norms, ft, mean_one, losses, norm_sums, at,
        smem_in=(14,),
        scratch=[pltpu.VMEM((nodes, HID), BF), pltpu.VMEM((nodes, HID), F32), pltpu.VMEM((2, feats * FEAT_PAD, HID), F32),
                 pltpu.VMEM((halo, HID), BF)],
    )
    recv = exchange(send, parts)
    grads, gnorm, total, gmid, gout, square = run(
        functools.partial(total_kernel, width=width),
        [shape(CHUNK_ROW, HID), shape(8, HID), shape(8, LANE), shape(2 * share, HID), shape(share, HID), shape(8, LANE)], recv,
    )
    squares = [square]
    for k in range(1, feats):
        squares.append(lax.ppermute(square, "feat", [(s, s ^ k) for s in range(feats)]))
    outs = [shape(1, 1)] * 3 + [shape(*p.shape) for p in params] * 3 + [bf(*p.shape) for p in params[:3]]
    grads = run(turn_kernel, [shape(*p.shape) for p in params], grads, gnorm, gmid, gout, at, smem_in=(4,))
    result = run(update_kernel, outs, total, *squares, losses, *grads, *params, *firsts, *seconds)
    return (
        tuple(r.reshape(()) for r in result[:3])
        + restore(*result[3:7]) + restore(*result[7:11]) + restore(*result[11:15]) + restore(*result[15:])
    )


def solution(mesh):
    weight = P(None, "feat", None)
    norm = P(None, None, "feat")
    placed = (
        P("dom", "feat"), P("dom", None), P("dom", None), P("dom", None), P("dom", None, None), P("dom"), P("dom"),
    ) + (weight, weight, weight, norm) * 3
    return jax.shard_map(
        functools.partial(shards, parts=mesh.shape["dom"], feats=mesh.shape["feat"]),
        mesh=mesh,
        in_specs=placed,
        out_specs=(P(), P(), P()) + (weight, weight, weight, norm) * 3 + (weight,) * 3,
        check_vma=False,
    )
```
